32 devices in a mesh: seq: 16 (over z, x, core), dp: 2 (over y).
Axes of the slice: x: 2, y: 2, z: 4, core: 2. Of those that a mesh axis runs over, the one named last changes fastest.
Arguments:
- queries: bfloat16 [2, 2048, 2048], P('dp', 'seq'), may hold values from -18 to 18
- key_vectors: bfloat16 [2, 2048, 2048], P('dp', 'seq'), may hold values from -18 to 18
- value_vectors: bfloat16 [2, 2048, 2048], P('dp', 'seq'), may hold values from -6 to 6
- cotangent: bfloat16 [2, 2048, 2048], P('dp', 'seq'), may hold values from -6 to 6
- compress_kernel: bfloat16 [512, 128], replicated, may hold values from -0.25 to 0.25
- memory_reach: int32 [2, 16], P('dp', 'seq'), may hold values from 1 to 4, as said below
Outputs:
- attended: bfloat16 [2, 2048, 2048], P('dp', 'seq')
- grad_queries: bfloat16 [2, 2048, 2048], P('dp', 'seq')
- grad_keys: bfloat16 [2, 2048, 2048], P('dp', 'seq')
- grad_values: bfloat16 [2, 2048, 2048], P('dp', 'seq')
- grad_kernel: float32 [512, 128], P('seq')
The draws below stay inside these ranges and needn't reach their ends.
Inputs may be any that keep to these rules, and one draw needn't show every extreme that they name: `memory_reach`: some segment reads 4 earlier segments and some reads 1.
All inputs are finite; a program needn't handle non-finite values.
Results may differ from the reference program's by a relative error of at most 0.0076.
Values may be sent and summed in bfloat16 or wider, within the bound.
No kernel may reach another device: no remote copies, remote signals or barrier semaphores. Data moves between devices by JAX's collectives and lax.ppermute only.
A program may use at most 64 MiB of HBM per device.

```python
import jax
import jax.numpy as jnp
from jax import lax

H = 16
E = 128
SEG = 128
SEGMENTS = 16
LEN = 2048
BOOKS = 2


def query_key_pair(key):
    shape_full = (BOOKS, LEN, H, E)
    query_full = jax.random.normal(jax.random.fold_in(key, 311), shape_full, jnp.float32)
    key_full = jax.random.normal(jax.random.fold_in(key, 312), shape_full, jnp.float32)
    query_full = jnp.clip(query_full, -18.0, 18.0).reshape(BOOKS, LEN, H * E)
    key_full = jnp.clip(key_full, -18.0, 18.0).reshape(BOOKS, LEN, H * E)
    return (query_full, key_full)


def draw_queries(key, part):
    return query_key_pair(key)[0].astype(jnp.bfloat16)


def draw_key_vectors(key, part):
    return query_key_pair(key)[1].astype(jnp.bfloat16)


def draw_memory_reach(key, part):
    counted = BOOKS * SEGMENTS
    drawn = jax.random.randint(jax.random.fold_in(key, 401), (counted,), 1, 5, dtype=jnp.int32)
    chosen_top = jax.random.randint(jax.random.fold_in(key, 402), (), 0, counted, dtype=jnp.int32)
    chosen_low = (chosen_top + 1) % counted
    flat_ids = jnp.arange(counted, dtype=jnp.int32)
    drawn = jnp.where(flat_ids == chosen_top, 4, drawn)
    drawn = jnp.where(flat_ids == chosen_low, 1, drawn)
    return drawn.reshape(BOOKS, SEGMENTS).astype(jnp.int32)


def levels(key, dims, pieces, low, top_value):
    gain = 1.0
    for dim, shards_of in pieces:
        heights = jax.random.uniform(jax.random.fold_in(jax.random.fold_in(key, 6), dim), (shards_of,), jnp.float32, low / len(pieces), top_value / len(pieces))
        gain = gain * jnp.repeat(jnp.exp(heights), dims[dim] // shards_of).reshape((-1,) + (1,) * (len(dims) - 1 - dim))
    return gain


def scatter_about(key, extent, deviation, bound, cuts=(), kind=jnp.bfloat16):
    entries = jax.random.normal(key, extent, jnp.float32) * deviation
    if len(cuts) > 0:
        entries = levels(key, extent, cuts, -0.22, 0.18) * entries
    return jnp.clip(entries, min=-bound, max=bound).astype(kind)


def setup_inputs(seed: int = 0) -> dict:
    seeds = jax.random.split(jax.random.key(seed), 7)
    queries = draw_queries(jax.random.fold_in(seeds[6], 71), 0)
    key_vectors = draw_key_vectors(jax.random.fold_in(seeds[6], 71), 0)
    value_vectors = scatter_about(seeds[2], (BOOKS, LEN, H * E), 1.0, 6.0, ((0, 2), (1, 16)))
    cotangent = scatter_about(seeds[3], (BOOKS, LEN, H * E), 1.0, 6.0, ((0, 2), (1, 16)))
    compress_kernel = scatter_about(seeds[4], (4 * E, E), (4 * E) ** -0.5, 0.25)
    memory_reach = draw_memory_reach(jax.random.fold_in(seeds[6], 71), 0)
    return dict(queries=queries, key_vectors=key_vectors, value_vectors=value_vectors, cotangent=cotangent, compress_kernel=compress_kernel, memory_reach=memory_reach)


def attend_block(query_rows, key_rows, value_rows, grad_rows, memory_keys, memory_values, visible):
    segment_len = query_rows.shape[0]
    slot_rows = segment_len // 4
    span_len = 2 * segment_len
    score_scale = E ** -0.5
    query_heads = query_rows.astype(jnp.float32).reshape(segment_len, H, E)
    grad_heads = grad_rows.astype(jnp.float32).reshape(segment_len, H, E)
    key_heads = jnp.concatenate([memory_keys, key_rows], 0).astype(jnp.float32).reshape(span_len, H, E)
    value_heads = jnp.concatenate([memory_values, value_rows], 0).astype(jnp.float32).reshape(span_len, H, E)
    columns = jnp.arange(span_len, dtype=jnp.int32)
    row_ids = jnp.arange(segment_len, dtype=jnp.int32)
    slot_of = jnp.minimum(columns // slot_rows, 3)
    memory_open = jnp.any((slot_of[:, None] == jnp.arange(4, dtype=jnp.int32)[None, :]) & visible[None, :], axis=1)
    allowed = jnp.where(columns[None, :] < segment_len, memory_open[None, :], columns[None, :] - segment_len <= row_ids[:, None])
    scores = jnp.einsum("shd,lhd->hsl", query_heads, key_heads) * score_scale
    scores = jnp.where(allowed[None], scores, -1e30)
    highest = jnp.max(scores, axis=2, keepdims=True)
    raised = jnp.where(allowed[None], jnp.exp(scores - highest), 0.0)
    weights = raised / jnp.sum(raised, axis=2, keepdims=True)
    weights_low = lax.optimization_barrier(weights.astype(jnp.bfloat16)).astype(jnp.float32)
    attended = jnp.einsum("hsl,lhd->shd", weights_low, value_heads)
    grad_weights = jnp.einsum("shd,lhd->hsl", grad_heads, value_heads)
    row_delta = jnp.sum(weights * grad_weights, axis=2, keepdims=True)
    grad_scores = (weights * (grad_weights - row_delta) * score_scale).astype(jnp.bfloat16)
    grad_scores = lax.optimization_barrier(grad_scores).astype(jnp.float32)
    grad_query = jnp.einsum("hsl,lhd->shd", grad_scores, key_heads)
    grad_key_list = jnp.einsum("hsl,shd->lhd", grad_scores, query_heads).reshape(span_len, H * E)
    grad_value_list = jnp.einsum("hsl,shd->lhd", weights_low, grad_heads).reshape(span_len, H * E)
    return (attended.reshape(segment_len, H * E).astype(jnp.bfloat16),
            grad_query.reshape(segment_len, H * E).astype(jnp.bfloat16),
            grad_key_list[segment_len:], grad_value_list[segment_len:],
            grad_key_list[:segment_len], grad_value_list[:segment_len])


def reference(queries, key_vectors, value_vectors, cotangent, compress_kernel, memory_reach):
    slot_rows = SEG // 4
    head_width = H * E
    kernel = compress_kernel.reshape(4, E, E).astype(jnp.float32)
    key_blocks = key_vectors.reshape(BOOKS, SEGMENTS, slot_rows, 4, H, E).astype(jnp.float32)
    value_blocks = value_vectors.reshape(BOOKS, SEGMENTS, slot_rows, 4, H, E).astype(jnp.float32)
    packed_keys = jnp.einsum("bsmthe,tef->bsmhf", key_blocks, kernel).astype(jnp.bfloat16)
    packed_values = jnp.einsum("bsmthe,tef->bsmhf", value_blocks, kernel).astype(jnp.bfloat16)
    packed_keys = packed_keys.reshape(BOOKS, SEGMENTS, slot_rows, head_width)
    packed_values = packed_values.reshape(BOOKS, SEGMENTS, slot_rows, head_width)
    padded_keys = jnp.pad(packed_keys, ((0, 0), (4, 0), (0, 0), (0, 0)))
    padded_values = jnp.pad(packed_values, ((0, 0), (4, 0), (0, 0), (0, 0)))
    zero_index = jnp.zeros((), jnp.int32)
    slot_ids = jnp.arange(1, 5, dtype=jnp.int32)

    def one_segment(index):
        book_id = (index // SEGMENTS).astype(jnp.int32)
        segment_id = (index % SEGMENTS).astype(jnp.int32)
        first_row = (segment_id * SEG).astype(jnp.int32)

        def rows_of(array):
            return lax.dynamic_slice(array, (book_id, first_row, zero_index), (1, SEG, head_width))[0]

        def memory_of(array):
            picked = lax.dynamic_slice(array, (book_id, segment_id, zero_index, zero_index), (1, 4, slot_rows, head_width))[0]
            return picked[::-1].reshape(4 * slot_rows, head_width)

        reach_here = lax.dynamic_slice(memory_reach, (book_id, segment_id), (1, 1))[0, 0]
        visible = (slot_ids <= reach_here) & (segment_id - slot_ids >= 0)
        return attend_block(rows_of(queries), rows_of(key_vectors), rows_of(value_vectors), rows_of(cotangent),
                            memory_of(padded_keys), memory_of(padded_values), visible)

    results = lax.map(one_segment, jnp.arange(BOOKS * SEGMENTS, dtype=jnp.int32))
    attended = results[0].reshape(BOOKS, LEN, head_width)
    grad_queries = results[1].reshape(BOOKS, LEN, head_width)
    local_keys = results[2].reshape(BOOKS, LEN, head_width)
    local_values = results[3].reshape(BOOKS, LEN, head_width)

    def gather_back(grads):
        shaped = grads.reshape(BOOKS, SEGMENTS, 4, slot_rows, head_width)
        padded = jnp.pad(shaped, ((0, 0), (0, 4), (0, 0), (0, 0), (0, 0)))
        summed = jnp.zeros((BOOKS, SEGMENTS, slot_rows, head_width), jnp.float32)
        for offset in range(1, 5):
            summed = summed + padded[:, offset:offset + SEGMENTS, offset - 1]
        rounded = lax.optimization_barrier(summed.astype(jnp.bfloat16))
        return rounded.astype(jnp.float32).reshape(BOOKS, SEGMENTS, slot_rows, H, E)

    memory_grad_keys = gather_back(results[4])
    memory_grad_values = gather_back(results[5])
    back_keys = jnp.einsum("bsmhf,tef->bsmthe", memory_grad_keys, kernel).reshape(BOOKS, LEN, head_width)
    back_values = jnp.einsum("bsmhf,tef->bsmthe", memory_grad_values, kernel).reshape(BOOKS, LEN, head_width)
    grad_keys = (local_keys + back_keys).astype(jnp.bfloat16)
    grad_values = (local_values + back_values).astype(jnp.bfloat16)
    grad_kernel = (jnp.einsum("bsmthe,bsmhf->tef", key_blocks, memory_grad_keys)
                   + jnp.einsum("bsmthe,bsmhf->tef", value_blocks, memory_grad_values)).reshape(4 * E, E)
    return (attended, grad_queries, grad_keys, grad_values, grad_kernel)
```

```python
import functools

import jax
import jax.numpy as jnp
from jax import lax
from jax.experimental import pallas as pl
from jax.experimental.pallas import tpu as pltpu
from jax.sharding import PartitionSpec as P

F32 = jnp.float32
BF16 = jnp.bfloat16
TAPS = 4
SLOTS = 4
MASKED = -1e30
VMEM_BYTES = 40 * 2**20


def nt(a, b):
    return lax.dot_general(a, b, (((1,), (1,)), ((), ())), preferred_element_type=F32)


def nn(a, b):
    return lax.dot_general(a, b, (((1,), (0,)), ((), ())), preferred_element_type=F32)


def tn(a, b):
    return lax.dot_general(a, b, (((0,), (0,)), ((), ())), preferred_element_type=F32)


def tap_major(seg, inverse=False):
    slot = seg // TAPS
    spot = lax.broadcasted_iota(jnp.int32, (seg, seg), 1 if inverse else 0)
    token = lax.broadcasted_iota(jnp.int32, (seg, seg), 0 if inverse else 1)
    return (token == TAPS * (spot % slot) + spot // slot).astype(BF16)


def pack_kernel(k_ref, v_ref, w_ref, kp_ref, vp_ref, packed_ref):
    seg, width = k_ref.shape
    feat = w_ref.shape[1]
    slot = seg // TAPS
    order = tap_major(seg)
    rows = []
    for src, dst in ((k_ref, kp_ref), (v_ref, vp_ref)):
        sorted_rows = nn(order, src[...]).astype(BF16)
        dst[...] = sorted_rows
        for h in range(width // feat):
            part = sorted_rows[:, h * feat : (h + 1) * feat]
            rows.append(
                jnp.concatenate([part[t * slot : (t + 1) * slot] for t in range(TAPS)], 1)
            )
    packed = nn(jnp.concatenate(rows, 0), w_ref[...]).astype(BF16)
    packed_ref[...] = packed.reshape(packed_ref.shape)


def own_kernel(q_ref, g_ref, kp_ref, vp_ref, stat_ref, kt_ref, vt_ref):
    seg, width = q_ref.shape
    heads = stat_ref.shape[1]
    feat = width // heads
    slot = seg // TAPS
    scale = feat**-0.5
    spot = lax.broadcasted_iota(jnp.int32, (seg, seg), 0)
    query = lax.broadcasted_iota(jnp.int32, (seg, seg), 1)
    allowed = TAPS * (spot % slot) + spot // slot <= query
    for h in range(heads):
        cols = slice(h * feat, (h + 1) * feat)
        scores = jnp.where(allowed, nt(kp_ref[:, cols], q_ref[:, cols]) * scale, MASKED)
        top = jnp.max(scores, axis=0, keepdims=True)
        raised = jnp.exp(scores - top)
        grad_weights = nt(vp_ref[:, cols], g_ref[:, cols])
        stat_ref[0, h] = top
        stat_ref[1, h] = jnp.sum(raised, axis=0, keepdims=True)
        stat_ref[2, h] = jnp.sum(raised * grad_weights, axis=0, keepdims=True)
    for src, dst in ((kp_ref, kt_ref), (vp_ref, vt_ref)):
        for t in range(TAPS):
            stacked = jnp.concatenate(
                [
                    src[t * slot : (t + 1) * slot, h * feat : (h + 1) * feat]
                    for h in range(heads)
                ],
                0,
            )
            dst[t * feat : (t + 1) * feat, :] = stacked.T


def memory_kernel(
    place_ref, q_ref, g_ref, stat_ref, near_ref, r2_ref, r2s_ref, r4_ref, r4s_ref,
    swap_ref, t2_ref, t4_ref, w_ref, gs_ref, fin_ref,
):
    seg, width = q_ref.shape
    heads = stat_ref.shape[1]
    feat = width // heads
    slot = seg // TAPS
    scale = feat**-0.5
    position, reach = place_ref[0], place_ref[1]
    even = position % 2 == 0
    slot_of = lax.broadcasted_iota(jnp.int32, (SLOTS * slot, seg), 0) // slot + 1
    allowed = slot_of <= jnp.minimum(reach, position)
    for h in range(heads):
        cols = slice(h * feat, (h + 1) * feat)
        memory = []
        for kv in range(2):
            far = r2s_ref[kv, h]
            memory.append(
                jnp.concatenate(
                    [
                        jnp.where(even, far, near_ref[kv, h]),
                        r2_ref[kv, h],
                        jnp.where(even, r4s_ref[kv, h], far),
                        r4_ref[kv, h],
                    ],
                    0,
                )
            )
        q, g = q_ref[:, cols], g_ref[:, cols]
        scores = jnp.where(allowed, nt(memory[0], q) * scale, MASKED)
        own_top = stat_ref[0, h]
        top = jnp.maximum(own_top, jnp.max(scores, axis=0, keepdims=True))
        raised = jnp.exp(scores - top)
        fade = jnp.exp(own_top - top)
        grad_weights = nt(memory[1], g)
        total = stat_ref[1, h] * fade + jnp.sum(raised, axis=0, keepdims=True)
        delta = stat_ref[2, h] * fade + jnp.sum(raised * grad_weights, axis=0, keepdims=True)
        inverse = 1.0 / total
        delta = delta * inverse
        weights = raised * inverse
        weights_low = weights.astype(BF16)
        grad_scores = (weights * (grad_weights - delta) * scale).astype(BF16)
        w_ref[h] = weights_low
        gs_ref[h] = grad_scores
        fin_ref[0, h] = top
        fin_ref[1, h] = inverse
        fin_ref[2, h] = delta
        for kv, terms in enumerate((nn(grad_scores, q), nn(weights_low, g))):
            terms = terms.astype(BF16)
            swap_ref[0, kv, h] = terms[:slot]
            t2_ref[kv, h] = terms[slot : 2 * slot]
            swap_ref[1, kv, h] = terms[2 * slot : 3 * slot]
            t4_ref[kv, h] = terms[3 * slot :]


def output_kernel(
    place_ref, q_ref, g_ref, kp_ref, vp_ref, near_ref, r2_ref, r2s_ref, r4_ref, r4s_ref,
    w_ref, gs_ref, fin_ref, att_ref, gq_ref, ok_ref, ov_ref,
):
    seg, width = q_ref.shape
    heads = fin_ref.shape[1]
    feat = width // heads
    slot = seg // TAPS
    scale = feat**-0.5
    even = place_ref[0] % 2 == 0
    spot = lax.broadcasted_iota(jnp.int32, (seg, seg), 0)
    query = lax.broadcasted_iota(jnp.int32, (seg, seg), 1)
    allowed = TAPS * (spot % slot) + spot // slot <= query
    for h in range(heads):
        cols = slice(h * feat, (h + 1) * feat)
        memory = []
        for kv in range(2):
            far = r2s_ref[kv, h]
            memory.append(
                jnp.concatenate(
                    [
                        jnp.where(even, far, near_ref[kv, h]),
                        r2_ref[kv, h],
                        jnp.where(even, r4s_ref[kv, h], far),
                        r4_ref[kv, h],
                    ],
                    0,
                )
            )
        q, g, k, v = q_ref[:, cols], g_ref[:, cols], kp_ref[:, cols], vp_ref[:, cols]
        scores = jnp.where(allowed, nt(k, q) * scale, MASKED)
        weights = jnp.exp(scores - fin_ref[0, h]) * fin_ref[1, h]
        grad_weights = nt(v, g)
        weights_low = weights.astype(BF16)
        grad_scores = (weights * (grad_weights - fin_ref[2, h]) * scale).astype(BF16)
        ok_ref[:, cols] = nn(grad_scores, q)
        ov_ref[:, cols] = nn(weights_low, g)
        att = tn(weights_low, v) + tn(w_ref[h], memory[1])
        att_ref[:, cols] = att.astype(BF16)
        gq = tn(grad_scores, k) + tn(gs_ref[h], memory[0])
        gq_ref[:, cols] = gq.astype(BF16)


def sum_kernel(place_ref, near_ref, a_ref, b_ref, kt_ref, vt_ref, mg_ref, mine_ref, other_ref):
    count = mine_ref.shape[0] * 2
    even = place_ref[0] % 2 == 0
    summed = a_ref[...].astype(F32) + b_ref[...].astype(F32)
    near = jnp.where(even, near_ref[0].astype(F32), 0.0)
    low = (summed + near).astype(BF16)
    mg_ref[...] = low
    half = low.shape[0] // 2
    terms = nn(kt_ref[...], low[:half]) + nn(vt_ref[...], low[half:])
    rows = terms.shape[0] // count
    bits = count.bit_length() - 1
    for p in range(0, count, 2):
        spot = int(format(p, "b").zfill(bits)[::-1], 2)
        first = terms[p * rows : (p + 1) * rows]
        second = terms[(p + 1) * rows : (p + 2) * rows]
        mine_ref[spot] = jnp.where(even, first, second)
        other_ref[spot] = jnp.where(even, second, first)


def back_kernel(mgk_ref, mgv_ref, w_ref, ok_ref, ov_ref, gk_ref, gv_ref):
    seg, width = ok_ref.shape
    heads, slot, feat = mgk_ref.shape
    restore = tap_major(seg, inverse=True)
    for mg_ref, own_ref, out_ref in ((mgk_ref, ok_ref, gk_ref), (mgv_ref, ov_ref, gv_ref)):
        back = nt(mg_ref[...].reshape(heads * slot, feat), w_ref[...])
        columns = []
        for h in range(heads):
            head = back[h * slot : (h + 1) * slot]
            columns.append(
                jnp.concatenate([head[:, t * feat : (t + 1) * feat] for t in range(TAPS)], 0)
            )
        total = (own_ref[...] + jnp.concatenate(columns, 1)).astype(BF16)
        out_ref[...] = nn(restore, total).astype(BF16)


def call(kernel, out_shape, grid, in_specs, out_specs, flops, moved, exps=0):
    return pl.pallas_call(
        kernel,
        out_shape=out_shape,
        grid=grid,
        in_specs=in_specs,
        out_specs=out_specs,
        compiler_params=pltpu.CompilerParams(vmem_limit_bytes=VMEM_BYTES),
        cost_estimate=pl.CostEstimate(flops=flops, bytes_accessed=moved, transcendentals=exps),
    )


def local(queries, key_vectors, value_vectors, cotangent, compress_kernel, memory_reach):
    q, k, v, g = queries[0], key_vectors[0], value_vectors[0], cotangent[0]
    seg, width = q.shape
    feat = compress_kernel.shape[1]
    heads = width // feat
    slot = seg // TAPS
    count = lax.axis_size("seq")
    books = lax.axis_size("dp")
    position = lax.axis_index("seq")
    place = jnp.stack([position.astype(jnp.int32), memory_reach[0, 0]])

    group = 4
    grid = (heads // group,)
    cols = pl.BlockSpec((seg, group * feat), lambda i: (0, i))
    whole = pl.BlockSpec(compress_kernel.shape, lambda i: (0, 0))
    small = pl.BlockSpec((2, group, slot, feat), lambda i: (0, i, 0, 0))
    pair = pl.BlockSpec((2, 2, group, slot, feat), lambda i: (0, 0, i, 0, 0))
    stats = pl.BlockSpec((3, group, 1, seg), lambda i: (0, i, 0, 0))
    square = pl.BlockSpec((group, SLOTS * slot, seg), lambda i: (i, 0, 0))
    turned = pl.BlockSpec((TAPS * feat, group * slot), lambda i: (0, i))
    scalars = pl.BlockSpec(memory_space=pltpu.SMEM)
    rows_low = jax.ShapeDtypeStruct((seg, width), BF16)
    rows_full = jax.ShapeDtypeStruct((seg, width), F32)
    packed_shape = jax.ShapeDtypeStruct((2, heads, slot, feat), BF16)
    stat_shape = jax.ShapeDtypeStruct((3, heads, 1, seg), F32)
    square_shape = jax.ShapeDtypeStruct((heads, SLOTS * slot, seg), BF16)
    turned_shape = jax.ShapeDtypeStruct((TAPS * feat, heads * slot), BF16)
    row_bytes = 2 * seg * width
    unit = 2 * heads * seg * seg * feat

    kp, vp, packed = call(
        pack_kernel,
        (rows_low, rows_low, packed_shape),
        grid, [cols, cols, whole], (cols, cols, small), 4 * unit, 5 * row_bytes,
    )(k, v, compress_kernel)

    def shift(value, steps):
        return lax.ppermute(value, "seq", [(s, (s + steps) % count) for s in range(count)])

    def trade(value, bit, axis="seq"):
        size = lax.axis_size(axis)
        return lax.ppermute(value, axis, [(s, s ^ bit) for s in range(size)])

    near = lax.ppermute(packed, "seq", [(s, s + 1) for s in range(0, count, 2)])
    r2 = shift(packed, 2)
    r4 = shift(packed, 4)
    r2s = trade(r2, 1)
    r4s = lax.ppermute(r4, "seq", [(s + 1, s) for s in range(0, count, 2)])

    own_stats, kt, vt = call(
        own_kernel,
        (stat_shape, turned_shape, turned_shape),
        grid, [cols] * 4, (stats, turned, turned), 2 * unit, 6 * row_bytes, heads * seg * seg,
    )(q, g, kp, vp)

    swap, t2, t4, w_mem, gs_mem, final = call(
        memory_kernel,
        (
            jax.ShapeDtypeStruct((2, 2, heads, slot, feat), BF16),
            packed_shape, packed_shape, square_shape, square_shape, stat_shape,
        ),
        grid,
        [scalars, cols, cols, stats] + [small] * 5,
        (pair, small, small, square, square, stats),
        4 * unit, 7 * row_bytes, heads * seg * seg,
    )(place, q, g, own_stats, near, r2, r2s, r4, r4s)

    swapped = trade(swap, 1)
    even = position % 2 == 0
    send2 = (t2.astype(F32) + jnp.where(even, swapped[1], swapped[0]).astype(F32)).astype(BF16)
    send4 = (
        t4.astype(F32) + jnp.where(even, jnp.zeros_like(swapped[1]), swapped[1]).astype(F32)
    ).astype(BF16)
    back2 = shift(send2, -2)
    back4 = shift(send4, -4)

    attended, grad_queries, own_keys, own_values = call(
        output_kernel,
        (rows_low, rows_low, rows_full, rows_full),
        grid,
        [scalars] + [cols] * 4 + [small] * 5 + [square, square, stats],
        (cols, cols, cols, cols),
        8 * unit, 15 * row_bytes, heads * seg * seg,
    )(place, q, g, kp, vp, near, r2, r2s, r4, r4s, w_mem, gs_mem, final)

    flat = (2 * heads * slot, feat)
    kernel_rows = compress_kernel.shape[0]
    half_shape = jax.ShapeDtypeStruct((count // 2, kernel_rows // count, feat), F32)
    vmem = pl.BlockSpec(memory_space=pltpu.VMEM)
    memory_grads, mine, other = call(
        sum_kernel,
        (jax.ShapeDtypeStruct(flat, BF16), half_shape, half_shape),
        (1,),
        [
            scalars,
            pl.BlockSpec((1, *flat), lambda i: (0, 0, 0)),
            vmem, vmem, vmem, vmem,
        ],
        (vmem, vmem, vmem),
        unit, 4 * row_bytes,
    )(place, swapped.reshape(2, *flat), back2.reshape(flat), back4.reshape(flat), kt, vt)

    part = mine + trade(other, 1)
    bit = 2
    while bit < count:
        part = part.reshape(2, -1, *part.shape[1:])
        side = (position // bit) % 2
        kept = lax.dynamic_index_in_dim(part, side, 0, False)
        sent = lax.dynamic_index_in_dim(part, 1 - side, 0, False)
        part = kept + trade(sent, bit)
        bit *= 2
    part = part.reshape(kernel_rows // count, feat)
    bit = 1
    while bit < books:
        part = part + trade(part, bit, "dp")
        bit *= 2

    grads = memory_grads.reshape(2, heads, slot, feat)
    head_rows = pl.BlockSpec((group, slot, feat), lambda i: (i, 0, 0))
    grad_keys, grad_values = call(
        back_kernel,
        (rows_low, rows_low),
        grid, [head_rows, head_rows, whole, cols, cols], (cols, cols), 4 * unit, 7 * row_bytes,
    )(grads[0], grads[1], compress_kernel, own_keys, own_values)
    return (attended[None], grad_queries[None], grad_keys[None], grad_values[None], part)


def solution(mesh):
    rows = P("dp", "seq", None)
    return jax.shard_map(
        local,
        mesh=mesh,
        in_specs=(rows, rows, rows, rows, P(), P("dp", "seq")),
        out_specs=(rows, rows, rows, rows, P("seq", None)),
        check_vma=False,
    )
```

```python
import functools

import jax
import jax.numpy as jnp
from jax import lax
from jax.experimental import pallas as pl
from jax.experimental.pallas import tpu as pltpu
from jax.sharding import PartitionSpec as P

F32 = jnp.float32
BF16 = jnp.bfloat16
TAPS = 4
SLOTS = 4
MASKED = -1e30
VMEM_BYTES = 60 * 2**20


def nt(a, b):
    return lax.dot_general(a, b, (((1,), (1,)), ((), ())), preferred_element_type=F32)


def nn(a, b):
    return lax.dot_general(a, b, (((1,), (0,)), ((), ())), preferred_element_type=F32)


def tn(a, b):
    return lax.dot_general(a, b, (((0,), (0,)), ((), ())), preferred_element_type=F32)


def tap_major(seg, inverse=False):
    slot = seg // TAPS
    spot = lax.broadcasted_iota(jnp.int32, (seg, seg), 1 if inverse else 0)
    token = lax.broadcasted_iota(jnp.int32, (seg, seg), 0 if inverse else 1)
    return (token == TAPS * (spot % slot) + spot // slot).astype(BF16)


def staged(heads, first, second, third):
    pairs = [range(h, min(h + 2, heads)) for h in range(0, heads, 2)]
    begun, turned = {}, {}
    for i in range(len(pairs) + 2):
        if i < len(pairs):
            for h in pairs[i]:
                begun[h] = first(h)
        if i >= 2:
            for h in pairs[i - 2]:
                third(h, *turned.pop(h))
        if 1 <= i <= len(pairs):
            for h in pairs[i - 1]:
                turned[h] = second(h, *begun.pop(h))


def memory_rows(kv, h, even, near_ref, r2_ref, r2s_ref, r4_ref, r4s_ref):
    far = r2s_ref[kv, h]
    return jnp.concatenate(
        [
            jnp.where(even, far, near_ref[kv, h]),
            r2_ref[kv, h],
            jnp.where(even, r4s_ref[kv, h], far),
            r4_ref[kv, h],
        ],
        0,
    )


def pack_kernel(k_ref, v_ref, w_ref, kp_ref, vp_ref, packed_ref):
    seg, width = k_ref.shape
    feat = w_ref.shape[1]
    slot = seg // TAPS
    order = tap_major(seg)
    rows = []
    for src, dst in ((k_ref, kp_ref), (v_ref, vp_ref)):
        sorted_rows = nn(order, src[...]).astype(BF16)
        dst[...] = sorted_rows
        for h in range(width // feat):
            part = sorted_rows[:, h * feat : (h + 1) * feat]
            rows.append(
                jnp.concatenate([part[t * slot : (t + 1) * slot] for t in range(TAPS)], 1)
            )
    packed = nn(jnp.concatenate(rows, 0), w_ref[...]).astype(BF16)
    packed_ref[...] = packed.reshape(packed_ref.shape)


def own_kernel(q_ref, g_ref, kp_ref, vp_ref, stat_ref, kt_ref, vt_ref):
    seg, width = q_ref.shape
    heads = stat_ref.shape[1]
    feat = width // heads
    slot = seg // TAPS
    scale = feat**-0.5
    spot = lax.broadcasted_iota(jnp.int32, (seg, seg), 0)
    query = lax.broadcasted_iota(jnp.int32, (seg, seg), 1)
    allowed = TAPS * (spot % slot) + spot // slot <= query

    def cols(h):
        return slice(h * feat, (h + 1) * feat)

    def first(h):
        return nt(kp_ref[:, cols(h)], q_ref[:, cols(h)]), nt(vp_ref[:, cols(h)], g_ref[:, cols(h)])

    def second(h, scores, grad_weights):
        scores = jnp.where(allowed, scores * scale, MASKED)
        top = jnp.max(scores, axis=0, keepdims=True)
        raised = jnp.exp(scores - top)
        stat_ref[0, h] = top
        stat_ref[1, h] = jnp.sum(raised, axis=0, keepdims=True)
        stat_ref[2, h] = jnp.sum(raised * grad_weights, axis=0, keepdims=True)
        return ()

    staged(heads, first, second, lambda h: None)
    for src, dst in ((kp_ref, kt_ref), (vp_ref, vt_ref)):
        for t in range(TAPS):
            stacked = jnp.concatenate(
                [
                    src[t * slot : (t + 1) * slot, h * feat : (h + 1) * feat]
                    for h in range(heads)
                ],
                0,
            )
            dst[t * feat : (t + 1) * feat, :] = stacked.T


def memory_kernel(
    place_ref, q_ref, g_ref, stat_ref, near_ref, r2_ref, r2s_ref, r4_ref, r4s_ref,
    swap_ref, t2_ref, t4_ref, w_ref, gs_ref, fin_ref,
):
    seg, width = q_ref.shape
    heads = stat_ref.shape[1]
    feat = width // heads
    slot = seg // TAPS
    scale = feat**-0.5
    position, reach = lax.axis_index("seq"), place_ref[0, 0]
    even = position % 2 == 0
    slot_of = lax.broadcasted_iota(jnp.int32, (SLOTS * slot, seg), 0) // slot + 1
    allowed = slot_of <= jnp.minimum(reach, position)
    slots = (near_ref, r2_ref, r2s_ref, r4_ref, r4s_ref)

    def cols(h):
        return slice(h * feat, (h + 1) * feat)

    def first(h):
        return (
            nt(memory_rows(0, h, even, *slots), q_ref[:, cols(h)]),
            nt(memory_rows(1, h, even, *slots), g_ref[:, cols(h)]),
        )

    def second(h, scores, grad_weights):
        scores = jnp.where(allowed, scores * scale, MASKED)
        own_top = stat_ref[0, h]
        top = jnp.maximum(own_top, jnp.max(scores, axis=0, keepdims=True))
        raised = jnp.exp(scores - top)
        fade = jnp.exp(own_top - top)
        total = stat_ref[1, h] * fade + jnp.sum(raised, axis=0, keepdims=True)
        delta = stat_ref[2, h] * fade + jnp.sum(raised * grad_weights, axis=0, keepdims=True)
        inverse = 1.0 / total
        delta = delta * inverse
        weights = raised * inverse
        weights_low = weights.astype(BF16)
        grad_scores = (weights * (grad_weights - delta) * scale).astype(BF16)
        w_ref[h] = weights_low
        gs_ref[h] = grad_scores
        fin_ref[0, h] = top
        fin_ref[1, h] = inverse
        fin_ref[2, h] = delta
        return grad_scores, weights_low

    def third(h, grad_scores, weights_low):
        pair = (nn(grad_scores, q_ref[:, cols(h)]), nn(weights_low, g_ref[:, cols(h)]))
        for kv, terms in enumerate(pair):
            terms = terms.astype(BF16)
            swap_ref[0, kv, h] = terms[:slot]
            t2_ref[kv, h] = terms[slot : 2 * slot]
            swap_ref[1, kv, h] = terms[2 * slot : 3 * slot]
            t4_ref[kv, h] = terms[3 * slot :]

    staged(heads, first, second, third)


def output_kernel(
    place_ref, q_ref, g_ref, kp_ref, vp_ref, near_ref, r2_ref, r2s_ref, r4_ref, r4s_ref,
    w_ref, gs_ref, fin_ref, att_ref, gq_ref, ok_ref, ov_ref,
):
    seg, width = q_ref.shape
    heads = fin_ref.shape[1]
    feat = width // heads
    slot = seg // TAPS
    scale = feat**-0.5
    even = lax.axis_index("seq") % 2 == 0
    spot = lax.broadcasted_iota(jnp.int32, (seg, seg), 0)
    query = lax.broadcasted_iota(jnp.int32, (seg, seg), 1)
    allowed = TAPS * (spot % slot) + spot // slot <= query
    slots = (near_ref, r2_ref, r2s_ref, r4_ref, r4s_ref)

    def cols(h):
        return slice(h * feat, (h + 1) * feat)

    def first(h):
        return nt(kp_ref[:, cols(h)], q_ref[:, cols(h)]), nt(vp_ref[:, cols(h)], g_ref[:, cols(h)])

    def second(h, scores, grad_weights):
        scores = jnp.where(allowed, scores * scale, MASKED)
        weights = jnp.exp(scores - fin_ref[0, h]) * fin_ref[1, h]
        grad_scores = (weights * (grad_weights - fin_ref[2, h]) * scale).astype(BF16)
        return grad_scores, weights.astype(BF16)

    def third(h, grad_scores, weights_low):
        ok_ref[:, cols(h)] = nn(grad_scores, q_ref[:, cols(h)])
        ov_ref[:, cols(h)] = nn(weights_low, g_ref[:, cols(h)])
        att = tn(weights_low, vp_ref[:, cols(h)]) + tn(w_ref[h], memory_rows(1, h, even, *slots))
        att_ref[:, cols(h)] = att.astype(BF16)
        gq = tn(grad_scores, kp_ref[:, cols(h)]) + tn(gs_ref[h], memory_rows(0, h, even, *slots))
        gq_ref[:, cols(h)] = gq.astype(BF16)

    staged(heads, first, second, third)


def sum_kernel(place_ref, near_ref, a_ref, b_ref, kt_ref, vt_ref, mg_ref, mine_ref, other_ref):
    count = mine_ref.shape[0] * 2
    even = lax.axis_index("seq") % 2 == 0
    summed = a_ref[...].astype(F32) + b_ref[...].astype(F32)
    near = jnp.where(even, near_ref[0].astype(F32), 0.0)
    low = (summed + near).astype(BF16)
    mg_ref[...] = low
    half = low.shape[0] // 2
    terms = nn(kt_ref[...], low[:half]) + nn(vt_ref[...], low[half:])
    rows = terms.shape[0] // count
    bits = count.bit_length() - 1
    for p in range(0, count, 2):
        spot = int(format(p, "b").zfill(bits)[::-1], 2)
        first = terms[p * rows : (p + 1) * rows]
        second = terms[(p + 1) * rows : (p + 2) * rows]
        mine_ref[spot] = jnp.where(even, first, second)
        other_ref[spot] = jnp.where(even, second, first)


def back_kernel(mgk_ref, mgv_ref, w_ref, ok_ref, ov_ref, gk_ref, gv_ref):
    seg, width = ok_ref.shape
    heads, slot, feat = mgk_ref.shape
    restore = tap_major(seg, inverse=True)
    for mg_ref, own_ref, out_ref in ((mgk_ref, ok_ref, gk_ref), (mgv_ref, ov_ref, gv_ref)):
        back = nt(mg_ref[...].reshape(heads * slot, feat), w_ref[...])
        columns = []
        for h in range(heads):
            head = back[h * slot : (h + 1) * slot]
            columns.append(
                jnp.concatenate([head[:, t * feat : (t + 1) * feat] for t in range(TAPS)], 0)
            )
        total = (own_ref[...] + jnp.concatenate(columns, 1)).astype(BF16)
        out_ref[...] = nn(restore, total).astype(BF16)


def call(kernel, out_shape, grid, in_specs, out_specs, flops, moved, exps=0):
    return pl.pallas_call(
        kernel,
        out_shape=out_shape,
        grid=grid,
        in_specs=in_specs,
        out_specs=out_specs,
        compiler_params=pltpu.CompilerParams(vmem_limit_bytes=VMEM_BYTES),
        cost_estimate=pl.CostEstimate(flops=flops, bytes_accessed=moved, transcendentals=exps),
    )


def local(queries, key_vectors, value_vectors, cotangent, compress_kernel, memory_reach):
    q, k, v, g = queries[0], key_vectors[0], value_vectors[0], cotangent[0]
    seg, width = q.shape
    feat = compress_kernel.shape[1]
    heads = width // feat
    slot = seg // TAPS
    count = lax.axis_size("seq")
    books = lax.axis_size("dp")
    position = lax.axis_index("seq")
    place = memory_reach

    group = 8
    grid = (heads // group,)
    cols = pl.BlockSpec((seg, group * feat), lambda i: (0, i))
    whole = pl.BlockSpec(compress_kernel.shape, lambda i: (0, 0))
    small = pl.BlockSpec((2, group, slot, feat), lambda i: (0, i, 0, 0))
    pair = pl.BlockSpec((2, 2, group, slot, feat), lambda i: (0, 0, i, 0, 0))
    stats = pl.BlockSpec((3, group, 1, seg), lambda i: (0, i, 0, 0))
    square = pl.BlockSpec((group, SLOTS * slot, seg), lambda i: (i, 0, 0))
    turned = pl.BlockSpec((TAPS * feat, group * slot), lambda i: (0, i))
    scalars = pl.BlockSpec(memory_space=pltpu.SMEM)
    rows_low = jax.ShapeDtypeStruct((seg, width), BF16)
    rows_full = jax.ShapeDtypeStruct((seg, width), F32)
    packed_shape = jax.ShapeDtypeStruct((2, heads, slot, feat), BF16)
    stat_shape = jax.ShapeDtypeStruct((3, heads, 1, seg), F32)
    square_shape = jax.ShapeDtypeStruct((heads, SLOTS * slot, seg), BF16)
    turned_shape = jax.ShapeDtypeStruct((TAPS * feat, heads * slot), BF16)
    row_bytes = 2 * seg * width
    unit = 2 * heads * seg * seg * feat

    kp, vp, packed = call(
        pack_kernel,
        (rows_low, rows_low, packed_shape),
        grid, [cols, cols, whole], (cols, cols, small), 4 * unit, 5 * row_bytes,
    )(k, v, compress_kernel)

    def shift(value, steps):
        return lax.ppermute(value, "seq", [(s, (s + steps) % count) for s in range(count)])

    def trade(value, bit, axis="seq"):
        size = lax.axis_size(axis)
        return lax.ppermute(value, axis, [(s, s ^ bit) for s in range(size)])

    near = lax.ppermute(packed, "seq", [(s, s + 1) for s in range(0, count, 2)])
    r2 = shift(packed, 2)
    r4 = shift(packed, 4)
    r4s = lax.ppermute(r4, "seq", [(s + 1, s) for s in range(0, count, 2)])

    own_stats, kt, vt = call(
        own_kernel,
        (stat_shape, turned_shape, turned_shape),
        grid, [cols] * 4, (stats, turned, turned), 2 * unit, 6 * row_bytes, heads * seg * seg,
    )(q, g, kp, vp)

    r2, own_stats, kt, vt = lax.optimization_barrier((r2, own_stats, kt, vt))
    r2s = trade(r2, 1)

    swap, t2, t4, w_mem, gs_mem, final = call(
        memory_kernel,
        (
            jax.ShapeDtypeStruct((2, 2, heads, slot, feat), BF16),
            packed_shape, packed_shape, square_shape, square_shape, stat_shape,
        ),
        grid,
        [scalars, cols, cols, stats] + [small] * 5,
        (pair, small, small, square, square, stats),
        4 * unit, 7 * row_bytes, heads * seg * seg,
    )(place, q, g, own_stats, near, r2, r2s, r4, r4s)

    swapped = trade(swap, 1)
    even = position % 2 == 0
    send2 = (t2.astype(F32) + jnp.where(even, swapped[1], swapped[0]).astype(F32)).astype(BF16)
    send4 = (
        t4.astype(F32) + jnp.where(even, jnp.zeros_like(swapped[1]), swapped[1]).astype(F32)
    ).astype(BF16)
    back2 = shift(send2, -2)
    back4 = shift(send4, -4)

    attended, grad_queries, own_keys, own_values = call(
        output_kernel,
        (rows_low, rows_low, rows_full, rows_full),
        grid,
        [scalars] + [cols] * 4 + [small] * 5 + [square, square, stats],
        (cols, cols, cols, cols),
        8 * unit, 15 * row_bytes, heads * seg * seg,
    )(place, q, g, kp, vp, near, r2, r2s, r4, r4s, w_mem, gs_mem, final)

    back2, back4, own_keys, own_values = lax.optimization_barrier(
        (back2, back4, own_keys, own_values)
    )
    flat = (2 * heads * slot, feat)
    kernel_rows = compress_kernel.shape[0]
    half_shape = jax.ShapeDtypeStruct((count // 2, kernel_rows // count, feat), F32)
    vmem = pl.BlockSpec(memory_space=pltpu.VMEM)
    memory_grads, mine, other = call(
        sum_kernel,
        (jax.ShapeDtypeStruct(flat, BF16), half_shape, half_shape),
        (1,),
        [
            scalars,
            pl.BlockSpec((1, *flat), lambda i: (0, 0, 0)),
            vmem, vmem, vmem, vmem,
        ],
        (vmem, vmem, vmem),
        unit, 4 * row_bytes,
    )(place, swapped.reshape(2, *flat), back2.reshape(flat), back4.reshape(flat), kt, vt)

    part = mine + trade(other, 1)
    bit = 2
    while bit < count:
        part = part.reshape(2, -1, *part.shape[1:])
        side = (position // bit) % 2
        kept = lax.dynamic_index_in_dim(part, side, 0, False)
        sent = lax.dynamic_index_in_dim(part, 1 - side, 0, False)
        part = kept + trade(sent, bit)
        bit *= 2
    part = part.reshape(kernel_rows // count, feat)
    bit = 1
    while bit < books:
        part = part + trade(part, bit, "dp")
        bit *= 2

    grads = memory_grads.reshape(2, heads, slot, feat)
    head_rows = pl.BlockSpec((group, slot, feat), lambda i: (i, 0, 0))
    grad_keys, grad_values = call(
        back_kernel,
        (rows_low, rows_low),
        grid, [head_rows, head_rows, whole, cols, cols], (cols, cols), 4 * unit, 7 * row_bytes,
    )(grads[0], grads[1], compress_kernel, own_keys, own_values)
    return (attended[None], grad_queries[None], grad_keys[None], grad_values[None], part)


def solution(mesh):
    rows = P("dp", "seq", None)
    return jax.shard_map(
        local,
        mesh=mesh,
        in_specs=(rows, rows, rows, rows, P(), P("dp", "seq")),
        out_specs=(rows, rows, rows, rows, P("seq", None)),
        check_vma=False,
    )
```

```python
import jax
import jax.numpy as jnp
from jax import lax
from jax.experimental import pallas as pl
from jax.experimental.pallas import tpu as pltpu
from jax.sharding import PartitionSpec as P

F32 = jnp.float32
BF16 = jnp.bfloat16
TAPS = 4
MASKED = -1e30
VMEM_BYTES = 24 * 2**20
PIECES = 1
BLOCKS = 5


def nt(a, b):
    return lax.dot_general(a, b, (((1,), (1,)), ((), ())), preferred_element_type=F32)


def nn(a, b):
    return lax.dot_general(a, b, (((1,), (0,)), ((), ())), preferred_element_type=F32)


def tn(a, b):
    return lax.dot_general(a, b, (((0,), (0,)), ((), ())), preferred_element_type=F32)


def tap_major(seg, inverse=False):
    slot = seg // TAPS
    spot = lax.broadcasted_iota(jnp.int32, (seg, seg), 1 if inverse else 0)
    token = lax.broadcasted_iota(jnp.int32, (seg, seg), 0 if inverse else 1)
    return (token == TAPS * (spot % slot) + spot // slot).astype(BF16)


def causal(seg):
    slot = seg // TAPS
    spot = lax.broadcasted_iota(jnp.int32, (seg, seg), 0)
    query = lax.broadcasted_iota(jnp.int32, (seg, seg), 1)
    return TAPS * (spot % slot) + spot // slot <= query


def head(h, feat):
    return slice(h * feat, (h + 1) * feat)


def staged(items, first, second, third, size=2):
    groups = [items[i : i + size] for i in range(0, len(items), size)]
    begun, turned = {}, {}
    for i in range(len(groups) + 2):
        if i < len(groups):
            for item in groups[i]:
                begun[item] = first(item)
        if i >= 2:
            for item in groups[i - 2]:
                third(item, *turned.pop(item))
        if 1 <= i <= len(groups):
            for item in groups[i - 1]:
                turned[item] = second(item, *begun.pop(item))


def tap_rows(rows, heads, feat):
    slot = rows.shape[0] // TAPS
    return jnp.concatenate(
        [
            jnp.concatenate(
                [rows[t * slot : (t + 1) * slot, head(h, feat)] for t in range(TAPS)], 1
            )
            for h in range(heads)
        ],
        0,
    )


def pack_kernel(reach_ref, k_hbm, v_hbm, q_hbm, g_hbm, w_hbm, *refs):
    *packed_refs, give_ref, rows_ref, w_ref, sems = refs
    seg, width = k_hbm.shape
    feat = w_hbm.shape[1]
    heads = width // feat
    slot = seg // TAPS
    share = heads // 2 // len(packed_refs)
    order = tap_major(seg)
    parts = [
        (half, i, kv)
        for half in range(2)
        for i in range(len(packed_refs))
        for kv in range(2)
    ]
    copies = []
    for n, (half, i, kv) in enumerate(parts):
        cols = pl.ds((half * len(packed_refs) + i) * share * feat, share * feat)
        copies.append(
            pltpu.make_async_copy(
                (k_hbm, v_hbm)[kv].at[:, cols], rows_ref.at[kv, :, cols], sems.at[n]
            )
        )
    copies.append(pltpu.make_async_copy(w_hbm, w_ref, sems.at[len(parts)]))
    for n in (0, 1, len(parts), *range(2, len(parts))):
        copies[n].start()
    start = pl.multiple_of((1 - lax.axis_index("seq") % 2) * (width // 2), width // 2)
    given = [
        pltpu.make_async_copy(
            src.at[:, pl.ds(start, width // 2)],
            give_ref.at[pl.ds(i * seg, seg)],
            sems.at[len(parts) + 1 + i],
        )
        for i, src in enumerate((k_hbm, v_hbm, q_hbm, g_hbm))
    ]
    for copy in given:
        copy.start()
    tail = (give_ref.shape[0] - 4 * seg, give_ref.shape[1])
    reach = jnp.full(tail, reach_ref[0, 0], jnp.int32)
    give_ref[4 * seg :] = reach.astype(F32).astype(BF16)
    for n, (half, i, kv) in enumerate(parts):
        copies[n].wait()
        begin = (half * len(packed_refs) + i) * share * feat
        rows = nn(order, rows_ref[kv, :, begin : begin + share * feat]).astype(BF16)
        if n == 0:
            copies[-1].wait()
        packed = nn(tap_rows(rows, share, feat), w_ref[...]).astype(BF16)
        packed_refs[i][kv, half] = packed.reshape(share, slot, feat)
    for copy in given:
        copy.wait()


def own_kernel(
    reach_ref, k_ref, v_ref, q_ref, g_ref, got_ref, w_ref,
    kv_ref, near_ref, stat_ref, kt_ref, vt_ref, bias_ref,
):
    seg, width = q_ref.shape
    feat = w_ref.shape[1]
    heads = width // feat
    slot = seg // TAPS
    scale = feat**-0.5
    mine = lax.axis_index("seq")
    partner = mine + 1 - 2 * (mine % 2)
    even = mine % 2 == 0
    sources = (mine - mine % 2, mine - 2, partner - 2, mine - 4, partner - 4)
    reach = jnp.full((slot, seg), reach_ref[0, 0], jnp.int32).astype(F32)
    reach_s = jnp.broadcast_to(got_ref[4 * seg : 4 * seg + 1, :seg].astype(F32), (slot, seg))
    for b, source in enumerate(sources):
        for u, (reader, limit) in enumerate(((mine, reach), (partner, reach_s))):
            steps = reader - source
            near_enough = (steps >= 1) & (steps <= 4) & (source >= 0)
            wanted = jnp.full((slot, seg), jnp.where(near_enough, steps, 9), jnp.int32)
            bias_ref[b * slot : (b + 1) * slot, u * seg : (u + 1) * seg] = jnp.where(
                wanted.astype(F32) <= limit, 0.0, MASKED
            )
    allowed = causal(seg)
    order = tap_major(seg)
    for kv, src in enumerate((k_ref, v_ref)):
        kv_ref[kv, 0] = nn(order, src[...]).astype(BF16)
        kv_ref[kv, 1] = nn(order, got_ref[kv * seg : (kv + 1) * seg]).astype(BF16)
    queries = (q_ref, got_ref.at[2 * seg : 3 * seg])
    grads = (g_ref, got_ref.at[3 * seg : 4 * seg])

    def first(item):
        h, u = item
        cols = head(h, feat)
        return (
            nt(kv_ref[0, u, :, cols], queries[u][:, cols]),
            nt(kv_ref[1, u, :, cols], grads[u][:, cols]),
        )

    def second(item, scores, grad_weights):
        h, u = item
        scores = jnp.where(allowed, scores * scale, MASKED)
        top = jnp.max(scores, axis=0, keepdims=True)
        raised = jnp.exp(scores - top)
        side = slice(u * seg, (u + 1) * seg)
        stat_ref[0, h, :, side] = top
        stat_ref[1, h, :, side] = jnp.sum(raised, axis=0, keepdims=True)
        stat_ref[2, h, :, side] = jnp.sum(raised * grad_weights, axis=0, keepdims=True)
        return ()

    staged([(h, u) for h in range(heads) for u in range(2)], first, second, lambda item: None, 4)
    rows = [
        tap_rows(jnp.where(even, kv_ref[kv, 0], kv_ref[kv, 1]), heads, feat) for kv in range(2)
    ]
    near = nn(jnp.concatenate(rows, 0), w_ref[...]).astype(BF16)
    near_ref[...] = near.reshape(near_ref.shape)
    for kv, dst in enumerate((kt_ref, vt_ref)):
        for u in range(2):
            lanes = slice(u * heads * slot, (u + 1) * heads * slot)
            for t in range(TAPS):
                part = kv_ref[kv, u, t * slot : (t + 1) * slot, :]
                stacked = jnp.concatenate([part[:, head(h, feat)] for h in range(heads)], 0)
                dst[t * feat : (t + 1) * feat, lanes] = stacked.T


def memory_rows(kv, h, slots):
    near_ref, *far_refs = slots
    return jnp.concatenate([near_ref[kv, h]] + [ref[kv, 0, h] for ref in far_refs], 0)


def memory_kernel(
    bias_ref, q_ref, qs_ref, g_ref, gs_ref, stat_ref,
    near_ref, r2_ref, r2s_ref, r4_ref, r4s_ref,
    t0_ref, t2_ref, t4_ref, w_ref, d_ref, fin_ref,
):
    seg, width = q_ref.shape
    heads = stat_ref.shape[1]
    feat = width // heads
    slot = seg // TAPS
    scale = feat**-0.5
    slots = (near_ref, r2_ref, r2s_ref, r4_ref, r4s_ref)

    def both(a_ref, b_ref, h):
        return jnp.concatenate([a_ref[:, head(h, feat)], b_ref[:, head(h, feat)]], 0)

    def first(h):
        return (
            nt(memory_rows(0, h, slots), both(q_ref, qs_ref, h)),
            nt(memory_rows(1, h, slots), both(g_ref, gs_ref, h)),
        )

    def second(h, scores, grad_weights):
        bias = bias_ref[...]
        scores = jnp.where(bias < 0.0, MASKED, scores * scale)
        own_top = stat_ref[0, h]
        top = jnp.maximum(own_top, jnp.max(scores, axis=0, keepdims=True))
        raised = jnp.exp(scores - top)
        fade = jnp.exp(own_top - top)
        total = stat_ref[1, h] * fade + jnp.sum(raised, axis=0, keepdims=True)
        delta = stat_ref[2, h] * fade + jnp.sum(raised * grad_weights, axis=0, keepdims=True)
        inverse = 1.0 / total
        delta = delta * inverse
        weights = raised * inverse
        weights_low = weights.astype(BF16)
        grad_scores = (weights * (grad_weights - delta) * scale).astype(BF16)
        w_ref[h] = weights_low
        d_ref[h] = grad_scores
        fin_ref[0, h] = top
        fin_ref[1, h] = inverse
        fin_ref[2, h] = delta
        return grad_scores, weights_low

    def third(h, grad_scores, weights_low):
        pair = (nn(grad_scores, both(q_ref, qs_ref, h)), nn(weights_low, both(g_ref, gs_ref, h)))
        for kv, terms in enumerate(pair):
            t0_ref[kv, h] = terms[:slot]
            terms = terms.astype(BF16)
            for i, (ref, u) in enumerate(((t2_ref, 0), (t2_ref, 1), (t4_ref, 0), (t4_ref, 1))):
                ref[u, kv, h] = terms[(i + 1) * slot : (i + 2) * slot]

    staged(list(range(heads)), first, second, third)


def output_kernel(*refs):
    q_ref, qs_ref, g_ref, gs_ref, kv_ref, near_ref = refs[:6]
    count = (len(refs) - 6 - 4) // 7
    pieces = [refs[6 + 7 * i : 13 + 7 * i] for i in range(count)]
    att_ref, gq_ref, give_ref, terms_ref = refs[-4:]
    seg, width = q_ref.shape
    feat = near_ref.shape[3]
    heads = width // feat
    share = heads // count
    scale = feat**-0.5
    allowed = causal(seg)
    queries, grads = (q_ref, qs_ref), (g_ref, gs_ref)

    def first(item):
        h, u = item
        cols = head(h, feat)
        return (
            nt(kv_ref[0, u, :, cols], queries[u][:, cols]),
            nt(kv_ref[1, u, :, cols], grads[u][:, cols]),
        )

    def second(item, scores, grad_weights):
        h, u = item
        fin_ref = pieces[h // share][6]
        side = slice(u * seg, (u + 1) * seg)
        top, inverse, delta = (fin_ref[i, h % share, :, side] for i in range(3))
        scores = jnp.where(allowed, scores * scale, MASKED)
        weights = jnp.exp(scores - top) * inverse
        grad_scores = (weights * (grad_weights - delta) * scale).astype(BF16)
        return grad_scores, weights.astype(BF16)

    def third(item, grad_scores, weights_low):
        h, u = item
        cols = head(h, feat)
        side = slice(u * seg, (u + 1) * seg)
        *far, w_ref, d_ref, _ = pieces[h // share]
        terms_ref[0, u, :, cols] = nn(grad_scores, queries[u][:, cols])
        terms_ref[1, u, :, cols] = nn(weights_low, grads[u][:, cols])

        def whole(kv, own, memory):
            rows = [near_ref[kv, h]] + [ref[kv, 0, h % share] for ref in far]
            return tn(own, kv_ref[kv, u, :, cols]) + tn(memory, jnp.concatenate(rows, 0))

        att = whole(1, weights_low, w_ref[h % share, :, side]).astype(BF16)
        gq = whole(0, grad_scores, d_ref[h % share, :, side]).astype(BF16)
        if u == 0:
            att_ref[:, cols] = att
            gq_ref[:, cols] = gq
        else:
            give_ref[0, :, cols] = att
            give_ref[1, :, cols] = gq

    staged([(h, u) for h in range(heads) for u in range(2)], first, second, third, 4)


def sum_kernel(kt_ref, vt_ref, *refs):
    mg_ref, mine_ref, other_ref = refs[-3:]
    pieces = [refs[i : i + 3] for i in range(0, len(refs) - 3, 3)]
    count = mine_ref.shape[0] * 2
    feat = mine_ref.shape[2]
    even = lax.axis_index("seq") % 2 == 0
    share, slot = pieces[0][0].shape[1:3]
    terms = jnp.zeros((kt_ref.shape[0], feat), F32)
    for kv, turned_ref in enumerate((kt_ref, vt_ref)):
        rows = []
        for u in range(2):
            for i, (t0_ref, a_ref, b_ref) in enumerate(pieces):
                near = jnp.where(even == (u == 0), t0_ref[kv], 0.0)
                low = (near + a_ref[u, kv].astype(F32) + b_ref[u, kv].astype(F32)).astype(BF16)
                mg_ref[kv, u, i * share : (i + 1) * share] = low
                rows.append(low.reshape(share * slot, feat))
        terms = terms + nn(turned_ref[...], jnp.concatenate(rows, 0))
    rows = terms.shape[0] // count
    bits = count.bit_length() - 1
    for p in range(0, count, 2):
        spot = int(format(p, "b").zfill(bits)[::-1], 2)
        first = terms[p * rows : (p + 1) * rows]
        second = terms[(p + 1) * rows : (p + 2) * rows]
        mine_ref[spot] = jnp.where(even, first, second)
        other_ref[spot] = jnp.where(even, second, first)


def back_kernel(mg_ref, w_ref, terms_ref, gk_ref, gv_ref, give_ref):
    seg = terms_ref.shape[2]
    heads, slot, feat = mg_ref.shape[2:]
    restore = tap_major(seg, inverse=True)
    for kv, out_ref in enumerate((gk_ref, gv_ref)):
        for u in range(2):
            back = nt(mg_ref[kv, u].reshape(heads * slot, feat), w_ref[...])
            columns = []
            for h in range(heads):
                rows = back[h * slot : (h + 1) * slot]
                columns.append(
                    jnp.concatenate([rows[:, head(t, feat)] for t in range(TAPS)], 0)
                )
            total = (terms_ref[kv, u] + jnp.concatenate(columns, 1)).astype(BF16)
            result = nn(restore, total).astype(BF16)
            if u == 0:
                out_ref[...] = result
            else:
                give_ref[kv] = result


def finish_kernel(a_in, b_in, got_ref, a_ref, b_ref, sems):
    del a_in, b_in
    width = got_ref.shape[2]
    start = pl.multiple_of((1 - lax.axis_index("seq") % 2) * width, width)
    copies = [
        pltpu.make_async_copy(got_ref.at[i], dst.at[:, pl.ds(start, width)], sems.at[i])
        for i, dst in enumerate((a_ref, b_ref))
    ]
    for copy in copies:
        copy.start()
    for copy in copies:
        copy.wait()


def call(kernel, out_shape, in_specs, out_specs, flops, moved, exps=0, scratch=(), aliases=None):
    return pl.pallas_call(
        kernel,
        out_shape=out_shape,
        grid=(1,),
        in_specs=in_specs,
        out_specs=out_specs,
        scratch_shapes=scratch,
        input_output_aliases=aliases or {},
        compiler_params=pltpu.CompilerParams(vmem_limit_bytes=VMEM_BYTES),
        cost_estimate=pl.CostEstimate(flops=flops, bytes_accessed=moved, transcendentals=exps),
    )


def local(queries, key_vectors, value_vectors, cotangent, compress_kernel, memory_reach):
    q, k, v, g = queries[0], key_vectors[0], value_vectors[0], cotangent[0]
    seg, width = q.shape
    feat = compress_kernel.shape[1]
    heads = width // feat
    half = heads // 2
    share = half // PIECES
    slot = seg // TAPS
    span = BLOCKS * slot
    count = lax.axis_size("seq")
    books = lax.axis_size("dp")
    position = lax.axis_index("seq")
    row_bytes = 2 * seg * width
    unit = 2 * heads * seg * seg * feat

    def side():
        return lax.axis_index("seq") % 2

    def shift(value, steps):
        return lax.ppermute(value, "seq", [(s, (s + steps) % count) for s in range(count)])

    def trade(value):
        return lax.ppermute(value, "seq", [(s, s ^ 1) for s in range(count)])

    def in_hbm(value):
        return pltpu.with_memory_space_constraint(value, pltpu.HBM)

    def shape(dims, kind=BF16):
        return jax.ShapeDtypeStruct(dims, kind)

    def full(dims):
        return pl.BlockSpec(dims, lambda i: (0,) * len(dims))

    scalars = pl.BlockSpec(memory_space=pltpu.SMEM)
    mine_cols = pl.BlockSpec((seg, half * feat), lambda i: (0, side()))
    other_cols = pl.BlockSpec((seg, half * feat), lambda i: (0, 1 - side()))
    far = pl.BlockSpec((2, 1, share, slot, feat), lambda i: (0, side(), 0, 0, 0))
    kernel_spec = full(compress_kernel.shape)

    hbm = pl.BlockSpec(memory_space=pltpu.HBM)
    rows = 4 * seg + 16
    *packed, give = call(
        pack_kernel,
        [shape((2, 2, share, slot, feat))] * PIECES + [shape((rows, half * feat))],
        [scalars] + [hbm] * 5,
        [full((2, 2, share, slot, feat))] * PIECES + [full((rows, half * feat))],
        3 * unit, 5 * row_bytes,
        scratch=[
            pltpu.VMEM((2, seg, width), BF16),
            pltpu.VMEM(compress_kernel.shape, BF16),
            pltpu.SemaphoreType.DMA((4 * PIECES + 5,)),
        ],
    )(memory_reach, *[in_hbm(a) for a in (k, v, q, g, compress_kernel)])
    got = trade(give)

    r2, r4 = [], []
    for piece in packed:
        r2.append(shift(piece, 2))
        r4.append(shift(piece, 4))
    kvp, near, own_stats, kt, vt, bias = call(
        own_kernel,
        (
            shape((2, 2, seg, half * feat)),
            shape((2, half, slot, feat)),
            shape((3, half, 1, 2 * seg), F32),
            shape((TAPS * feat, heads * slot)),
            shape((TAPS * feat, heads * slot)),
            shape((span, 2 * seg), F32),
        ),
        [scalars] + [mine_cols] * 4 + [full((rows, half * feat)), kernel_spec],
        (
            full((2, 2, seg, half * feat)),
            full((2, half, slot, feat)),
            full((3, half, 1, 2 * seg)),
            full((TAPS * feat, heads * slot)),
            full((TAPS * feat, heads * slot)),
            full((span, 2 * seg)),
        ),
        5 * unit, 8 * row_bytes, heads * seg * seg,
    )(memory_reach, k, v, q, g, got, compress_kernel)

    pieces, sums, terms = [], [], []
    for i in range(PIECES):
        if i == 0:
            first2, own_stats, near = lax.optimization_barrier((r2[0], own_stats, near))
            r2[0] = first2
        else:
            r2[i], r4[i], t2, t4 = lax.optimization_barrier((r2[i], r4[i], *terms[-1]))
            terms[-1] = (t2, t4)
        slots = [r2[i], trade(r2[i]), r4[i], trade(r4[i])]
        cols = pl.BlockSpec((seg, share * feat), lambda s, i=i: (0, side() * PIECES + i))
        got_q = pl.BlockSpec((seg, share * feat), lambda s, i=i: (2, i))
        got_g = pl.BlockSpec((seg, share * feat), lambda s, i=i: (3, i))
        stats = pl.BlockSpec((3, share, 1, 2 * seg), lambda s, i=i: (0, i, 0, 0))
        near_spec = pl.BlockSpec((2, share, slot, feat), lambda s, i=i: (0, i, 0, 0))
        t0, t2, t4, w_mem, d_mem, final = call(
            memory_kernel,
            (
                shape((2, share, slot, feat), F32),
                shape((2, 2, share, slot, feat)),
                shape((2, 2, share, slot, feat)),
                shape((share, span, 2 * seg)),
                shape((share, span, 2 * seg)),
                shape((3, share, 1, 2 * seg), F32),
            ),
            [full((span, 2 * seg)), cols, got_q, cols, got_g, stats, near_spec] + [far] * 4,
            (
                full((2, share, slot, feat)),
                full((2, 2, share, slot, feat)),
                full((2, 2, share, slot, feat)),
                full((share, span, 2 * seg)),
                full((share, span, 2 * seg)),
                full((3, share, 1, 2 * seg)),
            ),
            4 * unit // PIECES, 8 * row_bytes // PIECES, heads * seg * seg,
        )(bias, q, got, g, got, own_stats, near, *slots)
        sums.append([t0])
        terms.append((t2, t4))
        pieces.append([*slots, w_mem, d_mem, final])

    for total, (t2, t4) in zip(sums, terms):
        total += [shift(t2, -2), shift(t4, -4)]
    piece_specs = [
        far, far, far, far,
        full((share, span, 2 * seg)), full((share, span, 2 * seg)), full((3, share, 1, 2 * seg)),
    ]
    attended, grad_queries, give_first, own_terms = call(
        output_kernel,
        (
            shape((seg, width)),
            shape((seg, width)),
            shape((2, seg, half * feat)),
            shape((2, 2, seg, half * feat), F32),
        ),
        [
            mine_cols,
            pl.BlockSpec((seg, half * feat), lambda i: (2, 0)),
            mine_cols,
            pl.BlockSpec((seg, half * feat), lambda i: (3, 0)),
        ]
        + [full((2, 2, seg, half * feat)), full((2, half, slot, feat))]
        + piece_specs * PIECES,
        (
            mine_cols, mine_cols,
            full((2, seg, half * feat)),
            full((2, 2, seg, half * feat)),
        ),
        8 * unit, 12 * row_bytes, heads * seg * seg,
    )(q, got, g, got, kvp, near, *[a for piece in pieces for a in piece])

    def finish(a, b, give):
        anywhere = pl.BlockSpec(memory_space=pl.ANY)
        return call(
            finish_kernel,
            (shape((seg, width)), shape((seg, width))),
            [anywhere] * 3,
            (anywhere, anywhere),
            0, 2 * row_bytes,
            scratch=[pltpu.SemaphoreType.DMA((2,))],
            aliases={0: 0, 1: 1},
        )(a, b, trade(give))

    attended, grad_queries = finish(attended, grad_queries, give_first)
    sums[-1][2], own_terms = lax.optimization_barrier((sums[-1][2], own_terms))
    kernel_rows = compress_kernel.shape[0]
    half_dims = (count // 2, kernel_rows // count, feat)
    sum_specs = [
        full((2, share, slot, feat)),
        full((2, 2, share, slot, feat)),
        full((2, 2, share, slot, feat)),
    ]
    memory_grads, mine, other = call(
        sum_kernel,
        (shape((2, 2, half, slot, feat)), shape(half_dims, F32), shape(half_dims, F32)),
        [full((TAPS * feat, heads * slot))] * 2 + sum_specs * PIECES,
        (full((2, 2, half, slot, feat)), full(half_dims), full(half_dims)),
        unit, 4 * row_bytes,
    )(kt, vt, *[a for piece in sums for a in piece])

    grad_keys, grad_values, give_last = call(
        back_kernel,
        (shape((seg, width)), shape((seg, width)), shape((2, seg, half * feat))),
        [full((2, 2, half, slot, feat)), kernel_spec, full((2, 2, seg, half * feat))],
        (mine_cols, mine_cols, full((2, seg, half * feat))),
        4 * unit, 7 * row_bytes,
    )(memory_grads, compress_kernel, own_terms)

    grad_keys, grad_values = finish(grad_keys, grad_values, give_last)
    part = mine + trade(other)
    part, (attended, grad_queries, grad_keys, grad_values) = reduce_rest(
        part, position, count, books, [(attended, grad_queries), (grad_keys, grad_values)]
    )
    return (attended[None], grad_queries[None], grad_keys[None], grad_values[None], part)


def reduce_rest(part, position, count, books, beside):
    bits = []
    step = 2
    while step < count:
        bits.append(("seq", step))
        step *= 2
    step = 1
    while step < books:
        bits.append(("dp", step))
        step *= 2
    for i in range(0, len(bits), 2):
        phase = bits[i : i + 2]
        split = [step for axis, step in phase if axis == "seq"]
        part = part.reshape(2 ** len(split), -1, *part.shape[1:])
        mine = jnp.int32(0)
        for step in split:
            mine = mine * 2 + (position // step) % 2
        arrived = []
        for mask in range(1, 2 ** len(phase)):
            flip, seq_xor, dp_xor = 0, 0, 0
            for j, (axis, step) in enumerate(phase):
                chosen = (mask >> (len(phase) - 1 - j)) & 1
                if axis == "seq":
                    flip = flip * 2 + chosen
                    seq_xor |= chosen * step
                else:
                    dp_xor |= chosen * step
            sent = lax.dynamic_index_in_dim(part, mine ^ flip, 0, False)
            pairs = [
                (s * books + d, (s ^ seq_xor) * books + (d ^ dp_xor))
                for s in range(count)
                for d in range(books)
            ]
            arrived.append(lax.ppermute(sent, ("seq", "dp"), pairs))
        part = lax.dynamic_index_in_dim(part, mine, 0, False)
        if i // 2 < len(beside):
            arrived[0], *beside[i // 2] = lax.optimization_barrier(
                (arrived[0], *beside[i // 2])
            )
        for piece in arrived:
            part = part + piece
    return part.reshape(-1, part.shape[-1]), [array for arrays in beside for array in arrays]


def solution(mesh):
    rows = P("dp", "seq", None)
    return jax.shard_map(
        local,
        mesh=mesh,
        in_specs=(rows, rows, rows, rows, P(), P("dp", "seq")),
        out_specs=(rows, rows, rows, rows, P("seq", None)),
        check_vma=False,
    )
```

```python
import jax
import jax.numpy as jnp
from jax import lax
from jax.experimental import pallas as pl
from jax.experimental.pallas import tpu as pltpu
from jax.sharding import PartitionSpec as P

F32 = jnp.float32
BF16 = jnp.bfloat16
TAPS = 4
MASKED = -1e30
VMEM_BYTES = 24 * 2**20
BLOCKS = 5


def nt(a, b):
    return lax.dot_general(a, b, (((1,), (1,)), ((), ())), preferred_element_type=F32)


def nn(a, b):
    return lax.dot_general(a, b, (((1,), (0,)), ((), ())), preferred_element_type=F32)


def tn(a, b):
    return lax.dot_general(a, b, (((0,), (0,)), ((), ())), preferred_element_type=F32)


def tap_major(seg, inverse=False):
    slot = seg // TAPS
    spot = lax.broadcasted_iota(jnp.int32, (seg, seg), 1 if inverse else 0)
    token = lax.broadcasted_iota(jnp.int32, (seg, seg), 0 if inverse else 1)
    return (token == TAPS * (spot % slot) + spot // slot).astype(BF16)


def causal(seg):
    slot = seg // TAPS
    spot = lax.broadcasted_iota(jnp.int32, (seg, seg), 0)
    query = lax.broadcasted_iota(jnp.int32, (seg, seg), 1)
    return TAPS * (spot % slot) + spot // slot <= query


def head(h, feat):
    return slice(h * feat, (h + 1) * feat)


def staged(items, first, second, third, size=2):
    groups = [items[i : i + size] for i in range(0, len(items), size)]
    begun, turned = {}, {}
    for i in range(len(groups) + 2):
        if i < len(groups):
            for item in groups[i]:
                begun[item] = first(item)
        if i >= 2:
            for item in groups[i - 2]:
                third(item, *turned.pop(item))
        if 1 <= i <= len(groups):
            for item in groups[i - 1]:
                turned[item] = second(item, *begun.pop(item))


def tap_rows(rows, heads, feat):
    slot = rows.shape[0] // TAPS
    return jnp.concatenate(
        [
            jnp.concatenate(
                [rows[t * slot : (t + 1) * slot, head(h, feat)] for t in range(TAPS)], 1
            )
            for h in range(heads)
        ],
        0,
    )


def pack_kernel(
    reach_ref, k_hbm, v_hbm, q_hbm, g_hbm, w_hbm,
    mine_ref, other_ref, give_ref, rows_ref, w_ref, sems,
):
    seg, width = k_hbm.shape
    feat = w_hbm.shape[1]
    half = width // 2
    heads = half // feat
    slot = seg // TAPS
    order = tap_major(seg)
    core = lax.axis_index("seq") % 2
    begin = [pl.multiple_of(core * half, half), pl.multiple_of((1 - core) * half, half)]
    steps = [(part, kv) for part in range(2) for kv in range(2)]
    pairs = [
        ((k_hbm, v_hbm)[kv].at[:, pl.ds(begin[part], half)], rows_ref.at[part, kv])
        for part, kv in steps
    ]
    pairs.insert(2, (w_hbm, w_ref))
    pairs += [
        (src.at[:, pl.ds(begin[1], half)], give_ref.at[pl.ds((2 + i) * seg, seg)])
        for i, src in enumerate((q_hbm, g_hbm))
    ]
    copies = [pltpu.make_async_copy(*pair, sems.at[n]) for n, pair in enumerate(pairs)]
    for copy in copies:
        copy.start()
    for n, (part, kv) in enumerate(steps):
        copies[n if n < 2 else n + 1].wait()
        rows = nn(order, rows_ref[part, kv]).astype(BF16)
        if n == 0:
            copies[2].wait()
        packed = nn(tap_rows(rows, heads, feat), w_ref[...]).astype(BF16)
        (mine_ref, other_ref)[part][kv] = packed.reshape(heads, slot, feat)
        if part == 1:
            give_ref[kv * seg : (kv + 1) * seg] = rows_ref[part, kv]
    for copy in copies[5:]:
        copy.wait()
    give_ref[4 * seg :] = reach_ref[...]


def own_kernel(
    k_ref, v_ref, q_ref, g_ref, reach_ref, got_ref, w_ref,
    kv_ref, near_ref, stat_ref, kt_ref, vt_ref, bias_ref,
):
    seg, width = q_ref.shape
    feat = w_ref.shape[1]
    heads = width // feat
    slot = seg // TAPS
    scale = feat**-0.5
    mine = lax.axis_index("seq")
    partner = mine + 1 - 2 * (mine % 2)
    even = mine % 2 == 0
    sources = (mine - mine % 2, mine - 2, partner - 2, mine - 4, partner - 4)
    reach = jnp.broadcast_to(reach_ref[:1].astype(F32), (slot, seg))
    reach_s = jnp.broadcast_to(got_ref[4 * seg : 4 * seg + 1, :seg].astype(F32), (slot, seg))
    for b, source in enumerate(sources):
        for u, (reader, limit) in enumerate(((mine, reach), (partner, reach_s))):
            steps = reader - source
            near_enough = (steps >= 1) & (steps <= 4) & (source >= 0)
            wanted = jnp.full((slot, seg), jnp.where(near_enough, steps, 9), jnp.int32)
            bias_ref[b * slot : (b + 1) * slot, u * seg : (u + 1) * seg] = jnp.where(
                wanted.astype(F32) <= limit, 0.0, MASKED
            )
    allowed = causal(seg)
    order = tap_major(seg)
    for kv, src in enumerate((k_ref, v_ref)):
        kv_ref[kv, 0] = nn(order, src[...]).astype(BF16)
        kv_ref[kv, 1] = nn(order, got_ref[kv * seg : (kv + 1) * seg]).astype(BF16)
    queries = (q_ref, got_ref.at[2 * seg : 3 * seg])
    grads = (g_ref, got_ref.at[3 * seg : 4 * seg])

    def first(item):
        h, u = item
        cols = head(h, feat)
        return (
            nt(kv_ref[0, u, :, cols], queries[u][:, cols]),
            nt(kv_ref[1, u, :, cols], grads[u][:, cols]),
        )

    def second(item, scores, grad_weights):
        h, u = item
        scores = jnp.where(allowed, scores * scale, MASKED)
        top = jnp.max(scores, axis=0, keepdims=True)
        raised = jnp.exp(scores - top)
        side = slice(u * seg, (u + 1) * seg)
        stat_ref[0, h, :, side] = top
        stat_ref[1, h, :, side] = jnp.sum(raised, axis=0, keepdims=True)
        stat_ref[2, h, :, side] = jnp.sum(raised * grad_weights, axis=0, keepdims=True)
        return ()

    staged([(h, u) for h in range(heads) for u in range(2)], first, second, lambda item: None, 4)
    rows = [
        tap_rows(jnp.where(even, kv_ref[kv, 0], kv_ref[kv, 1]), heads, feat) for kv in range(2)
    ]
    near = nn(jnp.concatenate(rows, 0), w_ref[...]).astype(BF16)
    near_ref[...] = near.reshape(near_ref.shape)
    for kv, dst in enumerate((kt_ref, vt_ref)):
        for u in range(2):
            lanes = slice(u * heads * slot, (u + 1) * heads * slot)
            for t in range(TAPS):
                part = kv_ref[kv, u, t * slot : (t + 1) * slot, :]
                stacked = jnp.concatenate([part[:, head(h, feat)] for h in range(heads)], 0)
                dst[t * feat : (t + 1) * feat, lanes] = stacked.T


def memory_rows(kv, h, slots):
    return jnp.concatenate([ref[kv, h] for ref in slots], 0)


def memory_kernel(
    bias_ref, q_ref, qs_ref, g_ref, gs_ref, stat_ref,
    near_ref, r2_ref, r2s_ref, r4_ref, r4s_ref,
    t0_ref, t2_ref, t4_ref, w_ref, d_ref, fin_ref,
):
    seg, width = q_ref.shape
    heads = stat_ref.shape[1]
    feat = width // heads
    slot = seg // TAPS
    scale = feat**-0.5
    slots = (near_ref, r2_ref, r2s_ref, r4_ref, r4s_ref)

    def both(a_ref, b_ref, h):
        return jnp.concatenate([a_ref[:, head(h, feat)], b_ref[:, head(h, feat)]], 0)

    def first(h):
        return (
            nt(memory_rows(0, h, slots), both(q_ref, qs_ref, h)),
            nt(memory_rows(1, h, slots), both(g_ref, gs_ref, h)),
        )

    def second(h, scores, grad_weights):
        bias = bias_ref[...]
        scores = jnp.where(bias < 0.0, MASKED, scores * scale)
        own_top = stat_ref[0, h]
        top = jnp.maximum(own_top, jnp.max(scores, axis=0, keepdims=True))
        raised = jnp.exp(scores - top)
        fade = jnp.exp(own_top - top)
        total = stat_ref[1, h] * fade + jnp.sum(raised, axis=0, keepdims=True)
        delta = stat_ref[2, h] * fade + jnp.sum(raised * grad_weights, axis=0, keepdims=True)
        inverse = 1.0 / total
        delta = delta * inverse
        weights = raised * inverse
        weights_low = weights.astype(BF16)
        grad_scores = (weights * (grad_weights - delta) * scale).astype(BF16)
        w_ref[h] = weights_low
        d_ref[h] = grad_scores
        fin_ref[0, h] = top
        fin_ref[1, h] = inverse
        fin_ref[2, h] = delta
        return grad_scores, weights_low

    def third(h, grad_scores, weights_low):
        pair = (nn(grad_scores, both(q_ref, qs_ref, h)), nn(weights_low, both(g_ref, gs_ref, h)))
        for kv, terms in enumerate(pair):
            t0_ref[kv, h] = terms[:slot]
            terms = terms.astype(BF16)
            for i in range(4):
                (t2_ref, t4_ref)[i // 2][i % 2, kv, h] = terms[(i + 1) * slot : (i + 2) * slot]

    staged(list(range(heads)), first, second, third)


def output_kernel(*refs):
    q_ref, qs_ref, g_ref, gs_ref, kv_ref = refs[:5]
    slots = refs[5 : 5 + BLOCKS]
    w_ref, d_ref, fin_ref, att_ref, gq_ref, give_ref, terms_ref = refs[5 + BLOCKS :]
    seg, width = q_ref.shape
    feat = slots[0].shape[3]
    heads = width // feat
    scale = feat**-0.5
    allowed = causal(seg)
    queries, grads = (q_ref, qs_ref), (g_ref, gs_ref)

    def first(item):
        h, u = item
        cols = head(h, feat)
        return (
            nt(kv_ref[0, u, :, cols], queries[u][:, cols]),
            nt(kv_ref[1, u, :, cols], grads[u][:, cols]),
        )

    def second(item, scores, grad_weights):
        h, u = item
        side = slice(u * seg, (u + 1) * seg)
        top, inverse, delta = (fin_ref[i, h, :, side] for i in range(3))
        scores = jnp.where(allowed, scores * scale, MASKED)
        weights = jnp.exp(scores - top) * inverse
        grad_scores = (weights * (grad_weights - delta) * scale).astype(BF16)
        return grad_scores, weights.astype(BF16)

    def third(item, grad_scores, weights_low):
        h, u = item
        cols = head(h, feat)
        side = slice(u * seg, (u + 1) * seg)
        terms_ref[0, u, :, cols] = nn(grad_scores, queries[u][:, cols])
        terms_ref[1, u, :, cols] = nn(weights_low, grads[u][:, cols])

        def whole(kv, own, memory):
            return tn(own, kv_ref[kv, u, :, cols]) + tn(memory, memory_rows(kv, h, slots))

        att = whole(1, weights_low, w_ref[h, :, side]).astype(BF16)
        gq = whole(0, grad_scores, d_ref[h, :, side]).astype(BF16)
        if u == 0:
            att_ref[:, cols] = att
            gq_ref[:, cols] = gq
        else:
            give_ref[0, :, cols] = att
            give_ref[1, :, cols] = gq

    staged([(h, u) for h in range(heads) for u in range(2)], first, second, third, 4)


def sum_kernel(kt_ref, vt_ref, t0_ref, b4_ref, b2_ref, mg_ref, mine_ref, other_ref):
    count = mine_ref.shape[0] * 2
    feat = mine_ref.shape[2]
    even = lax.axis_index("seq") % 2 == 0
    terms = jnp.zeros((kt_ref.shape[0], feat), F32)
    for kv, turned_ref in enumerate((kt_ref, vt_ref)):
        rows = []
        for u in range(2):
            low = jnp.where(even == (u == 0), t0_ref[kv], 0.0)
            low = (low + b2_ref[u, kv].astype(F32) + b4_ref[u, kv].astype(F32)).astype(BF16)
            mg_ref[kv, u] = low
            rows.append(low.reshape(-1, feat))
        terms = terms + nn(turned_ref[...], jnp.concatenate(rows, 0))
    rows = terms.shape[0] // count
    bits = count.bit_length() - 1
    for p in range(0, count, 2):
        spot = int(format(p, "b").zfill(bits)[::-1], 2)
        first = terms[p * rows : (p + 1) * rows]
        second = terms[(p + 1) * rows : (p + 2) * rows]
        mine_ref[spot] = jnp.where(even, first, second)
        other_ref[spot] = jnp.where(even, second, first)


def back_kernel(mg_ref, w_ref, terms_ref, gk_ref, gv_ref, give_ref):
    seg = terms_ref.shape[2]
    heads, slot, feat = mg_ref.shape[2:]
    restore = tap_major(seg, inverse=True)
    for kv, out_ref in enumerate((gk_ref, gv_ref)):
        for u in range(2):
            back = nt(mg_ref[kv, u].reshape(heads * slot, feat), w_ref[...])
            columns = []
            for h in range(heads):
                rows = back[h * slot : (h + 1) * slot]
                columns.append(
                    jnp.concatenate([rows[:, head(t, feat)] for t in range(TAPS)], 0)
                )
            total = (terms_ref[kv, u] + jnp.concatenate(columns, 1)).astype(BF16)
            result = nn(restore, total).astype(BF16)
            if u == 0:
                out_ref[...] = result
            else:
                give_ref[kv] = result


def finish_kernel(a_in, b_in, got_ref, a_ref, b_ref, sems):
    del a_in, b_in
    width = got_ref.shape[2]
    start = pl.multiple_of((1 - lax.axis_index("seq") % 2) * width, width)
    copies = [
        pltpu.make_async_copy(got_ref.at[i], dst.at[:, pl.ds(start, width)], sems.at[i])
        for i, dst in enumerate((a_ref, b_ref))
    ]
    for copy in copies:
        copy.start()
    for copy in copies:
        copy.wait()


def call(kernel, out_shape, in_specs, out_specs, flops, moved, exps=0, scratch=(), aliases=None):
    return pl.pallas_call(
        kernel,
        out_shape=out_shape,
        grid=(1,),
        in_specs=in_specs,
        out_specs=out_specs,
        scratch_shapes=scratch,
        input_output_aliases=aliases or {},
        compiler_params=pltpu.CompilerParams(vmem_limit_bytes=VMEM_BYTES),
        cost_estimate=pl.CostEstimate(flops=flops, bytes_accessed=moved, transcendentals=exps),
    )


def local(queries, key_vectors, value_vectors, cotangent, compress_kernel, memory_reach):
    q, k, v, g = queries[0], key_vectors[0], value_vectors[0], cotangent[0]
    seg, width = q.shape
    feat = compress_kernel.shape[1]
    heads = width // feat
    half = heads // 2
    slot = seg // TAPS
    span = BLOCKS * slot
    count = lax.axis_size("seq")
    books = lax.axis_size("dp")
    position = lax.axis_index("seq")
    row_bytes = 2 * seg * width
    unit = 2 * heads * seg * seg * feat

    def side():
        return lax.axis_index("seq") % 2

    def shift(value, steps):
        return lax.ppermute(value, "seq", [(s, (s + steps) % count) for s in range(count)])

    def cross(value, steps):
        return lax.ppermute(value, "seq", [(s, ((s ^ 1) + steps) % count) for s in range(count)])

    def trade(value, flip=1):
        return lax.ppermute(value, "seq", [(s, s ^ flip) for s in range(count)])

    def in_hbm(value):
        return pltpu.with_memory_space_constraint(value, pltpu.HBM)

    def shape(dims, kind=BF16):
        return jax.ShapeDtypeStruct(dims, kind)

    def full(dims):
        return pl.BlockSpec(dims, lambda i: (0,) * len(dims))

    mine_cols = pl.BlockSpec((seg, half * feat), lambda i: (0, side()))
    kernel_spec = full(compress_kernel.shape)

    hbm = pl.BlockSpec(memory_space=pltpu.HBM)
    rows = 4 * seg + 16
    half_dims = (2, half, slot, feat)
    packed_mine, packed_other, give = call(
        pack_kernel,
        (shape(half_dims), shape(half_dims), shape((rows, half * feat))),
        [full((16, half * feat))] + [hbm] * 5,
        (full(half_dims), full(half_dims), full((rows, half * feat))),
        3 * unit, 5 * row_bytes,
        scratch=[
            pltpu.VMEM((2, 2, seg, half * feat), BF16),
            pltpu.VMEM(compress_kernel.shape, BF16),
            pltpu.SemaphoreType.DMA((7,)),
        ],
    )(jnp.full((16, half * feat), memory_reach[0, 0].astype(BF16)), *[in_hbm(a) for a in (k, v, q, g, compress_kernel)])
    got = trade(give)

    r4 = shift(packed_mine, 4)
    r2 = shift(packed_mine, 2)
    r4s = cross(packed_other, 4)
    r2s = cross(packed_other, 2)
    kvp, near, own_stats, kt, vt, bias = call(
        own_kernel,
        (
            shape((2, 2, seg, half * feat)),
            shape((2, half, slot, feat)),
            shape((3, half, 1, 2 * seg), F32),
            shape((TAPS * feat, heads * slot)),
            shape((TAPS * feat, heads * slot)),
            shape((span, 2 * seg), F32),
        ),
        [mine_cols] * 4
        + [
            pl.BlockSpec((16, seg), lambda i: (4 * seg // 16, 0)),
            full((rows, half * feat)),
            kernel_spec,
        ],
        (
            full((2, 2, seg, half * feat)),
            full((2, half, slot, feat)),
            full((3, half, 1, 2 * seg)),
            full((TAPS * feat, heads * slot)),
            full((TAPS * feat, heads * slot)),
            full((span, 2 * seg)),
        ),
        unit, 8 * row_bytes, heads * seg * seg,
    )(k, v, q, g, give, got, compress_kernel)

    slots = [near, r2, r2s, r4, r4s]
    got_q = pl.BlockSpec((seg, half * feat), lambda i: (2, 0))
    got_g = pl.BlockSpec((seg, half * feat), lambda i: (3, 0))
    one = (2, half, slot, feat)
    soft = (half, span, 2 * seg)
    stats = (3, half, 1, 2 * seg)
    pair = (2, 2, half, slot, feat)
    t0, t2, t4, w_mem, d_mem, final = call(
        memory_kernel,
        (shape(one, F32), *[shape(pair)] * 2, shape(soft), shape(soft), shape(stats, F32)),
        [full((span, 2 * seg)), mine_cols, got_q, mine_cols, got_g, full(stats)]
        + [full(one)] * BLOCKS,
        (full(one), *[full(pair)] * 2, full(soft), full(soft), full(stats)),
        4 * unit, 8 * row_bytes, heads * seg * seg,
    )(bias, q, got, g, got, own_stats, *slots)

    back4 = shift(t4, -4)
    back2 = shift(t2, -2)
    attended, grad_queries, give_first, own_terms = call(
        output_kernel,
        (
            shape((seg, width)),
            shape((seg, width)),
            shape((2, seg, half * feat)),
            shape((2, 2, seg, half * feat), F32),
        ),
        [mine_cols, got_q, mine_cols, got_g, full((2, 2, seg, half * feat))]
        + [full(one)] * BLOCKS
        + [full(soft), full(soft), full(stats)],
        (
            mine_cols, mine_cols,
            full((2, seg, half * feat)),
            full((2, 2, seg, half * feat)),
        ),
        8 * unit, 12 * row_bytes, heads * seg * seg,
    )(q, got, g, got, kvp, *slots, w_mem, d_mem, final)

    def finish(a, b, give):
        anywhere = pl.BlockSpec(memory_space=pl.ANY)
        return call(
            finish_kernel,
            (shape((seg, width)), shape((seg, width))),
            [anywhere] * 3,
            (anywhere, anywhere),
            0, 2 * row_bytes,
            scratch=[pltpu.SemaphoreType.DMA((2,))],
            aliases={0: 0, 1: 1},
        )(a, b, trade(give))

    attended, grad_queries = finish(attended, grad_queries, give_first)
    back2, own_terms = lax.optimization_barrier((back2, own_terms))
    kernel_rows = compress_kernel.shape[0]
    split = (count // 2, kernel_rows // count, feat)
    turned = full((TAPS * feat, heads * slot))
    memory_grads, mine, other = call(
        sum_kernel,
        (shape(pair), shape(split, F32), shape(split, F32)),
        [turned] * 2 + [full(one)] + [full(pair)] * 2,
        (full(pair), full(split), full(split)),
        unit, 4 * row_bytes,
    )(kt, vt, t0, back4, back2)

    grad_keys, grad_values, give_last = call(
        back_kernel,
        (shape((seg, width)), shape((seg, width)), shape((2, seg, half * feat))),
        [full(pair), kernel_spec, full((2, 2, seg, half * feat))],
        (mine_cols, mine_cols, full((2, seg, half * feat))),
        4 * unit, 7 * row_bytes,
    )(memory_grads, compress_kernel, own_terms)

    grad_keys, grad_values = finish(grad_keys, grad_values, give_last)
    part = mine + trade(other)
    part, (attended, grad_queries, grad_keys, grad_values) = reduce_rest(
        part, position, count, books, [(attended, grad_queries), (grad_keys, grad_values)]
    )
    return (attended[None], grad_queries[None], grad_keys[None], grad_values[None], part)


def reduce_rest(part, position, count, books, beside):
    bits = []
    step = 2
    while step < count:
        bits.append(("seq", step))
        step *= 2
    step = 1
    while step < books:
        bits.append(("dp", step))
        step *= 2
    for i in range(0, len(bits), 2):
        phase = bits[i : i + 2]
        split = [step for axis, step in phase if axis == "seq"]
        part = part.reshape(2 ** len(split), -1, *part.shape[1:])
        mine = jnp.int32(0)
        for step in split:
            mine = mine * 2 + (position // step) % 2
        arrived = []
        for mask in range(1, 2 ** len(phase)):
            flip, seq_xor, dp_xor = 0, 0, 0
            for j, (axis, step) in enumerate(phase):
                chosen = (mask >> (len(phase) - 1 - j)) & 1
                if axis == "seq":
                    flip = flip * 2 + chosen
                    seq_xor |= chosen * step
                else:
                    dp_xor |= chosen * step
            sent = lax.dynamic_index_in_dim(part, mine ^ flip, 0, False)
            pairs = [
                (s * books + d, (s ^ seq_xor) * books + (d ^ dp_xor))
                for s in range(count)
                for d in range(books)
            ]
            arrived.append(lax.ppermute(sent, ("seq", "dp"), pairs))
        part = lax.dynamic_index_in_dim(part, mine, 0, False)
        if i // 2 < len(beside):
            arrived[0], *beside[i // 2] = lax.optimization_barrier(
                (arrived[0], *beside[i // 2])
            )
        for piece in arrived:
            part = part + piece
    return part.reshape(-1, part.shape[-1]), [array for arrays in beside for array in arrays]


def solution(mesh):
    rows = P("dp", "seq", None)
    return jax.shard_map(
        local,
        mesh=mesh,
        in_specs=(rows, rows, rows, rows, P(), P("dp", "seq")),
        out_specs=(rows, rows, rows, rows, P("seq", None)),
        check_vma=False,
    )
```

```python
import jax
import jax.numpy as jnp
from jax import lax
from jax.experimental import pallas as pl
from jax.experimental.pallas import tpu as pltpu
from jax.sharding import PartitionSpec as P

F32 = jnp.float32
BF16 = jnp.bfloat16
TAPS = 4
MASKED = -1e30
VMEM_BYTES = 24 * 2**20
BLOCKS = 5


def nt(a, b):
    return lax.dot_general(a, b, (((1,), (1,)), ((), ())), preferred_element_type=F32)


def nn(a, b):
    return lax.dot_general(a, b, (((1,), (0,)), ((), ())), preferred_element_type=F32)


def tn(a, b):
    return lax.dot_general(a, b, (((0,), (0,)), ((), ())), preferred_element_type=F32)


def tap_major(seg, inverse=False):
    slot = seg // TAPS
    spot = lax.broadcasted_iota(jnp.int32, (seg, seg), 1 if inverse else 0)
    token = lax.broadcasted_iota(jnp.int32, (seg, seg), 0 if inverse else 1)
    return (token == TAPS * (spot % slot) + spot // slot).astype(BF16)


def causal(seg):
    slot = seg // TAPS
    spot = lax.broadcasted_iota(jnp.int32, (seg, seg), 0)
    query = lax.broadcasted_iota(jnp.int32, (seg, seg), 1)
    return TAPS * (spot % slot) + spot // slot <= query


def head(h, feat):
    return slice(h * feat, (h + 1) * feat)


def staged(items, first, second, third, size=2):
    groups = [items[i : i + size] for i in range(0, len(items), size)]
    begun, turned = {}, {}
    for i in range(len(groups) + 2):
        if i < len(groups):
            for item in groups[i]:
                begun[item] = first(item)
        if i >= 2:
            for item in groups[i - 2]:
                third(item, *turned.pop(item))
        if 1 <= i <= len(groups):
            for item in groups[i - 1]:
                turned[item] = second(item, *begun.pop(item))


def tap_rows(rows, heads, feat):
    slot = rows.shape[0] // TAPS
    return jnp.concatenate(
        [
            jnp.concatenate(
                [rows[t * slot : (t + 1) * slot, head(h, feat)] for t in range(TAPS)], 1
            )
            for h in range(heads)
        ],
        0,
    )


def pack_kernel(
    k_hbm, v_hbm, q_hbm, g_hbm, w_hbm,
    mine_ref, other_ref, give_ref, rows_ref, w_ref, sems,
):
    seg, width = k_hbm.shape
    feat = w_hbm.shape[1]
    half = width // 2
    heads = half // feat
    slot = seg // TAPS
    order = tap_major(seg)
    core = lax.axis_index("seq") % 2
    begin = [pl.multiple_of(core * half, half), pl.multiple_of((1 - core) * half, half)]
    steps = [(part, kv) for part in range(2) for kv in range(2)]
    pairs = [
        ((k_hbm, v_hbm)[kv].at[:, pl.ds(begin[part], half)], rows_ref.at[part, kv])
        for part, kv in steps
    ]
    pairs.insert(2, (w_hbm, w_ref))
    pairs += [
        (src.at[:, pl.ds(begin[1], half)], give_ref.at[pl.ds((2 + i) * seg, seg)])
        for i, src in enumerate((q_hbm, g_hbm))
    ]
    copies = [pltpu.make_async_copy(*pair, sems.at[n]) for n, pair in enumerate(pairs)]
    for copy in copies:
        copy.start()
    sorted_rows = []
    for n, (part, kv) in enumerate(steps):
        copies[n if n < 2 else n + 1].wait()
        sorted_rows.append(nn(order, rows_ref[part, kv]).astype(BF16))
    copies[2].wait()
    for (part, kv), rows in zip(steps, sorted_rows):
        packed = nn(tap_rows(rows, heads, feat), w_ref[...]).astype(BF16)
        (mine_ref, other_ref)[part][kv] = packed.reshape(heads, slot, feat)
        if part == 1:
            give_ref[kv * seg : (kv + 1) * seg] = rows_ref[part, kv]
    for copy in copies[5:]:
        copy.wait()


def own_kernel(
    reach_ref, reach_s_ref, k_ref, v_ref, q_ref, g_ref, got_ref, w_ref,
    kv_ref, near_ref, stat_ref, kt_ref, vt_ref, bias_ref,
):
    seg, width = q_ref.shape
    feat = w_ref.shape[1]
    heads = width // feat
    slot = seg // TAPS
    scale = feat**-0.5
    mine = lax.axis_index("seq")
    partner = mine + 1 - 2 * (mine % 2)
    even = mine % 2 == 0
    sources = (mine - mine % 2, mine - 2, partner - 2, mine - 4, partner - 4)
    for b, source in enumerate(sources):
        for u, (reader, limit) in enumerate(((mine, reach_ref), (partner, reach_s_ref))):
            steps = reader - source
            shown = (steps >= 1) & (steps <= jnp.minimum(limit[0, 0], 4)) & (source >= 0)
            bias_ref[b * slot : (b + 1) * slot, u * seg : (u + 1) * seg] = jnp.full(
                (slot, seg), jnp.where(shown, 0.0, MASKED), F32
            )
    allowed = causal(seg)
    order = tap_major(seg)
    for kv, src in enumerate((k_ref, v_ref)):
        kv_ref[kv, 0] = nn(order, src[...]).astype(BF16)
        kv_ref[kv, 1] = nn(order, got_ref[kv * seg : (kv + 1) * seg]).astype(BF16)
    queries = (q_ref, got_ref.at[2 * seg : 3 * seg])
    grads = (g_ref, got_ref.at[3 * seg : 4 * seg])

    def first(item):
        h, u = item
        cols = head(h, feat)
        return (
            nt(kv_ref[0, u, :, cols], queries[u][:, cols]),
            nt(kv_ref[1, u, :, cols], grads[u][:, cols]),
        )

    def second(item, scores, grad_weights):
        h, u = item
        scores = jnp.where(allowed, scores * scale, MASKED)
        top = jnp.max(scores, axis=0, keepdims=True)
        raised = jnp.exp(scores - top)
        side = slice(u * seg, (u + 1) * seg)
        stat_ref[0, h, :, side] = top
        stat_ref[1, h, :, side] = jnp.sum(raised, axis=0, keepdims=True)
        stat_ref[2, h, :, side] = jnp.sum(raised * grad_weights, axis=0, keepdims=True)
        return ()

    staged([(h, u) for h in range(heads) for u in range(2)], first, second, lambda item: None, 4)
    rows = [
        tap_rows(jnp.where(even, kv_ref[kv, 0], kv_ref[kv, 1]), heads, feat) for kv in range(2)
    ]
    near = nn(jnp.concatenate(rows, 0), w_ref[...]).astype(BF16)
    near_ref[...] = near.reshape(near_ref.shape)
    for kv, dst in enumerate((kt_ref, vt_ref)):
        for u in range(2):
            lanes = slice(u * heads * slot, (u + 1) * heads * slot)
            for t in range(TAPS):
                part = kv_ref[kv, u, t * slot : (t + 1) * slot, :]
                stacked = jnp.concatenate([part[:, head(h, feat)] for h in range(heads)], 0)
                dst[t * feat : (t + 1) * feat, lanes] = stacked.T


def memory_rows(kv, h, slots):
    return jnp.concatenate([ref[kv, h] for ref in slots], 0)


def memory_kernel(
    bias_ref, q_ref, qs_ref, g_ref, gs_ref, stat_ref,
    near_ref, r2_ref, r2s_ref, r4_ref, r4s_ref,
    t0_ref, t2_ref, t4_ref, w_ref, d_ref, fin_ref,
):
    seg, width = q_ref.shape
    heads = stat_ref.shape[1]
    feat = width // heads
    slot = seg // TAPS
    scale = feat**-0.5
    slots = (near_ref, r2_ref, r2s_ref, r4_ref, r4s_ref)

    def both(a_ref, b_ref, h):
        return jnp.concatenate([a_ref[:, head(h, feat)], b_ref[:, head(h, feat)]], 0)

    def first(h):
        return (
            nt(memory_rows(0, h, slots), both(q_ref, qs_ref, h)),
            nt(memory_rows(1, h, slots), both(g_ref, gs_ref, h)),
        )

    def second(h, scores, grad_weights):
        bias = bias_ref[...]
        scores = jnp.where(bias < 0.0, MASKED, scores * scale)
        own_top = stat_ref[0, h]
        top = jnp.maximum(own_top, jnp.max(scores, axis=0, keepdims=True))
        raised = jnp.exp(scores - top)
        fade = jnp.exp(own_top - top)
        total = stat_ref[1, h] * fade + jnp.sum(raised, axis=0, keepdims=True)
        delta = stat_ref[2, h] * fade + jnp.sum(raised * grad_weights, axis=0, keepdims=True)
        inverse = 1.0 / total
        delta = delta * inverse
        weights = raised * inverse
        weights_low = weights.astype(BF16)
        grad_scores = (weights * (grad_weights - delta) * scale).astype(BF16)
        w_ref[h] = weights_low
        d_ref[h] = grad_scores
        fin_ref[0, h] = top
        fin_ref[1, h] = inverse
        fin_ref[2, h] = delta
        return grad_scores, weights_low

    def third(h, grad_scores, weights_low):
        pair = (nn(grad_scores, both(q_ref, qs_ref, h)), nn(weights_low, both(g_ref, gs_ref, h)))
        for kv, terms in enumerate(pair):
            t0_ref[kv, h] = terms[:slot]
            terms = terms.astype(BF16)
            for i in range(4):
                (t2_ref, t4_ref)[i // 2][i % 2, kv, h] = terms[(i + 1) * slot : (i + 2) * slot]

    staged(list(range(heads)), first, second, third)


def output_kernel(*refs):
    q_ref, qs_ref, g_ref, gs_ref, kv_ref = refs[:5]
    slots = refs[5 : 5 + BLOCKS]
    w_ref, d_ref, fin_ref, *results = refs[5 + BLOCKS :]
    att_ref, gq_ref, givea_ref, giveg_ref, terms_ref = results
    seg, width = q_ref.shape
    feat = slots[0].shape[3]
    heads = width // feat
    scale = feat**-0.5
    allowed = causal(seg)
    queries, grads = (q_ref, qs_ref), (g_ref, gs_ref)

    def first(item):
        h, u = item
        cols = head(h, feat)
        return (
            nt(kv_ref[0, u, :, cols], queries[u][:, cols]),
            nt(kv_ref[1, u, :, cols], grads[u][:, cols]),
        )

    def second(item, scores, grad_weights):
        h, u = item
        side = slice(u * seg, (u + 1) * seg)
        top, inverse, delta = (fin_ref[i, h, :, side] for i in range(3))
        scores = jnp.where(allowed, scores * scale, MASKED)
        weights = jnp.exp(scores - top) * inverse
        grad_scores = (weights * (grad_weights - delta) * scale).astype(BF16)
        return grad_scores, weights.astype(BF16)

    def third(item, grad_scores, weights_low):
        h, u = item
        cols = head(h, feat)
        side = slice(u * seg, (u + 1) * seg)
        terms_ref[0, u, :, cols] = nn(grad_scores, queries[u][:, cols])
        terms_ref[1, u, :, cols] = nn(weights_low, grads[u][:, cols])

        def whole(kv, own, memory):
            return tn(own, kv_ref[kv, u, :, cols]) + tn(memory, memory_rows(kv, h, slots))

        att = whole(1, weights_low, w_ref[h, :, side]).astype(BF16)
        gq = whole(0, grad_scores, d_ref[h, :, side]).astype(BF16)
        if u == 0:
            att_ref[:, cols] = att
            gq_ref[:, cols] = gq
        else:
            givea_ref[:, cols] = att
            giveg_ref[:, cols] = gq

    staged([(h, u) for h in range(heads) for u in range(2)], first, second, third, 4)


def first_sum_kernel(t0_ref, b4_ref, low_ref):
    even = lax.axis_index("seq") % 2 == 0
    for kv in range(2):
        for u in range(2):
            low = jnp.where(even == (u == 0), t0_ref[kv], 0.0)
            low_ref[u, kv] = low + b4_ref[u, kv].astype(F32)


def sum_kernel(kt_ref, vt_ref, low_ref, b2_ref, mg_ref, mine_ref, other_ref):
    count = mine_ref.shape[0] * 2
    feat = mine_ref.shape[2]
    even = lax.axis_index("seq") % 2 == 0
    terms = jnp.zeros((kt_ref.shape[0], feat), F32)
    for kv, turned_ref in enumerate((kt_ref, vt_ref)):
        rows = []
        for u in range(2):
            low = (low_ref[u, kv] + b2_ref[u, kv].astype(F32)).astype(BF16)
            mg_ref[kv, u] = low
            rows.append(low.reshape(-1, feat))
        terms = terms + nn(turned_ref[...], jnp.concatenate(rows, 0))
    rows = terms.shape[0] // count
    bits = count.bit_length() - 1
    for p in range(0, count, 2):
        spot = int(format(p, "b").zfill(bits)[::-1], 2)
        first = terms[p * rows : (p + 1) * rows]
        second = terms[(p + 1) * rows : (p + 2) * rows]
        mine_ref[spot] = jnp.where(even, first, second)
        other_ref[spot] = jnp.where(even, second, first).astype(BF16)


def back_kernel(mg_ref, w_ref, terms_ref, gk_ref, gv_ref, givek_ref, givev_ref):
    seg = terms_ref.shape[2]
    heads, slot, feat = mg_ref.shape[2:]
    restore = tap_major(seg, inverse=True)
    for kv, out_ref in enumerate((gk_ref, gv_ref)):
        for u in range(2):
            back = nt(mg_ref[kv, u].reshape(heads * slot, feat), w_ref[...])
            columns = []
            for h in range(heads):
                rows = back[h * slot : (h + 1) * slot]
                columns.append(
                    jnp.concatenate([rows[:, head(t, feat)] for t in range(TAPS)], 0)
                )
            total = (terms_ref[kv, u] + jnp.concatenate(columns, 1)).astype(BF16)
            result = nn(restore, total).astype(BF16)
            if u == 0:
                out_ref[...] = result
            else:
                (givek_ref, givev_ref)[kv][...] = result


def finish_kernel(a_in, b_in, got_a, got_b, a_ref, b_ref, sems):
    del a_in, b_in
    width = got_a.shape[1]
    start = pl.multiple_of((1 - lax.axis_index("seq") % 2) * width, width)
    copies = [
        pltpu.make_async_copy(got, dst.at[:, pl.ds(start, width)], sems.at[i])
        for i, (got, dst) in enumerate(((got_a, a_ref), (got_b, b_ref)))
    ]
    for copy in copies:
        copy.start()
    for copy in copies:
        copy.wait()


def call(kernel, out_shape, in_specs, out_specs, flops, moved, exps=0, scratch=(), aliases=None):
    return pl.pallas_call(
        kernel,
        out_shape=out_shape,
        grid=(1,),
        in_specs=in_specs,
        out_specs=out_specs,
        scratch_shapes=scratch,
        input_output_aliases=aliases or {},
        compiler_params=pltpu.CompilerParams(vmem_limit_bytes=VMEM_BYTES),
        cost_estimate=pl.CostEstimate(flops=flops, bytes_accessed=moved, transcendentals=exps),
    )


def local(queries, key_vectors, value_vectors, cotangent, compress_kernel, memory_reach):
    q, k, v, g = queries[0], key_vectors[0], value_vectors[0], cotangent[0]
    seg, width = q.shape
    feat = compress_kernel.shape[1]
    heads = width // feat
    half = heads // 2
    slot = seg // TAPS
    span = BLOCKS * slot
    count = lax.axis_size("seq")
    books = lax.axis_size("dp")
    position = lax.axis_index("seq")
    row_bytes = 2 * seg * width
    unit = 2 * heads * seg * seg * feat

    def side():
        return lax.axis_index("seq") % 2

    def shift(value, steps):
        return lax.ppermute(value, "seq", [(s, (s + steps) % count) for s in range(count)])

    def cross(value, steps):
        return lax.ppermute(value, "seq", [(s, ((s ^ 1) + steps) % count) for s in range(count)])

    def trade(value, flip=1):
        return lax.ppermute(value, "seq", [(s, s ^ flip) for s in range(count)])

    def in_hbm(value):
        return pltpu.with_memory_space_constraint(value, pltpu.HBM)

    def shape(dims, kind=BF16):
        return jax.ShapeDtypeStruct(dims, kind)

    def full(dims):
        return pl.BlockSpec(dims, lambda i: (0,) * len(dims))

    mine_cols = pl.BlockSpec((seg, half * feat), lambda i: (0, side()))
    kernel_spec = full(compress_kernel.shape)

    hbm = pl.BlockSpec(memory_space=pltpu.HBM)
    rows = 4 * seg
    half_dims = (2, half, slot, feat)
    packed_mine, packed_other, give = call(
        pack_kernel,
        (shape(half_dims), shape(half_dims), shape((rows, half * feat))),
        [hbm] * 5,
        (full(half_dims), full(half_dims), full((rows, half * feat))),
        3 * unit, 5 * row_bytes,
        scratch=[
            pltpu.VMEM((2, 2, seg, half * feat), BF16),
            pltpu.VMEM(compress_kernel.shape, BF16),
            pltpu.SemaphoreType.DMA((7,)),
        ],
    )(*[in_hbm(a) for a in (k, v, q, g, compress_kernel)])
    got = trade(give)

    r4 = shift(packed_mine, 4)
    r2 = shift(packed_mine, 2)
    r4s = cross(packed_other, 4)
    r2s = cross(packed_other, 2)
    got, late_reach = lax.optimization_barrier((got, memory_reach))
    scalar = pl.BlockSpec(memory_space=pltpu.SMEM)
    kvp, near, own_stats, kt, vt, bias = call(
        own_kernel,
        (
            shape((2, 2, seg, half * feat)),
            shape((2, half, slot, feat)),
            shape((3, half, 1, 2 * seg), F32),
            shape((TAPS * feat, heads * slot)),
            shape((TAPS * feat, heads * slot)),
            shape((span, 2 * seg), F32),
        ),
        [scalar] * 2 + [mine_cols] * 4 + [full((rows, half * feat)), kernel_spec],
        (
            full((2, 2, seg, half * feat)),
            full((2, half, slot, feat)),
            full((3, half, 1, 2 * seg)),
            full((TAPS * feat, heads * slot)),
            full((TAPS * feat, heads * slot)),
            full((span, 2 * seg)),
        ),
        unit, 8 * row_bytes, heads * seg * seg,
    )(late_reach, trade(late_reach), k, v, q, g, got, compress_kernel)

    slots = [near, r2, r2s, r4, r4s]
    got_q = pl.BlockSpec((seg, half * feat), lambda i: (2, 0))
    got_g = pl.BlockSpec((seg, half * feat), lambda i: (3, 0))
    one = (2, half, slot, feat)
    soft = (half, span, 2 * seg)
    stats = (3, half, 1, 2 * seg)
    pair = (2, 2, half, slot, feat)
    t0, t2, t4, w_mem, d_mem, final = call(
        memory_kernel,
        (shape(one, F32), *[shape(pair)] * 2, shape(soft), shape(soft), shape(stats, F32)),
        [full((span, 2 * seg)), mine_cols, got_q, mine_cols, got_g, full(stats)]
        + [full(one)] * BLOCKS,
        (full(one), *[full(pair)] * 2, full(soft), full(soft), full(stats)),
        4 * unit, 8 * row_bytes, heads * seg * seg,
    )(bias, q, got, g, got, own_stats, *slots)

    back4 = shift(t4, -4)
    back2 = shift(t2, -2)
    attended, grad_queries, give_a, give_g, own_terms = call(
        output_kernel,
        (
            shape((seg, width)),
            shape((seg, width)),
            shape((seg, half * feat)),
            shape((seg, half * feat)),
            shape((2, 2, seg, half * feat), F32),
        ),
        [mine_cols, got_q, mine_cols, got_g, full((2, 2, seg, half * feat))]
        + [full(one)] * BLOCKS
        + [full(soft), full(soft), full(stats)],
        (
            mine_cols, mine_cols,
            full((seg, half * feat)),
            full((seg, half * feat)),
            full((2, 2, seg, half * feat)),
        ),
        8 * unit, 12 * row_bytes, heads * seg * seg,
    )(q, got, g, got, kvp, *slots, w_mem, d_mem, final)

    def finish(a, b, give_a, give_b):
        anywhere = pl.BlockSpec(memory_space=pl.ANY)
        return call(
            finish_kernel,
            (shape((seg, width)), shape((seg, width))),
            [anywhere] * 4,
            (anywhere, anywhere),
            0, 2 * row_bytes,
            scratch=[pltpu.SemaphoreType.DMA((2,))],
            aliases={0: 0, 1: 1},
        )(a, b, trade(give_a), trade(give_b))

    attended, grad_queries = finish(attended, grad_queries, give_a, give_g)
    kernel_rows = compress_kernel.shape[0]
    split = (count // 2, kernel_rows // count, feat)
    turned = full((TAPS * feat, heads * slot))
    low = call(
        first_sum_kernel, shape(pair, F32), [full(one), full(pair)], full(pair), 0, 2 * row_bytes * 10
    )(t0, back4)
    low, own_terms = lax.optimization_barrier((low, own_terms))
    memory_grads, mine, other = call(
        sum_kernel,
        (shape(pair), shape(split, F32), shape(split)),
        [turned] * 2 + [full(pair)] * 2,
        (full(pair), full(split), full(split)),
        unit, 4 * row_bytes,
    )(kt, vt, low, back2)

    grad_keys, grad_values, give_k, give_v = call(
        back_kernel,
        (shape((seg, width)), shape((seg, width)), *[shape((seg, half * feat))] * 2),
        [full(pair), kernel_spec, full((2, 2, seg, half * feat))],
        (mine_cols, mine_cols, *[full((seg, half * feat))] * 2),
        4 * unit, 7 * row_bytes,
    )(memory_grads, compress_kernel, own_terms)

    grad_keys, grad_values = finish(grad_keys, grad_values, give_k, give_v)
    part = mine + trade(other).astype(F32)
    part, (attended, grad_queries, grad_keys, grad_values) = reduce_rest(
        part, position, count, books, [(attended, grad_queries), (grad_keys, grad_values)]
    )
    return (attended[None], grad_queries[None], grad_keys[None], grad_values[None], part)


def reduce_rest(part, position, count, books, beside):
    bits = []
    step = 2
    while step < count:
        bits.append(("seq", step))
        step *= 2
    step = 1
    while step < books:
        bits.append(("dp", step))
        step *= 2
    for i in range(0, len(bits), 2):
        phase = bits[i : i + 2]
        split = [step for axis, step in phase if axis == "seq"]
        part = part.reshape(2 ** len(split), -1, *part.shape[1:])
        mine = jnp.int32(0)
        for step in split:
            mine = mine * 2 + (position // step) % 2
        arrived = []
        for mask in range(1, 2 ** len(phase)):
            flip, seq_xor, dp_xor = 0, 0, 0
            for j, (axis, step) in enumerate(phase):
                chosen = (mask >> (len(phase) - 1 - j)) & 1
                if axis == "seq":
                    flip = flip * 2 + chosen
                    seq_xor |= chosen * step
                else:
                    dp_xor |= chosen * step
            sent = lax.dynamic_index_in_dim(part, mine ^ flip, 0, False)
            pairs = [
                (s * books + d, (s ^ seq_xor) * books + (d ^ dp_xor))
                for s in range(count)
                for d in range(books)
            ]
            arrived.append(lax.ppermute(sent.astype(BF16), ("seq", "dp"), pairs))
        part = lax.dynamic_index_in_dim(part, mine, 0, False)
        if i // 2 < len(beside):
            arrived[0], *beside[i // 2] = lax.optimization_barrier(
                (arrived[0], *beside[i // 2])
            )
        for piece in arrived:
            part = part + piece.astype(F32)
    return part.reshape(-1, part.shape[-1]), [array for arrays in beside for array in arrays]


def solution(mesh):
    rows = P("dp", "seq", None)
    return jax.shard_map(
        local,
        mesh=mesh,
        in_specs=(rows, rows, rows, rows, P(), P("dp", "seq")),
        out_specs=(rows, rows, rows, rows, P("seq", None)),
        check_vma=False,
    )
```

```python
import jax
import jax.numpy as jnp
from jax import lax
from jax.experimental import pallas as pl
from jax.experimental.pallas import tpu as pltpu
from jax.sharding import PartitionSpec as P

F32 = jnp.float32
BF16 = jnp.bfloat16
TAPS = 4
MASKED = -1e30
VMEM_BYTES = 24 * 2**20
BLOCKS = 5


def nt(a, b):
    return lax.dot_general(a, b, (((1,), (1,)), ((), ())), preferred_element_type=F32)


def nn(a, b):
    return lax.dot_general(a, b, (((1,), (0,)), ((), ())), preferred_element_type=F32)


def tn(a, b):
    return lax.dot_general(a, b, (((0,), (0,)), ((), ())), preferred_element_type=F32)


def tap_major(seg, inverse=False):
    slot = seg // TAPS
    spot = lax.broadcasted_iota(jnp.int32, (seg, seg), 1 if inverse else 0)
    token = lax.broadcasted_iota(jnp.int32, (seg, seg), 0 if inverse else 1)
    return (token == TAPS * (spot % slot) + spot // slot).astype(BF16)


def causal(seg):
    slot = seg // TAPS
    spot = lax.broadcasted_iota(jnp.int32, (seg, seg), 0)
    query = lax.broadcasted_iota(jnp.int32, (seg, seg), 1)
    return TAPS * (spot % slot) + spot // slot <= query


def head(h, feat):
    return slice(h * feat, (h + 1) * feat)


def staged(items, first, second, third, size=2):
    groups = [items[i : i + size] for i in range(0, len(items), size)]
    begun, turned = {}, {}
    for i in range(len(groups) + 2):
        if i < len(groups):
            for item in groups[i]:
                begun[item] = first(item)
        if i >= 2:
            for item in groups[i - 2]:
                third(item, *turned.pop(item))
        if 1 <= i <= len(groups):
            for item in groups[i - 1]:
                turned[item] = second(item, *begun.pop(item))


def tap_rows(rows, heads, feat):
    slot = rows.shape[0] // TAPS
    return jnp.concatenate(
        [
            jnp.concatenate(
                [rows[t * slot : (t + 1) * slot, head(h, feat)] for t in range(TAPS)], 1
            )
            for h in range(heads)
        ],
        0,
    )


def pack_kernel(
    k_hbm, v_hbm, q_hbm, g_hbm, w_hbm,
    mine_ref, other_ref, give_ref, rows_ref, w_ref, sems,
):
    seg, width = k_hbm.shape
    feat = w_hbm.shape[1]
    half = width // 2
    heads = half // feat
    slot = seg // TAPS
    order = tap_major(seg)
    core = lax.axis_index("seq") % 2
    begin = [pl.multiple_of(core * half, half), pl.multiple_of((1 - core) * half, half)]
    steps = [(part, kv) for part in range(2) for kv in range(2)]
    pairs = [
        ((k_hbm, v_hbm)[kv].at[:, pl.ds(begin[part], half)], rows_ref.at[part, kv])
        for part, kv in steps
    ]
    pairs.insert(2, (w_hbm, w_ref))
    pairs += [
        (src.at[:, pl.ds(begin[1], half)], give_ref.at[pl.ds((2 + i) * seg, seg)])
        for i, src in enumerate((q_hbm, g_hbm))
    ]
    copies = [pltpu.make_async_copy(*pair, sems.at[n]) for n, pair in enumerate(pairs)]
    for copy in copies:
        copy.start()
    sorted_rows = []
    for n, (part, kv) in enumerate(steps):
        copies[n if n < 2 else n + 1].wait()
    copies[2].wait()
    every = jnp.concatenate([rows_ref[part, kv] for part, kv in steps], 1)
    every = nn(order, every).astype(BF16)
    half_width = heads * feat
    sorted_rows = [
        every[:, n * half_width : (n + 1) * half_width] for n in range(len(steps))
    ]
    rows = jnp.concatenate([tap_rows(rows, heads, feat) for rows in sorted_rows], 0)
    packed = nn(rows, w_ref[...]).astype(BF16).reshape(len(steps), heads, slot, feat)
    for n, (part, kv) in enumerate(steps):
        (mine_ref, other_ref)[part][kv] = packed[n]
        if part == 1:
            give_ref[kv * seg : (kv + 1) * seg] = rows_ref[part, kv]
    for copy in copies[5:]:
        copy.wait()


def own_kernel(
    reach_ref, reach_s_ref, k_ref, v_ref, q_ref, g_ref, got_ref, w_ref,
    kv_ref, near_ref, stat_ref, kt_ref, vt_ref, bias_ref,
):
    seg, width = q_ref.shape
    feat = w_ref.shape[1]
    heads = width // feat
    slot = seg // TAPS
    scale = feat**-0.5
    mine = lax.axis_index("seq")
    partner = mine + 1 - 2 * (mine % 2)
    even = mine % 2 == 0
    sources = (mine - mine % 2, mine - 2, partner - 2, mine - 4, partner - 4)
    for b, source in enumerate(sources):
        for u, (reader, limit) in enumerate(((mine, reach_ref), (partner, reach_s_ref))):
            steps = reader - source
            shown = (steps >= 1) & (steps <= jnp.minimum(limit[0, 0], 4)) & (source >= 0)
            bias_ref[b * slot : (b + 1) * slot, u * seg : (u + 1) * seg] = jnp.full(
                (slot, seg), jnp.where(shown, 0.0, MASKED), F32
            )
    allowed = causal(seg)
    order = tap_major(seg)
    for kv, src in enumerate((k_ref, v_ref)):
        kv_ref[kv, 0] = nn(order, src[...]).astype(BF16)
        kv_ref[kv, 1] = nn(order, got_ref[kv * seg : (kv + 1) * seg]).astype(BF16)
    queries = (q_ref, got_ref.at[2 * seg : 3 * seg])
    grads = (g_ref, got_ref.at[3 * seg : 4 * seg])

    def first(item):
        h, u = item
        cols = head(h, feat)
        return (
            nt(kv_ref[0, u, :, cols], queries[u][:, cols]),
            nt(kv_ref[1, u, :, cols], grads[u][:, cols]),
        )

    def second(item, scores, grad_weights):
        h, u = item
        scores = jnp.where(allowed, scores * scale, MASKED)
        top = jnp.max(scores, axis=0, keepdims=True)
        raised = jnp.exp(scores - top)
        side = slice(u * seg, (u + 1) * seg)
        stat_ref[0, h, :, side] = top
        stat_ref[1, h, :, side] = jnp.sum(raised, axis=0, keepdims=True)
        stat_ref[2, h, :, side] = jnp.sum(raised * grad_weights, axis=0, keepdims=True)
        return ()

    staged([(h, u) for h in range(heads) for u in range(2)], first, second, lambda item: None, 4)
    rows = [
        tap_rows(jnp.where(even, kv_ref[kv, 0], kv_ref[kv, 1]), heads, feat) for kv in range(2)
    ]
    near = nn(jnp.concatenate(rows, 0), w_ref[...]).astype(BF16)
    near_ref[...] = near.reshape(near_ref.shape)
    for kv, dst in enumerate((kt_ref, vt_ref)):
        for u in range(2):
            lanes = slice(u * heads * slot, (u + 1) * heads * slot)
            for t in range(TAPS):
                part = kv_ref[kv, u, t * slot : (t + 1) * slot, :]
                stacked = jnp.concatenate([part[:, head(h, feat)] for h in range(heads)], 0)
                dst[t * feat : (t + 1) * feat, lanes] = stacked.T


def memory_rows(kv, h, slots):
    return jnp.concatenate([ref[kv, h] for ref in slots], 0)


def memory_kernel(
    bias_ref, q_ref, qs_ref, g_ref, gs_ref, stat_ref,
    near_ref, r2_ref, r2s_ref, r4_ref, r4s_ref,
    t0_ref, t2_ref, t4_ref, w_ref, d_ref, fin_ref,
):
    seg, width = q_ref.shape
    heads = stat_ref.shape[1]
    feat = width // heads
    slot = seg // TAPS
    scale = feat**-0.5
    slots = (near_ref, r2_ref, r2s_ref, r4_ref, r4s_ref)

    def both(a_ref, b_ref, h):
        return jnp.concatenate([a_ref[:, head(h, feat)], b_ref[:, head(h, feat)]], 0)

    def first(h):
        return (
            nt(memory_rows(0, h, slots), both(q_ref, qs_ref, h)),
            nt(memory_rows(1, h, slots), both(g_ref, gs_ref, h)),
        )

    def second(h, scores, grad_weights):
        bias = bias_ref[...]
        scores = jnp.where(bias < 0.0, MASKED, scores * scale)
        own_top = stat_ref[0, h]
        top = jnp.maximum(own_top, jnp.max(scores, axis=0, keepdims=True))
        raised = jnp.exp(scores - top)
        fade = jnp.exp(own_top - top)
        total = stat_ref[1, h] * fade + jnp.sum(raised, axis=0, keepdims=True)
        delta = stat_ref[2, h] * fade + jnp.sum(raised * grad_weights, axis=0, keepdims=True)
        inverse = 1.0 / total
        delta = delta * inverse
        weights = raised * inverse
        weights_low = weights.astype(BF16)
        grad_scores = (weights * (grad_weights - delta) * scale).astype(BF16)
        w_ref[h] = weights_low
        d_ref[h] = grad_scores
        fin_ref[0, h] = top
        fin_ref[1, h] = inverse
        fin_ref[2, h] = delta
        return grad_scores, weights_low

    def third(h, grad_scores, weights_low):
        pair = (nn(grad_scores, both(q_ref, qs_ref, h)), nn(weights_low, both(g_ref, gs_ref, h)))
        for kv, terms in enumerate(pair):
            t0_ref[kv, h] = terms[:slot]
            terms = terms.astype(BF16)
            for i in range(4):
                (t2_ref, t4_ref)[i // 2][i % 2, kv, h] = terms[(i + 1) * slot : (i + 2) * slot]

    staged(list(range(heads)), first, second, third)


def output_kernel(*refs):
    q_ref, qs_ref, g_ref, gs_ref, kv_ref = refs[:5]
    slots = refs[5 : 5 + BLOCKS]
    w_ref, d_ref, fin_ref, *results = refs[5 + BLOCKS :]
    att_ref, gq_ref, givea_ref, giveg_ref, terms_ref = results
    seg, width = q_ref.shape
    feat = slots[0].shape[3]
    heads = width // feat
    scale = feat**-0.5
    allowed = causal(seg)
    queries, grads = (q_ref, qs_ref), (g_ref, gs_ref)

    def first(item):
        h, u = item
        cols = head(h, feat)
        return (
            nt(kv_ref[0, u, :, cols], queries[u][:, cols]),
            nt(kv_ref[1, u, :, cols], grads[u][:, cols]),
        )

    def second(item, scores, grad_weights):
        h, u = item
        side = slice(u * seg, (u + 1) * seg)
        top, inverse, delta = (fin_ref[i, h, :, side] for i in range(3))
        scores = jnp.where(allowed, scores * scale, MASKED)
        weights = jnp.exp(scores - top) * inverse
        grad_scores = (weights * (grad_weights - delta) * scale).astype(BF16)
        return grad_scores, weights.astype(BF16)

    def third(item, grad_scores, weights_low):
        h, u = item
        cols = head(h, feat)
        side = slice(u * seg, (u + 1) * seg)
        terms_ref[0, u, :, cols] = nn(grad_scores, queries[u][:, cols])
        terms_ref[1, u, :, cols] = nn(weights_low, grads[u][:, cols])

        def whole(kv, own, memory):
            return tn(own, kv_ref[kv, u, :, cols]) + tn(memory, memory_rows(kv, h, slots))

        att = whole(1, weights_low, w_ref[h, :, side]).astype(BF16)
        gq = whole(0, grad_scores, d_ref[h, :, side]).astype(BF16)
        if u == 0:
            att_ref[:, cols] = att
            gq_ref[:, cols] = gq
        else:
            givea_ref[:, cols] = att
            giveg_ref[:, cols] = gq

    staged([(h, u) for h in range(heads) for u in range(2)], first, second, third, 4)


def first_sum_kernel(t0_ref, b4_ref, low_ref):
    even = lax.axis_index("seq") % 2 == 0
    for kv in range(2):
        for u in range(2):
            low = jnp.where(even == (u == 0), t0_ref[kv], 0.0)
            low_ref[u, kv] = low + b4_ref[u, kv].astype(F32)


def sum_kernel(kt_ref, vt_ref, low_ref, b2_ref, mg_ref, mine_ref, other_ref):
    count = mine_ref.shape[0] * 2
    feat = mine_ref.shape[2]
    even = lax.axis_index("seq") % 2 == 0
    terms = jnp.zeros((kt_ref.shape[0], feat), F32)
    for kv, turned_ref in enumerate((kt_ref, vt_ref)):
        rows = []
        for u in range(2):
            low = (low_ref[u, kv] + b2_ref[u, kv].astype(F32)).astype(BF16)
            mg_ref[kv, u] = low
            rows.append(low.reshape(-1, feat))
        terms = terms + nn(turned_ref[...], jnp.concatenate(rows, 0))
    rows = terms.shape[0] // count
    bits = count.bit_length() - 1
    for p in range(0, count, 2):
        spot = int(format(p, "b").zfill(bits)[::-1], 2)
        first = terms[p * rows : (p + 1) * rows]
        second = terms[(p + 1) * rows : (p + 2) * rows]
        mine_ref[spot] = jnp.where(even, first, second)
        other_ref[spot] = jnp.where(even, second, first).astype(BF16)


def back_kernel(mg_ref, w_ref, terms_ref, gk_ref, gv_ref, givek_ref, givev_ref):
    seg = terms_ref.shape[2]
    heads, slot, feat = mg_ref.shape[2:]
    restore = tap_major(seg, inverse=True)
    parts = [(kv, u) for kv in range(2) for u in range(2)]
    backs = [nt(mg_ref[kv, u].reshape(heads * slot, feat), w_ref[...]) for kv, u in parts]
    totals = []
    for (kv, u), back in zip(parts, backs):
        columns = []
        for h in range(heads):
            rows = back[h * slot : (h + 1) * slot]
            columns.append(jnp.concatenate([rows[:, head(t, feat)] for t in range(TAPS)], 0))
        totals.append((terms_ref[kv, u] + jnp.concatenate(columns, 1)).astype(BF16))
    for (kv, u), total in zip(parts, totals):
        result = nn(restore, total).astype(BF16)
        ((gk_ref, gv_ref), (givek_ref, givev_ref))[u][kv][...] = result


def finish_kernel(a_in, b_in, got_a, got_b, a_ref, b_ref, sems):
    del a_in, b_in
    width = got_a.shape[1]
    start = pl.multiple_of((1 - lax.axis_index("seq") % 2) * width, width)
    copies = [
        pltpu.make_async_copy(got, dst.at[:, pl.ds(start, width)], sems.at[i])
        for i, (got, dst) in enumerate(((got_a, a_ref), (got_b, b_ref)))
    ]
    for copy in copies:
        copy.start()
    for copy in copies:
        copy.wait()


def call(kernel, out_shape, in_specs, out_specs, flops, moved, exps=0, scratch=(), aliases=None):
    return pl.pallas_call(
        kernel,
        out_shape=out_shape,
        grid=(1,),
        in_specs=in_specs,
        out_specs=out_specs,
        scratch_shapes=scratch,
        input_output_aliases=aliases or {},
        compiler_params=pltpu.CompilerParams(vmem_limit_bytes=VMEM_BYTES),
        cost_estimate=pl.CostEstimate(flops=flops, bytes_accessed=moved, transcendentals=exps),
    )


def local(queries, key_vectors, value_vectors, cotangent, compress_kernel, memory_reach):
    q, k, v, g = queries[0], key_vectors[0], value_vectors[0], cotangent[0]
    seg, width = q.shape
    feat = compress_kernel.shape[1]
    heads = width // feat
    half = heads // 2
    slot = seg // TAPS
    span = BLOCKS * slot
    count = lax.axis_size("seq")
    books = lax.axis_size("dp")
    position = lax.axis_index("seq")
    row_bytes = 2 * seg * width
    unit = 2 * heads * seg * seg * feat

    def side():
        return lax.axis_index("seq") % 2

    def shift(value, steps):
        return lax.ppermute(value, "seq", [(s, (s + steps) % count) for s in range(count)])

    def cross(value, steps):
        return lax.ppermute(value, "seq", [(s, ((s ^ 1) + steps) % count) for s in range(count)])

    def trade(value, flip=1):
        return lax.ppermute(value, "seq", [(s, s ^ flip) for s in range(count)])

    def in_hbm(value):
        return pltpu.with_memory_space_constraint(value, pltpu.HBM)

    def shape(dims, kind=BF16):
        return jax.ShapeDtypeStruct(dims, kind)

    def full(dims):
        return pl.BlockSpec(dims, lambda i: (0,) * len(dims))

    mine_cols = pl.BlockSpec((seg, half * feat), lambda i: (0, side()))
    kernel_spec = full(compress_kernel.shape)

    hbm = pl.BlockSpec(memory_space=pltpu.HBM)
    rows = 4 * seg
    half_dims = (2, half, slot, feat)
    packed_mine, packed_other, give = call(
        pack_kernel,
        (shape(half_dims), shape(half_dims), shape((rows, half * feat))),
        [hbm] * 5,
        (full(half_dims), full(half_dims), full((rows, half * feat))),
        3 * unit, 5 * row_bytes,
        scratch=[
            pltpu.VMEM((2, 2, seg, half * feat), BF16),
            pltpu.VMEM(compress_kernel.shape, BF16),
            pltpu.SemaphoreType.DMA((7,)),
        ],
    )(*[in_hbm(a) for a in (k, v, q, g, compress_kernel)])
    got = trade(give)

    r4 = shift(packed_mine, 4)
    r2 = shift(packed_mine, 2)
    r4s = cross(packed_other, 4)
    r2s = cross(packed_other, 2)
    got, late_reach = lax.optimization_barrier((got, memory_reach))
    scalar = pl.BlockSpec(memory_space=pltpu.SMEM)
    kvp, near, own_stats, kt, vt, bias = call(
        own_kernel,
        (
            shape((2, 2, seg, half * feat)),
            shape((2, half, slot, feat)),
            shape((3, half, 1, 2 * seg), F32),
            shape((TAPS * feat, heads * slot)),
            shape((TAPS * feat, heads * slot)),
            shape((span, 2 * seg), F32),
        ),
        [scalar] * 2 + [mine_cols] * 4 + [full((rows, half * feat)), kernel_spec],
        (
            full((2, 2, seg, half * feat)),
            full((2, half, slot, feat)),
            full((3, half, 1, 2 * seg)),
            full((TAPS * feat, heads * slot)),
            full((TAPS * feat, heads * slot)),
            full((span, 2 * seg)),
        ),
        unit, 8 * row_bytes, heads * seg * seg,
    )(late_reach, trade(late_reach), k, v, q, g, got, compress_kernel)

    slots = [near, r2, r2s, r4, r4s]
    got_q = pl.BlockSpec((seg, half * feat), lambda i: (2, 0))
    got_g = pl.BlockSpec((seg, half * feat), lambda i: (3, 0))
    one = (2, half, slot, feat)
    soft = (half, span, 2 * seg)
    stats = (3, half, 1, 2 * seg)
    pair = (2, 2, half, slot, feat)
    t0, t2, t4, w_mem, d_mem, final = call(
        memory_kernel,
        (shape(one, F32), *[shape(pair)] * 2, shape(soft), shape(soft), shape(stats, F32)),
        [full((span, 2 * seg)), mine_cols, got_q, mine_cols, got_g, full(stats)]
        + [full(one)] * BLOCKS,
        (full(one), *[full(pair)] * 2, full(soft), full(soft), full(stats)),
        4 * unit, 8 * row_bytes, heads * seg * seg,
    )(bias, q, got, g, got, own_stats, *slots)

    back4 = shift(t4, -4)
    back2 = shift(t2, -2)
    attended, grad_queries, give_a, give_g, own_terms = call(
        output_kernel,
        (
            shape((seg, width)),
            shape((seg, width)),
            shape((seg, half * feat)),
            shape((seg, half * feat)),
            shape((2, 2, seg, half * feat), F32),
        ),
        [mine_cols, got_q, mine_cols, got_g, full((2, 2, seg, half * feat))]
        + [full(one)] * BLOCKS
        + [full(soft), full(soft), full(stats)],
        (
            mine_cols, mine_cols,
            full((seg, half * feat)),
            full((seg, half * feat)),
            full((2, 2, seg, half * feat)),
        ),
        8 * unit, 12 * row_bytes, heads * seg * seg,
    )(q, got, g, got, kvp, *slots, w_mem, d_mem, final)

    def finish(a, b, give_a, give_b):
        anywhere = pl.BlockSpec(memory_space=pl.ANY)
        return call(
            finish_kernel,
            (shape((seg, width)), shape((seg, width))),
            [anywhere] * 4,
            (anywhere, anywhere),
            0, 2 * row_bytes,
            scratch=[pltpu.SemaphoreType.DMA((2,))],
            aliases={0: 0, 1: 1},
        )(a, b, trade(give_a), trade(give_b))

    attended, grad_queries = finish(attended, grad_queries, give_a, give_g)
    kernel_rows = compress_kernel.shape[0]
    split = (count // 2, kernel_rows // count, feat)
    turned = full((TAPS * feat, heads * slot))
    low = call(
        first_sum_kernel, shape(pair, F32), [full(one), full(pair)], full(pair), 0, 2 * row_bytes * 10
    )(t0, back4)
    low, own_terms = lax.optimization_barrier((low, own_terms))
    memory_grads, mine, other = call(
        sum_kernel,
        (shape(pair), shape(split, F32), shape(split)),
        [turned] * 2 + [full(pair)] * 2,
        (full(pair), full(split), full(split)),
        unit, 4 * row_bytes,
    )(kt, vt, low, back2)

    grad_keys, grad_values, give_k, give_v = call(
        back_kernel,
        (shape((seg, width)), shape((seg, width)), *[shape((seg, half * feat))] * 2),
        [full(pair), kernel_spec, full((2, 2, seg, half * feat))],
        (mine_cols, mine_cols, *[full((seg, half * feat))] * 2),
        4 * unit, 7 * row_bytes,
    )(memory_grads, compress_kernel, own_terms)

    grad_keys, grad_values = finish(grad_keys, grad_values, give_k, give_v)
    part = mine + trade(other).astype(F32)
    part, (attended, grad_queries, grad_keys, grad_values) = reduce_rest(
        part, position, count, books, (attended, grad_queries, grad_keys, grad_values)
    )
    return (attended[None], grad_queries[None], grad_keys[None], grad_values[None], part)


def reduce_rest(part, position, count, books, beside):
    bits = []
    step = 2
    while step < count:
        bits.append(("seq", step))
        step *= 2
    step = 1
    while step < books:
        bits.append(("dp", step))
        step *= 2
    for i in range(0, len(bits), 2):
        phase = bits[i : i + 2]
        split = [step for axis, step in phase if axis == "seq"]
        part = part.reshape(2 ** len(split), -1, *part.shape[1:])
        mine = jnp.int32(0)
        for step in split:
            mine = mine * 2 + (position // step) % 2
        arrived = []
        for mask in range(1, 2 ** len(phase)):
            flip, seq_xor, dp_xor = 0, 0, 0
            for j, (axis, step) in enumerate(phase):
                chosen = (mask >> (len(phase) - 1 - j)) & 1
                if axis == "seq":
                    flip = flip * 2 + chosen
                    seq_xor |= chosen * step
                else:
                    dp_xor |= chosen * step
            sent = lax.dynamic_index_in_dim(part, mine ^ flip, 0, False)
            pairs = [
                (s * books + d, (s ^ seq_xor) * books + (d ^ dp_xor))
                for s in range(count)
                for d in range(books)
            ]
            arrived.append(lax.ppermute(sent.astype(BF16), ("seq", "dp"), pairs))
        part = lax.dynamic_index_in_dim(part, mine, 0, False)
        if i + 2 >= len(bits):
            arrived[0], *beside = lax.optimization_barrier((arrived[0], *beside))
        for piece in arrived:
            part = part + piece.astype(F32)
    return part.reshape(-1, part.shape[-1]), beside


def solution(mesh):
    rows = P("dp", "seq", None)
    return jax.shard_map(
        local,
        mesh=mesh,
        in_specs=(rows, rows, rows, rows, P(), P("dp", "seq")),
        out_specs=(rows, rows, rows, rows, P("seq", None)),
        check_vma=False,
    )
```

```python
import jax
import jax.numpy as jnp
from jax import lax
from jax.experimental import pallas as pl
from jax.experimental.pallas import tpu as pltpu
from jax.sharding import PartitionSpec as P

F32 = jnp.float32
BF16 = jnp.bfloat16
TAPS = 4
PLANE = 4
MASKED = -1e30
VMEM_BYTES = 24 * 2**20
BLOCKS = 5


def nt(a, b):
    return lax.dot_general(a, b, (((1,), (1,)), ((), ())), preferred_element_type=F32)


def nn(a, b):
    return lax.dot_general(a, b, (((1,), (0,)), ((), ())), preferred_element_type=F32)


def tn(a, b):
    return lax.dot_general(a, b, (((0,), (0,)), ((), ())), preferred_element_type=F32)


def tap_major(seg, inverse=False):
    slot = seg // TAPS
    spot = lax.broadcasted_iota(jnp.int32, (seg, seg), 1 if inverse else 0)
    token = lax.broadcasted_iota(jnp.int32, (seg, seg), 0 if inverse else 1)
    return (token == TAPS * (spot % slot) + spot // slot).astype(BF16)


def causal(seg):
    slot = seg // TAPS
    spot = lax.broadcasted_iota(jnp.int32, (seg, seg), 0)
    query = lax.broadcasted_iota(jnp.int32, (seg, seg), 1)
    return TAPS * (spot % slot) + spot // slot <= query


def head(h, feat):
    return slice(h * feat, (h + 1) * feat)


def staged(items, first, second, third, size=2):
    groups = [items[i : i + size] for i in range(0, len(items), size)]
    begun, turned = {}, {}
    for i in range(len(groups) + 2):
        if i < len(groups):
            for item in groups[i]:
                begun[item] = first(item)
        if i >= 2:
            for item in groups[i - 2]:
                third(item, *turned.pop(item))
        if 1 <= i <= len(groups):
            for item in groups[i - 1]:
                turned[item] = second(item, *begun.pop(item))


def tap_rows(rows, heads, feat):
    slot = rows.shape[0] // TAPS
    return jnp.concatenate(
        [
            jnp.concatenate(
                [rows[t * slot : (t + 1) * slot, head(h, feat)] for t in range(TAPS)], 1
            )
            for h in range(heads)
        ],
        0,
    )


def pack_kernel(
    k_hbm, v_hbm, q_hbm, g_hbm, w_hbm,
    mine_ref, other_ref, give_ref, rows_ref, w_ref, sems,
):
    seg, width = k_hbm.shape
    feat = w_hbm.shape[1]
    half = width // 2
    heads = half // feat
    slot = seg // TAPS
    order = tap_major(seg)
    core = lax.axis_index("seq") % 2
    begin = [pl.multiple_of(core * half, half), pl.multiple_of((1 - core) * half, half)]
    steps = [(part, kv) for part in range(2) for kv in range(2)]
    pairs = [
        ((k_hbm, v_hbm)[kv].at[:, pl.ds(begin[part], half)], rows_ref.at[part, kv])
        for part, kv in steps
    ]
    pairs.insert(2, (w_hbm, w_ref))
    pairs += [
        (src.at[:, pl.ds(begin[1], half)], give_ref.at[pl.ds((2 + i) * seg, seg)])
        for i, src in enumerate((q_hbm, g_hbm))
    ]
    copies = [pltpu.make_async_copy(*pair, sems.at[n]) for n, pair in enumerate(pairs)]
    for copy in copies:
        copy.start()
    sorted_rows = []
    for n, (part, kv) in enumerate(steps):
        copies[n if n < 2 else n + 1].wait()
    copies[2].wait()
    every = jnp.concatenate([rows_ref[part, kv] for part, kv in steps], 1)
    every = nn(order, every).astype(BF16)
    half_width = heads * feat
    sorted_rows = [
        every[:, n * half_width : (n + 1) * half_width] for n in range(len(steps))
    ]
    rows = jnp.concatenate([tap_rows(rows, heads, feat) for rows in sorted_rows], 0)
    packed = nn(rows, w_ref[...]).astype(BF16).reshape(len(steps), heads, slot, feat)
    for n, (part, kv) in enumerate(steps):
        (mine_ref, other_ref)[part][kv] = packed[n]
        if part == 1:
            give_ref[kv * seg : (kv + 1) * seg] = rows_ref[part, kv]
    for copy in copies[5:]:
        copy.wait()


def choose_kernel(own_ref, got_ref, out_ref):
    first_chip = lax.axis_index("seq") % PLANE < 2
    out_ref[...] = jnp.where(first_chip, own_ref[...], got_ref[...])


def join_kernel(a_ref, b_ref, out_ref):
    slot = a_ref.shape[2]
    out_ref[:, :, :slot] = a_ref[...]
    out_ref[:, :, slot:] = b_ref[...]


def own_kernel(
    reach_ref, reach_s_ref, k_ref, v_ref, q_ref, g_ref, got_ref, w_ref,
    kv_ref, near_ref, stat_ref, kt_ref, vt_ref, bias_ref,
):
    seg, width = q_ref.shape
    feat = w_ref.shape[1]
    heads = width // feat
    slot = seg // TAPS
    scale = feat**-0.5
    mine = lax.axis_index("seq")
    partner = mine + 1 - 2 * (mine % 2)
    even = mine % 2 == 0
    sources = (mine - mine % 2, mine - 2, mine - 4, partner - 2, partner - 4)
    for b, source in enumerate(sources):
        for u, (reader, limit) in enumerate(((mine, reach_ref), (partner, reach_s_ref))):
            steps = reader - source
            shown = (steps >= 1) & (steps <= jnp.minimum(limit[0, 0], 4)) & (source >= 0)
            bias_ref[b * slot : (b + 1) * slot, u * seg : (u + 1) * seg] = jnp.full(
                (slot, seg), jnp.where(shown, 0.0, MASKED), F32
            )
    allowed = causal(seg)
    order = tap_major(seg)
    for kv, src in enumerate((k_ref, v_ref)):
        kv_ref[kv, 0] = nn(order, src[...]).astype(BF16)
        kv_ref[kv, 1] = nn(order, got_ref[kv * seg : (kv + 1) * seg]).astype(BF16)
    queries = (q_ref, got_ref.at[2 * seg : 3 * seg])
    grads = (g_ref, got_ref.at[3 * seg : 4 * seg])

    def first(item):
        h, u = item
        cols = head(h, feat)
        return (
            nt(kv_ref[0, u, :, cols], queries[u][:, cols]),
            nt(kv_ref[1, u, :, cols], grads[u][:, cols]),
        )

    def second(item, scores, grad_weights):
        h, u = item
        scores = jnp.where(allowed, scores * scale, MASKED)
        top = jnp.max(scores, axis=0, keepdims=True)
        raised = jnp.exp(scores - top)
        side = slice(u * seg, (u + 1) * seg)
        stat_ref[0, h, :, side] = top
        stat_ref[1, h, :, side] = jnp.sum(raised, axis=0, keepdims=True)
        stat_ref[2, h, :, side] = jnp.sum(raised * grad_weights, axis=0, keepdims=True)
        return ()

    staged([(h, u) for h in range(heads) for u in range(2)], first, second, lambda item: None, 4)
    rows = [
        tap_rows(jnp.where(even, kv_ref[kv, 0], kv_ref[kv, 1]), heads, feat) for kv in range(2)
    ]
    near = nn(jnp.concatenate(rows, 0), w_ref[...]).astype(BF16)
    near_ref[...] = near.reshape(near_ref.shape)
    for kv, dst in enumerate((kt_ref, vt_ref)):
        for u in range(2):
            lanes = slice(u * heads * slot, (u + 1) * heads * slot)
            for t in range(TAPS):
                part = kv_ref[kv, u, t * slot : (t + 1) * slot, :]
                stacked = jnp.concatenate([part[:, head(h, feat)] for h in range(heads)], 0)
                dst[t * feat : (t + 1) * feat, lanes] = stacked.T


def memory_rows(kv, h, slots):
    return jnp.concatenate([ref[kv, h] for ref in slots], 0)


def memory_kernel(
    bias_ref, q_ref, qs_ref, g_ref, gs_ref, stat_ref,
    near_ref, joined_ref, r2s_ref, r4s_ref,
    t0_ref, t2k_ref, t2v_ref, t4k_ref, t4v_ref, w_ref, d_ref, fin_ref,
):
    seg, width = q_ref.shape
    heads = stat_ref.shape[1]
    feat = width // heads
    slot = seg // TAPS
    scale = feat**-0.5
    slots = (near_ref, joined_ref, r2s_ref, r4s_ref)

    def both(a_ref, b_ref, h):
        return jnp.concatenate([a_ref[:, head(h, feat)], b_ref[:, head(h, feat)]], 0)

    def first(h):
        return (
            nt(memory_rows(0, h, slots), both(q_ref, qs_ref, h)),
            nt(memory_rows(1, h, slots), both(g_ref, gs_ref, h)),
        )

    def second(h, scores, grad_weights):
        bias = bias_ref[...]
        scores = jnp.where(bias < 0.0, MASKED, scores * scale)
        own_top = stat_ref[0, h]
        top = jnp.maximum(own_top, jnp.max(scores, axis=0, keepdims=True))
        raised = jnp.exp(scores - top)
        fade = jnp.exp(own_top - top)
        total = stat_ref[1, h] * fade + jnp.sum(raised, axis=0, keepdims=True)
        delta = stat_ref[2, h] * fade + jnp.sum(raised * grad_weights, axis=0, keepdims=True)
        inverse = 1.0 / total
        delta = delta * inverse
        weights = raised * inverse
        weights_low = weights.astype(BF16)
        grad_scores = (weights * (grad_weights - delta) * scale).astype(BF16)
        w_ref[h] = weights_low
        d_ref[h] = grad_scores
        fin_ref[0, h] = top
        fin_ref[1, h] = inverse
        fin_ref[2, h] = delta
        return grad_scores, weights_low

    def third(h, grad_scores, weights_low):
        pair = (nn(grad_scores, both(q_ref, qs_ref, h)), nn(weights_low, both(g_ref, gs_ref, h)))
        for kv, terms in enumerate(pair):
            t0_ref[kv, h] = terms[:slot]
            terms = terms.astype(BF16)
            for i in range(4):
                ((t2k_ref, t2v_ref), (t4k_ref, t4v_ref))[i % 2][kv][i // 2, h] = terms[(i + 1) * slot : (i + 2) * slot]

    staged(list(range(heads)), first, second, third)


def output_kernel(*refs):
    q_ref, qs_ref, g_ref, gs_ref, kv_ref = refs[:5]
    slots = refs[5:9]
    w_ref, d_ref, fin_ref, *results = refs[9:]
    att_ref, gq_ref, givea_ref, giveg_ref, terms_ref = results
    seg, width = q_ref.shape
    feat = slots[0].shape[3]
    heads = width // feat
    scale = feat**-0.5
    allowed = causal(seg)
    queries, grads = (q_ref, qs_ref), (g_ref, gs_ref)

    def first(item):
        h, u = item
        cols = head(h, feat)
        return (
            nt(kv_ref[0, u, :, cols], queries[u][:, cols]),
            nt(kv_ref[1, u, :, cols], grads[u][:, cols]),
        )

    def second(item, scores, grad_weights):
        h, u = item
        side = slice(u * seg, (u + 1) * seg)
        top, inverse, delta = (fin_ref[i, h, :, side] for i in range(3))
        scores = jnp.where(allowed, scores * scale, MASKED)
        weights = jnp.exp(scores - top) * inverse
        grad_scores = (weights * (grad_weights - delta) * scale).astype(BF16)
        return grad_scores, weights.astype(BF16)

    def third(item, grad_scores, weights_low):
        h, u = item
        cols = head(h, feat)
        side = slice(u * seg, (u + 1) * seg)
        terms_ref[0, u, :, cols] = nn(grad_scores, queries[u][:, cols])
        terms_ref[1, u, :, cols] = nn(weights_low, grads[u][:, cols])

        def whole(kv, own, memory):
            return tn(own, kv_ref[kv, u, :, cols]) + tn(memory, memory_rows(kv, h, slots))

        att = whole(1, weights_low, w_ref[h, :, side]).astype(BF16)
        gq = whole(0, grad_scores, d_ref[h, :, side]).astype(BF16)
        if u == 0:
            att_ref[:, cols] = att
            gq_ref[:, cols] = gq
        else:
            givea_ref[:, cols] = att
            giveg_ref[:, cols] = gq

    staged([(h, u) for h in range(heads) for u in range(2)], first, second, third, 4)


def relay_kernel(own_ref, passed_ref, out_ref):
    first_chip = lax.axis_index("seq") % PLANE < 2
    passed = jnp.where(first_chip, 0.0, passed_ref[...].astype(F32))
    out_ref[...] = (own_ref[...].astype(F32) + passed).astype(BF16)


def first_sum_kernel(t0_ref, k4_ref, k2_ref, v2_ref, low_ref):
    position = lax.axis_index("seq")
    even = position % 2 == 0
    first_chip = position % PLANE < 2
    for u in range(2):
        near = [jnp.where(even == (u == 0), t0_ref[kv], 0.0) for kv in range(2)]
        low_ref[0, u] = near[0] + k4_ref[u].astype(F32) + k2_ref[u].astype(F32)
        low_ref[1, u] = near[1] + jnp.where(first_chip, v2_ref[u].astype(F32), 0.0)


def sum_kernel(kt_ref, vt_ref, low_ref, v4_ref, mg_ref, mine_ref, other_ref):
    count = mine_ref.shape[0] * 2
    feat = mine_ref.shape[2]
    even = lax.axis_index("seq") % 2 == 0
    terms = jnp.zeros((kt_ref.shape[0], feat), F32)
    for kv, turned_ref in enumerate((kt_ref, vt_ref)):
        rows = []
        for u in range(2):
            low = low_ref[kv, u]
            if kv == 1:
                low = low + v4_ref[u].astype(F32)
            low = low.astype(BF16)
            mg_ref[kv, u] = low
            rows.append(low.reshape(-1, feat))
        terms = terms + nn(turned_ref[...], jnp.concatenate(rows, 0))
    rows = terms.shape[0] // count
    bits = count.bit_length() - 1
    for p in range(0, count, 2):
        spot = int(format(p, "b").zfill(bits)[::-1], 2)
        first = terms[p * rows : (p + 1) * rows]
        second = terms[(p + 1) * rows : (p + 2) * rows]
        mine_ref[spot] = jnp.where(even, first, second)
        other_ref[spot] = jnp.where(even, second, first).astype(BF16)


def back_kernel(mg_ref, w_ref, terms_ref, gk_ref, gv_ref, givek_ref, givev_ref):
    seg = terms_ref.shape[2]
    heads, slot, feat = mg_ref.shape[2:]
    restore = tap_major(seg, inverse=True)
    parts = [(kv, u) for kv in range(2) for u in range(2)]
    backs = [nt(mg_ref[kv, u].reshape(heads * slot, feat), w_ref[...]) for kv, u in parts]
    totals = []
    for (kv, u), back in zip(parts, backs):
        columns = []
        for h in range(heads):
            rows = back[h * slot : (h + 1) * slot]
            columns.append(jnp.concatenate([rows[:, head(t, feat)] for t in range(TAPS)], 0))
        totals.append((terms_ref[kv, u] + jnp.concatenate(columns, 1)).astype(BF16))
    for (kv, u), total in zip(parts, totals):
        result = nn(restore, total).astype(BF16)
        ((gk_ref, gv_ref), (givek_ref, givev_ref))[u][kv][...] = result


def finish_kernel(a_in, b_in, got_a, got_b, a_ref, b_ref, sems):
    del a_in, b_in
    width = got_a.shape[1]
    start = pl.multiple_of((1 - lax.axis_index("seq") % 2) * width, width)
    copies = [
        pltpu.make_async_copy(got, dst.at[:, pl.ds(start, width)], sems.at[i])
        for i, (got, dst) in enumerate(((got_a, a_ref), (got_b, b_ref)))
    ]
    for copy in copies:
        copy.start()
    for copy in copies:
        copy.wait()


def call(kernel, out_shape, in_specs, out_specs, flops, moved, exps=0, scratch=(), aliases=None):
    return pl.pallas_call(
        kernel,
        out_shape=out_shape,
        grid=(1,),
        in_specs=in_specs,
        out_specs=out_specs,
        scratch_shapes=scratch,
        input_output_aliases=aliases or {},
        compiler_params=pltpu.CompilerParams(vmem_limit_bytes=VMEM_BYTES),
        cost_estimate=pl.CostEstimate(flops=flops, bytes_accessed=moved, transcendentals=exps),
    )


def local(queries, key_vectors, value_vectors, cotangent, compress_kernel, memory_reach):
    q, k, v, g = queries[0], key_vectors[0], value_vectors[0], cotangent[0]
    seg, width = q.shape
    feat = compress_kernel.shape[1]
    heads = width // feat
    half = heads // 2
    slot = seg // TAPS
    span = BLOCKS * slot
    count = lax.axis_size("seq")
    books = lax.axis_size("dp")
    position = lax.axis_index("seq")
    row_bytes = 2 * seg * width
    unit = 2 * heads * seg * seg * feat

    def side():
        return lax.axis_index("seq") % 2

    def shift(value, steps):
        return lax.ppermute(value, "seq", [(s, (s + steps) % count) for s in range(count)])

    def shift_part(value, steps):
        return lax.ppermute(
            value, "seq", [(s, s + steps) for s in range(count) if 0 <= s + steps < count]
        )

    def cross_part(value, steps):
        pairs = [(s, (s ^ 1) + steps) for s in range(count)]
        return lax.ppermute(value, "seq", [(s, t) for s, t in pairs if t < count])

    def cross(value, steps):
        return lax.ppermute(value, "seq", [(s, ((s ^ 1) + steps) % count) for s in range(count)])

    def trade(value, flip=1):
        return lax.ppermute(value, "seq", [(s, s ^ flip) for s in range(count)])

    def in_hbm(value):
        return pltpu.with_memory_space_constraint(value, pltpu.HBM)

    def shape(dims, kind=BF16):
        return jax.ShapeDtypeStruct(dims, kind)

    def full(dims):
        return pl.BlockSpec(dims, lambda i: (0,) * len(dims))

    mine_cols = pl.BlockSpec((seg, half * feat), lambda i: (0, side()))
    kernel_spec = full(compress_kernel.shape)

    hbm = pl.BlockSpec(memory_space=pltpu.HBM)
    rows = 4 * seg
    half_dims = (2, half, slot, feat)
    packed_mine, packed_other, give = call(
        pack_kernel,
        (shape(half_dims), shape(half_dims), shape((rows, half * feat))),
        [hbm] * 5,
        (full(half_dims), full(half_dims), full((rows, half * feat))),
        3 * unit, 5 * row_bytes,
        scratch=[
            pltpu.VMEM((2, 2, seg, half * feat), BF16),
            pltpu.VMEM(compress_kernel.shape, BF16),
            pltpu.SemaphoreType.DMA((7,)),
        ],
    )(*[in_hbm(a) for a in (k, v, q, g, compress_kernel)])
    got = trade(give)

    r4s = cross(packed_other, 4)
    r2 = shift(packed_mine, 2)
    r4 = shift(packed_mine, 4)
    plane = range(0, count, PLANE)
    r2s = lax.ppermute(
        call(
            choose_kernel, shape(half_dims), [full(half_dims)] * 2, full(half_dims), 0, row_bytes
        )(packed_other, r4s),
        "seq",
        [(p + s, p + t) for p in plane for s, t in ((0, 3), (1, 2), (2, 0), (3, 1))],
    )
    got, late_reach = lax.optimization_barrier((got, memory_reach))
    scalar = pl.BlockSpec(memory_space=pltpu.SMEM)
    kvp, near, own_stats, kt, vt, bias = call(
        own_kernel,
        (
            shape((2, 2, seg, half * feat)),
            shape((2, half, slot, feat)),
            shape((3, half, 1, 2 * seg), F32),
            shape((TAPS * feat, heads * slot)),
            shape((TAPS * feat, heads * slot)),
            shape((span, 2 * seg), F32),
        ),
        [scalar] * 2 + [mine_cols] * 4 + [full((rows, half * feat)), kernel_spec],
        (
            full((2, 2, seg, half * feat)),
            full((2, half, slot, feat)),
            full((3, half, 1, 2 * seg)),
            full((TAPS * feat, heads * slot)),
            full((TAPS * feat, heads * slot)),
            full((span, 2 * seg)),
        ),
        unit, 8 * row_bytes, heads * seg * seg,
    )(late_reach, trade(late_reach), k, v, q, g, got, compress_kernel)

    r2, own_stats = lax.optimization_barrier((r2, own_stats))
    joined_dims = (2, half, 2 * slot, feat)
    joined = call(
        join_kernel, shape(joined_dims), [full(half_dims)] * 2, full(joined_dims), 0, 10 * row_bytes
    )(r2, r4)
    slots = [near, joined, r2s, r4s]
    got_q = pl.BlockSpec((seg, half * feat), lambda i: (2, 0))
    got_g = pl.BlockSpec((seg, half * feat), lambda i: (3, 0))
    one = (2, half, slot, feat)
    soft = (half, span, 2 * seg)
    stats = (3, half, 1, 2 * seg)
    pair = (2, 2, half, slot, feat)
    t0, t2k, t2v, t4k, t4v, w_mem, d_mem, final = call(
        memory_kernel,
        (shape(one, F32), *[shape(one)] * 4, shape(soft), shape(soft), shape(stats, F32)),
        [full((span, 2 * seg)), mine_cols, got_q, mine_cols, got_g, full(stats)]
        + [full(one), full(joined_dims), full(one), full(one)],
        (full(one), *[full(one)] * 4, full(soft), full(soft), full(stats)),
        4 * unit, 8 * row_bytes, heads * seg * seg,
    )(bias, q, got, g, got, own_stats, *slots)

    v2 = trade(t2v, 2)
    k4 = shift_part(t4k, -4)
    k2 = shift(t2k, -2)
    v4 = shift_part(
        call(relay_kernel, shape(one), [full(one)] * 2, full(one), 0, row_bytes)(t4v, v2), -4
    )
    attended, grad_queries, give_a, give_g, own_terms = call(
        output_kernel,
        (
            shape((seg, width)),
            shape((seg, width)),
            shape((seg, half * feat)),
            shape((seg, half * feat)),
            shape((2, 2, seg, half * feat), F32),
        ),
        [mine_cols, got_q, mine_cols, got_g, full((2, 2, seg, half * feat))]
        + [full(one), full(joined_dims), full(one), full(one)]
        + [full(soft), full(soft), full(stats)],
        (
            mine_cols, mine_cols,
            full((seg, half * feat)),
            full((seg, half * feat)),
            full((2, 2, seg, half * feat)),
        ),
        8 * unit, 12 * row_bytes, heads * seg * seg,
    )(q, got, g, got, kvp, *slots, w_mem, d_mem, final)

    def finish(a, b, give_a, give_b):
        anywhere = pl.BlockSpec(memory_space=pl.ANY)
        return call(
            finish_kernel,
            (shape((seg, width)), shape((seg, width))),
            [anywhere] * 4,
            (anywhere, anywhere),
            0, 2 * row_bytes,
            scratch=[pltpu.SemaphoreType.DMA((2,))],
            aliases={0: 0, 1: 1},
        )(a, b, trade(give_a), trade(give_b))

    attended, grad_queries = finish(attended, grad_queries, give_a, give_g)
    kernel_rows = compress_kernel.shape[0]
    split = (count // 2, kernel_rows // count, feat)
    turned = full((TAPS * feat, heads * slot))
    low = call(
        first_sum_kernel,
        shape(pair, F32),
        [full(one)] * 4,
        full(pair),
        0, 4 * row_bytes,
    )(t0, k4, k2, v2)
    low, own_terms = lax.optimization_barrier((low, own_terms))
    memory_grads, mine, other = call(
        sum_kernel,
        (shape(pair), shape(split, F32), shape(split)),
        [turned] * 2 + [full(pair), full(one)],
        (full(pair), full(split), full(split)),
        unit, 4 * row_bytes,
    )(kt, vt, low, v4)

    grad_keys, grad_values, give_k, give_v = call(
        back_kernel,
        (shape((seg, width)), shape((seg, width)), *[shape((seg, half * feat))] * 2),
        [full(pair), kernel_spec, full((2, 2, seg, half * feat))],
        (mine_cols, mine_cols, *[full((seg, half * feat))] * 2),
        4 * unit, 7 * row_bytes,
    )(memory_grads, compress_kernel, own_terms)

    grad_keys, grad_values = finish(grad_keys, grad_values, give_k, give_v)
    part = mine + trade(other).astype(F32)
    part, (attended, grad_queries, grad_keys, grad_values) = reduce_rest(
        part, position, count, books, (attended, grad_queries, grad_keys, grad_values)
    )
    return (attended[None], grad_queries[None], grad_keys[None], grad_values[None], part)


def reduce_rest(part, position, count, books, beside):
    bits = []
    step = 2
    while step < count:
        bits.append(("seq", step))
        step *= 2
    step = 1
    while step < books:
        bits.append(("dp", step))
        step *= 2
    for i in range(0, len(bits), 2):
        phase = bits[i : i + 2]
        split = [step for axis, step in phase if axis == "seq"]
        part = part.reshape(2 ** len(split), -1, *part.shape[1:])
        mine = jnp.int32(0)
        for step in split:
            mine = mine * 2 + (position // step) % 2
        arrived = []
        for mask in range(1, 2 ** len(phase)):
            flip, seq_xor, dp_xor = 0, 0, 0
            for j, (axis, step) in enumerate(phase):
                chosen = (mask >> (len(phase) - 1 - j)) & 1
                if axis == "seq":
                    flip = flip * 2 + chosen
                    seq_xor |= chosen * step
                else:
                    dp_xor |= chosen * step
            sent = lax.dynamic_index_in_dim(part, mine ^ flip, 0, False)
            pairs = [
                (s * books + d, (s ^ seq_xor) * books + (d ^ dp_xor))
                for s in range(count)
                for d in range(books)
            ]
            arrived.append(lax.ppermute(sent.astype(BF16), ("seq", "dp"), pairs))
        part = lax.dynamic_index_in_dim(part, mine, 0, False)
        if i + 2 >= len(bits):
            arrived[0], *beside = lax.optimization_barrier((arrived[0], *beside))
        for piece in arrived:
            part = part + piece.astype(F32)
    return part.reshape(-1, part.shape[-1]), beside


def solution(mesh):
    rows = P("dp", "seq", None)
    return jax.shard_map(
        local,
        mesh=mesh,
        in_specs=(rows, rows, rows, rows, P(), P("dp", "seq")),
        out_specs=(rows, rows, rows, rows, P("seq", None)),
        check_vma=False,
    )
```

```python
import jax
import jax.numpy as jnp
from jax import lax
from jax.experimental import pallas as pl
from jax.experimental.pallas import tpu as pltpu
from jax.sharding import PartitionSpec as P

F32 = jnp.float32
BF16 = jnp.bfloat16
TAPS = 4
PLANE = 4
MASKED = -1e30
VMEM_BYTES = 24 * 2**20
BLOCKS = 5


def nt(a, b):
    return lax.dot_general(a, b, (((1,), (1,)), ((), ())), preferred_element_type=F32)


def nn(a, b):
    return lax.dot_general(a, b, (((1,), (0,)), ((), ())), preferred_element_type=F32)


def tn(a, b):
    return lax.dot_general(a, b, (((0,), (0,)), ((), ())), preferred_element_type=F32)


def tap_major(seg, inverse=False):
    slot = seg // TAPS
    spot = lax.broadcasted_iota(jnp.int32, (seg, seg), 1 if inverse else 0)
    token = lax.broadcasted_iota(jnp.int32, (seg, seg), 0 if inverse else 1)
    return (token == TAPS * (spot % slot) + spot // slot).astype(BF16)


def causal(seg):
    slot = seg // TAPS
    spot = lax.broadcasted_iota(jnp.int32, (seg, seg), 0)
    query = lax.broadcasted_iota(jnp.int32, (seg, seg), 1)
    return TAPS * (spot % slot) + spot // slot <= query


def head(h, feat):
    return slice(h * feat, (h + 1) * feat)


def staged(items, first, second, third, size=2):
    groups = [items[i : i + size] for i in range(0, len(items), size)]
    begun, turned = {}, {}
    for i in range(len(groups) + 2):
        if i < len(groups):
            for item in groups[i]:
                begun[item] = first(item)
        if i >= 2:
            for item in groups[i - 2]:
                third(item, *turned.pop(item))
        if 1 <= i <= len(groups):
            for item in groups[i - 1]:
                turned[item] = second(item, *begun.pop(item))


def tap_rows(rows, heads, feat):
    slot = rows.shape[0] // TAPS
    return jnp.concatenate(
        [
            jnp.concatenate(
                [rows[t * slot : (t + 1) * slot, head(h, feat)] for t in range(TAPS)], 1
            )
            for h in range(heads)
        ],
        0,
    )


def pack_kernel(
    k_hbm, v_hbm, q_hbm, g_hbm, w_hbm,
    mine_ref, other_ref, give_ref, rows_ref, w_ref, sems,
):
    seg, width = k_hbm.shape
    feat = w_hbm.shape[1]
    half = width // 2
    heads = half // feat
    slot = seg // TAPS
    order = tap_major(seg)
    core = lax.axis_index("seq") % 2
    begin = [pl.multiple_of(core * half, half), pl.multiple_of((1 - core) * half, half)]
    steps = [(part, kv) for part in range(2) for kv in range(2)]
    pairs = [
        ((k_hbm, v_hbm)[kv].at[:, pl.ds(begin[part], half)], rows_ref.at[part, kv])
        for part, kv in steps
    ]
    pairs.insert(2, (w_hbm, w_ref))
    pairs += [
        (src.at[:, pl.ds(begin[1], half)], give_ref.at[pl.ds((2 + i) * seg, seg)])
        for i, src in enumerate((q_hbm, g_hbm))
    ]
    copies = [pltpu.make_async_copy(*pair, sems.at[n]) for n, pair in enumerate(pairs)]
    for copy in copies:
        copy.start()
    sorted_rows = []
    for n, (part, kv) in enumerate(steps):
        copies[n if n < 2 else n + 1].wait()
    copies[2].wait()
    every = jnp.concatenate([rows_ref[part, kv] for part, kv in steps], 1)
    every = nn(order, every).astype(BF16)
    half_width = heads * feat
    sorted_rows = [
        every[:, n * half_width : (n + 1) * half_width] for n in range(len(steps))
    ]
    rows = jnp.concatenate([tap_rows(rows, heads, feat) for rows in sorted_rows], 0)
    packed = nn(rows, w_ref[...]).astype(BF16).reshape(len(steps), heads, slot, feat)
    for n, (part, kv) in enumerate(steps):
        (mine_ref, other_ref)[part][kv] = packed[n]
        if part == 1:
            give_ref[kv * seg : (kv + 1) * seg] = rows_ref[part, kv]
    for copy in copies[5:]:
        copy.wait()


def choose_kernel(own_ref, got_ref, out_ref):
    first_chip = lax.axis_index("seq") % PLANE < 2
    out_ref[...] = jnp.where(first_chip, own_ref[...], got_ref[...])


def join_kernel(a_ref, b_ref, out_ref):
    slot = a_ref.shape[2]
    out_ref[:, :, :slot] = a_ref[...]
    out_ref[:, :, slot:] = b_ref[...]


def own_kernel(
    reach_ref, reach_s_ref, k_ref, v_ref, q_ref, g_ref, got_ref, w_ref,
    kv_ref, near_ref, stat_ref, kt_ref, vt_ref, bias_ref,
):
    seg, width = q_ref.shape
    feat = w_ref.shape[1]
    heads = width // feat
    slot = seg // TAPS
    scale = feat**-0.5
    mine = lax.axis_index("seq")
    partner = mine + 1 - 2 * (mine % 2)
    even = mine % 2 == 0
    sources = (mine - mine % 2, mine - 2, mine - 4, partner - 2, partner - 4)
    for b, source in enumerate(sources):
        for u, (reader, limit) in enumerate(((mine, reach_ref), (partner, reach_s_ref))):
            steps = reader - source
            shown = (steps >= 1) & (steps <= jnp.minimum(limit[0, 0], 4)) & (source >= 0)
            bias_ref[b * slot : (b + 1) * slot, u * seg : (u + 1) * seg] = jnp.full(
                (slot, seg), jnp.where(shown, 0.0, MASKED), F32
            )
    allowed = causal(seg)
    order = tap_major(seg)
    for kv, src in enumerate((k_ref, v_ref)):
        kv_ref[kv, 0] = nn(order, src[...]).astype(BF16)
        kv_ref[kv, 1] = nn(order, got_ref[kv * seg : (kv + 1) * seg]).astype(BF16)
    queries = (q_ref, got_ref.at[2 * seg : 3 * seg])
    grads = (g_ref, got_ref.at[3 * seg : 4 * seg])

    def first(item):
        h, u = item
        cols = head(h, feat)
        return (
            nt(kv_ref[0, u, :, cols], queries[u][:, cols]),
            nt(kv_ref[1, u, :, cols], grads[u][:, cols]),
        )

    def second(item, scores, grad_weights):
        h, u = item
        scores = jnp.where(allowed, scores * scale, MASKED)
        top = jnp.max(scores, axis=0, keepdims=True)
        raised = jnp.exp(scores - top)
        side = slice(u * seg, (u + 1) * seg)
        stat_ref[0, h, :, side] = top
        stat_ref[1, h, :, side] = jnp.sum(raised, axis=0, keepdims=True)
        stat_ref[2, h, :, side] = jnp.sum(raised * grad_weights, axis=0, keepdims=True)
        return ()

    staged([(h, u) for h in range(heads) for u in range(2)], first, second, lambda item: None, 4)
    rows = [
        tap_rows(jnp.where(even, kv_ref[kv, 0], kv_ref[kv, 1]), heads, feat) for kv in range(2)
    ]
    near = nn(jnp.concatenate(rows, 0), w_ref[...]).astype(BF16)
    near_ref[...] = near.reshape(near_ref.shape)
    for kv, dst in enumerate((kt_ref, vt_ref)):
        for u in range(2):
            lanes = slice(u * heads * slot, (u + 1) * heads * slot)
            for t in range(TAPS):
                part = kv_ref[kv, u, t * slot : (t + 1) * slot, :]
                stacked = jnp.concatenate([part[:, head(h, feat)] for h in range(heads)], 0)
                dst[t * feat : (t + 1) * feat, lanes] = stacked.T


def memory_rows(kv, h, slots):
    return jnp.concatenate([ref[kv, h] for ref in slots], 0)


def memory_kernel(
    bias_ref, q_ref, qs_ref, g_ref, gs_ref, stat_ref,
    near_ref, joined_ref, r2s_ref, r4s_ref,
    t0_ref, t2k_ref, t2v_ref, t4k_ref, t4v_ref, w_ref, d_ref, fin_ref,
):
    seg, width = q_ref.shape
    heads = stat_ref.shape[1]
    feat = width // heads
    slot = seg // TAPS
    scale = feat**-0.5
    slots = (near_ref, joined_ref, r2s_ref, r4s_ref)

    def both(a_ref, b_ref, h):
        return jnp.concatenate([a_ref[:, head(h, feat)], b_ref[:, head(h, feat)]], 0)

    def first(h):
        return (
            nt(memory_rows(0, h, slots), both(q_ref, qs_ref, h)),
            nt(memory_rows(1, h, slots), both(g_ref, gs_ref, h)),
        )

    def second(h, scores, grad_weights):
        scores = scores * scale + bias_ref[...]
        own_top = stat_ref[0, h]
        top = jnp.maximum(own_top, jnp.max(scores, axis=0, keepdims=True))
        raised = jnp.exp(scores - top)
        fade = jnp.exp(own_top - top)
        total = stat_ref[1, h] * fade + jnp.sum(raised, axis=0, keepdims=True)
        delta = stat_ref[2, h] * fade + jnp.sum(raised * grad_weights, axis=0, keepdims=True)
        inverse = 1.0 / total
        delta = delta * inverse
        weights = raised * inverse
        weights_low = weights.astype(BF16)
        grad_scores = (weights * (grad_weights - delta) * scale).astype(BF16)
        w_ref[h] = weights_low
        d_ref[h] = grad_scores
        fin_ref[0, h] = top
        fin_ref[1, h] = inverse
        fin_ref[2, h] = delta
        return grad_scores, weights_low

    def third(h, grad_scores, weights_low):
        pair = (nn(grad_scores, both(q_ref, qs_ref, h)), nn(weights_low, both(g_ref, gs_ref, h)))
        for kv, terms in enumerate(pair):
            t0_ref[kv, h] = terms[:slot]
            terms = terms.astype(BF16)
            for i in range(4):
                ((t2k_ref, t2v_ref), (t4k_ref, t4v_ref))[i % 2][kv][i // 2, h] = terms[(i + 1) * slot : (i + 2) * slot]

    staged(list(range(heads)), first, second, third)


def output_kernel(*refs):
    q_ref, qs_ref, g_ref, gs_ref, kv_ref = refs[:5]
    slots = refs[5:9]
    w_ref, d_ref, fin_ref, *results = refs[9:]
    att_ref, gq_ref, givea_ref, giveg_ref, terms_ref = results
    seg, width = q_ref.shape
    feat = slots[0].shape[3]
    heads = width // feat
    scale = feat**-0.5
    allowed = causal(seg)
    queries, grads = (q_ref, qs_ref), (g_ref, gs_ref)

    def first(item):
        h, u = item
        cols = head(h, feat)
        return (
            nt(kv_ref[0, u, :, cols], queries[u][:, cols]),
            nt(kv_ref[1, u, :, cols], grads[u][:, cols]),
        )

    def second(item, scores, grad_weights):
        h, u = item
        side = slice(u * seg, (u + 1) * seg)
        top, inverse, delta = (fin_ref[i, h, :, side] for i in range(3))
        scores = jnp.where(allowed, scores * scale, MASKED)
        weights = jnp.exp(scores - top) * inverse
        grad_scores = (weights * (grad_weights - delta) * scale).astype(BF16)
        return grad_scores, weights.astype(BF16)

    def third(item, grad_scores, weights_low):
        h, u = item
        cols = head(h, feat)
        side = slice(u * seg, (u + 1) * seg)
        terms_ref[0, u, :, cols] = nn(grad_scores, queries[u][:, cols])
        terms_ref[1, u, :, cols] = nn(weights_low, grads[u][:, cols])

        def whole(kv, own, memory):
            rows = jnp.concatenate([kv_ref[kv, u, :, cols], memory_rows(kv, h, slots)], 0)
            return tn(jnp.concatenate([own, memory], 0), rows)

        att = whole(1, weights_low, w_ref[h, :, side]).astype(BF16)
        gq = whole(0, grad_scores, d_ref[h, :, side]).astype(BF16)
        if u == 0:
            att_ref[:, cols] = att
            gq_ref[:, cols] = gq
        else:
            givea_ref[:, cols] = att
            giveg_ref[:, cols] = gq

    staged([(h, u) for h in range(heads) for u in range(2)], first, second, third, 4)


def relay_kernel(own_ref, passed_ref, out_ref):
    first_chip = lax.axis_index("seq") % PLANE < 2
    passed = jnp.where(first_chip, 0.0, passed_ref[...].astype(F32))
    out_ref[...] = (own_ref[...].astype(F32) + passed).astype(BF16)


def first_sum_kernel(t0_ref, k4_ref, k2_ref, v2_ref, low_ref):
    position = lax.axis_index("seq")
    even = position % 2 == 0
    first_chip = position % PLANE < 2
    for u in range(2):
        near = [jnp.where(even == (u == 0), t0_ref[kv], 0.0) for kv in range(2)]
        low_ref[0, u] = near[0] + k4_ref[u].astype(F32) + k2_ref[u].astype(F32)
        low_ref[1, u] = near[1] + jnp.where(first_chip, v2_ref[u].astype(F32), 0.0)


def sum_kernel(kt_ref, vt_ref, low_ref, v4_ref, mg_ref, mine_ref, other_ref):
    count = mine_ref.shape[0] * 2
    feat = mine_ref.shape[2]
    even = lax.axis_index("seq") % 2 == 0
    terms = jnp.zeros((kt_ref.shape[0], feat), F32)
    for kv, turned_ref in enumerate((kt_ref, vt_ref)):
        rows = []
        for u in range(2):
            low = low_ref[kv, u]
            if kv == 1:
                low = low + v4_ref[u].astype(F32)
            low = low.astype(BF16)
            mg_ref[kv, u] = low
            rows.append(low.reshape(-1, feat))
        terms = terms + nn(turned_ref[...], jnp.concatenate(rows, 0))
    rows = terms.shape[0] // count
    bits = count.bit_length() - 1
    for p in range(0, count, 2):
        spot = int(format(p, "b").zfill(bits)[::-1], 2)
        first = terms[p * rows : (p + 1) * rows]
        second = terms[(p + 1) * rows : (p + 2) * rows]
        mine_ref[spot] = jnp.where(even, first, second)
        other_ref[spot] = jnp.where(even, second, first).astype(BF16)


def back_kernel(mg_ref, w_ref, terms_ref, gk_ref, gv_ref, givek_ref, givev_ref):
    seg = terms_ref.shape[2]
    heads, slot, feat = mg_ref.shape[2:]
    restore = tap_major(seg, inverse=True)
    parts = [(kv, u) for kv in range(2) for u in range(2)]
    backs = [nt(mg_ref[kv, u].reshape(heads * slot, feat), w_ref[...]) for kv, u in parts]
    totals = []
    for (kv, u), back in zip(parts, backs):
        columns = []
        for h in range(heads):
            rows = back[h * slot : (h + 1) * slot]
            columns.append(jnp.concatenate([rows[:, head(t, feat)] for t in range(TAPS)], 0))
        totals.append((terms_ref[kv, u] + jnp.concatenate(columns, 1)).astype(BF16))
    for (kv, u), total in zip(parts, totals):
        result = nn(restore, total).astype(BF16)
        ((gk_ref, gv_ref), (givek_ref, givev_ref))[u][kv][...] = result


def finish_kernel(a_in, b_in, got_a, got_b, a_ref, b_ref, sems):
    del a_in, b_in
    width = got_a.shape[1]
    start = pl.multiple_of((1 - lax.axis_index("seq") % 2) * width, width)
    copies = [
        pltpu.make_async_copy(got, dst.at[:, pl.ds(start, width)], sems.at[i])
        for i, (got, dst) in enumerate(((got_a, a_ref), (got_b, b_ref)))
    ]
    for copy in copies:
        copy.start()
    for copy in copies:
        copy.wait()


def call(kernel, out_shape, in_specs, out_specs, flops, moved, exps=0, scratch=(), aliases=None):
    return pl.pallas_call(
        kernel,
        out_shape=out_shape,
        grid=(1,),
        in_specs=in_specs,
        out_specs=out_specs,
        scratch_shapes=scratch,
        input_output_aliases=aliases or {},
        compiler_params=pltpu.CompilerParams(vmem_limit_bytes=VMEM_BYTES),
        cost_estimate=pl.CostEstimate(flops=flops, bytes_accessed=moved, transcendentals=exps),
    )


def local(queries, key_vectors, value_vectors, cotangent, compress_kernel, memory_reach):
    q, k, v, g = queries[0], key_vectors[0], value_vectors[0], cotangent[0]
    seg, width = q.shape
    feat = compress_kernel.shape[1]
    heads = width // feat
    half = heads // 2
    slot = seg // TAPS
    span = BLOCKS * slot
    count = lax.axis_size("seq")
    books = lax.axis_size("dp")
    position = lax.axis_index("seq")
    row_bytes = 2 * seg * width
    unit = 2 * heads * seg * seg * feat

    def side():
        return lax.axis_index("seq") % 2

    def shift(value, steps):
        return lax.ppermute(value, "seq", [(s, (s + steps) % count) for s in range(count)])

    def shift_part(value, steps):
        return lax.ppermute(
            value, "seq", [(s, s + steps) for s in range(count) if 0 <= s + steps < count]
        )

    def cross_part(value, steps):
        pairs = [(s, (s ^ 1) + steps) for s in range(count)]
        return lax.ppermute(value, "seq", [(s, t) for s, t in pairs if t < count])

    def cross(value, steps):
        return lax.ppermute(value, "seq", [(s, ((s ^ 1) + steps) % count) for s in range(count)])

    def trade(value, flip=1):
        return lax.ppermute(value, "seq", [(s, s ^ flip) for s in range(count)])

    def in_hbm(value):
        return pltpu.with_memory_space_constraint(value, pltpu.HBM)

    def shape(dims, kind=BF16):
        return jax.ShapeDtypeStruct(dims, kind)

    def full(dims):
        return pl.BlockSpec(dims, lambda i: (0,) * len(dims))

    mine_cols = pl.BlockSpec((seg, half * feat), lambda i: (0, side()))
    kernel_spec = full(compress_kernel.shape)

    hbm = pl.BlockSpec(memory_space=pltpu.HBM)
    rows = 4 * seg
    half_dims = (2, half, slot, feat)
    packed_mine, packed_other, give = call(
        pack_kernel,
        (shape(half_dims), shape(half_dims), shape((rows, half * feat))),
        [hbm] * 5,
        (full(half_dims), full(half_dims), full((rows, half * feat))),
        3 * unit, 5 * row_bytes,
        scratch=[
            pltpu.VMEM((2, 2, seg, half * feat), BF16),
            pltpu.VMEM(compress_kernel.shape, BF16),
            pltpu.SemaphoreType.DMA((7,)),
        ],
    )(*[in_hbm(a) for a in (k, v, q, g, compress_kernel)])
    got = trade(give)

    r4s = cross(packed_other, 4)
    r2 = shift(packed_mine, 2)
    r4 = shift(packed_mine, 4)
    plane = range(0, count, PLANE)
    r2s = lax.ppermute(
        call(
            choose_kernel, shape(half_dims), [full(half_dims)] * 2, full(half_dims), 0, row_bytes
        )(packed_other, r4s),
        "seq",
        [(p + s, p + t) for p in plane for s, t in ((0, 3), (1, 2), (2, 0), (3, 1))],
    )
    got, late_reach = lax.optimization_barrier((got, memory_reach))
    scalar = pl.BlockSpec(memory_space=pltpu.SMEM)
    kvp, near, own_stats, kt, vt, bias = call(
        own_kernel,
        (
            shape((2, 2, seg, half * feat)),
            shape((2, half, slot, feat)),
            shape((3, half, 1, 2 * seg), F32),
            shape((TAPS * feat, heads * slot)),
            shape((TAPS * feat, heads * slot)),
            shape((span, 2 * seg), F32),
        ),
        [scalar] * 2 + [mine_cols] * 4 + [full((rows, half * feat)), kernel_spec],
        (
            full((2, 2, seg, half * feat)),
            full((2, half, slot, feat)),
            full((3, half, 1, 2 * seg)),
            full((TAPS * feat, heads * slot)),
            full((TAPS * feat, heads * slot)),
            full((span, 2 * seg)),
        ),
        unit, 8 * row_bytes, heads * seg * seg,
    )(late_reach, trade(late_reach), k, v, q, g, got, compress_kernel)

    r2, own_stats = lax.optimization_barrier((r2, own_stats))
    joined_dims = (2, half, 2 * slot, feat)
    joined = call(
        join_kernel, shape(joined_dims), [full(half_dims)] * 2, full(joined_dims), 0, 10 * row_bytes
    )(r2, r4)
    slots = [near, joined, r2s, r4s]
    got_q = pl.BlockSpec((seg, half * feat), lambda i: (2, 0))
    got_g = pl.BlockSpec((seg, half * feat), lambda i: (3, 0))
    one = (2, half, slot, feat)
    soft = (half, span, 2 * seg)
    stats = (3, half, 1, 2 * seg)
    pair = (2, 2, half, slot, feat)
    t0, t2k, t2v, t4k, t4v, w_mem, d_mem, final = call(
        memory_kernel,
        (shape(one, F32), *[shape(one)] * 4, shape(soft), shape(soft), shape(stats, F32)),
        [full((span, 2 * seg)), mine_cols, got_q, mine_cols, got_g, full(stats)]
        + [full(one), full(joined_dims), full(one), full(one)],
        (full(one), *[full(one)] * 4, full(soft), full(soft), full(stats)),
        4 * unit, 8 * row_bytes, heads * seg * seg,
    )(bias, q, got, g, got, own_stats, *slots)

    v2 = trade(t2v, 2)
    k4 = shift_part(t4k, -4)
    k2 = shift(t2k, -2)
    v4 = shift_part(
        call(relay_kernel, shape(one), [full(one)] * 2, full(one), 0, row_bytes)(t4v, v2), -4
    )
    attended, grad_queries, give_a, give_g, own_terms = call(
        output_kernel,
        (
            shape((seg, width)),
            shape((seg, width)),
            shape((seg, half * feat)),
            shape((seg, half * feat)),
            shape((2, 2, seg, half * feat), F32),
        ),
        [mine_cols, got_q, mine_cols, got_g, full((2, 2, seg, half * feat))]
        + [full(one), full(joined_dims), full(one), full(one)]
        + [full(soft), full(soft), full(stats)],
        (
            mine_cols, mine_cols,
            full((seg, half * feat)),
            full((seg, half * feat)),
            full((2, 2, seg, half * feat)),
        ),
        8 * unit, 12 * row_bytes, heads * seg * seg,
    )(q, got, g, got, kvp, *slots, w_mem, d_mem, final)

    def finish(a, b, give_a, give_b):
        anywhere = pl.BlockSpec(memory_space=pl.ANY)
        return call(
            finish_kernel,
            (shape((seg, width)), shape((seg, width))),
            [anywhere] * 4,
            (anywhere, anywhere),
            0, 2 * row_bytes,
            scratch=[pltpu.SemaphoreType.DMA((2,))],
            aliases={0: 0, 1: 1},
        )(a, b, trade(give_a), trade(give_b))

    attended, grad_queries = finish(attended, grad_queries, give_a, give_g)
    kernel_rows = compress_kernel.shape[0]
    split = (count // 2, kernel_rows // count, feat)
    turned = full((TAPS * feat, heads * slot))
    low = call(
        first_sum_kernel,
        shape(pair, F32),
        [full(one)] * 4,
        full(pair),
        0, 4 * row_bytes,
    )(t0, k4, k2, v2)
    low, own_terms = lax.optimization_barrier((low, own_terms))
    memory_grads, mine, other = call(
        sum_kernel,
        (shape(pair), shape(split, F32), shape(split)),
        [turned] * 2 + [full(pair), full(one)],
        (full(pair), full(split), full(split)),
        unit, 4 * row_bytes,
    )(kt, vt, low, v4)

    grad_keys, grad_values, give_k, give_v = call(
        back_kernel,
        (shape((seg, width)), shape((seg, width)), *[shape((seg, half * feat))] * 2),
        [full(pair), kernel_spec, full((2, 2, seg, half * feat))],
        (mine_cols, mine_cols, *[full((seg, half * feat))] * 2),
        4 * unit, 7 * row_bytes,
    )(memory_grads, compress_kernel, own_terms)

    grad_keys, grad_values = finish(grad_keys, grad_values, give_k, give_v)
    part = mine + trade(other).astype(F32)
    part, (attended, grad_queries, grad_keys, grad_values) = reduce_rest(
        part, position, count, books, (attended, grad_queries, grad_keys, grad_values)
    )
    return (attended[None], grad_queries[None], grad_keys[None], grad_values[None], part)


def reduce_rest(part, position, count, books, beside):
    bits = []
    step = 2
    while step < count:
        bits.append(("seq", step))
        step *= 2
    step = 1
    while step < books:
        bits.append(("dp", step))
        step *= 2
    for i in range(0, len(bits), 2):
        phase = bits[i : i + 2]
        split = [step for axis, step in phase if axis == "seq"]
        part = part.reshape(2 ** len(split), -1, *part.shape[1:])
        mine = jnp.int32(0)
        for step in split:
            mine = mine * 2 + (position // step) % 2
        arrived = []
        for mask in range(1, 2 ** len(phase)):
            flip, seq_xor, dp_xor = 0, 0, 0
            for j, (axis, step) in enumerate(phase):
                chosen = (mask >> (len(phase) - 1 - j)) & 1
                if axis == "seq":
                    flip = flip * 2 + chosen
                    seq_xor |= chosen * step
                else:
                    dp_xor |= chosen * step
            sent = lax.dynamic_index_in_dim(part, mine ^ flip, 0, False)
            pairs = [
                (s * books + d, (s ^ seq_xor) * books + (d ^ dp_xor))
                for s in range(count)
                for d in range(books)
            ]
            arrived.append(lax.ppermute(sent.astype(BF16), ("seq", "dp"), pairs))
        part = lax.dynamic_index_in_dim(part, mine, 0, False)
        if i + 2 >= len(bits):
            arrived[0], *beside = lax.optimization_barrier((arrived[0], *beside))
        for piece in arrived:
            part = part + piece.astype(F32)
    return part.reshape(-1, part.shape[-1]), beside


def solution(mesh):
    rows = P("dp", "seq", None)
    return jax.shard_map(
        local,
        mesh=mesh,
        in_specs=(rows, rows, rows, rows, P(), P("dp", "seq")),
        out_specs=(rows, rows, rows, rows, P("seq", None)),
        check_vma=False,
    )
```

```python
import jax
import jax.numpy as jnp
from jax import lax
from jax.experimental import pallas as pl
from jax.experimental.pallas import tpu as pltpu
from jax.sharding import PartitionSpec as P

F32 = jnp.float32
BF16 = jnp.bfloat16
TAPS = 4
PLANE = 4
MASKED = -1e30
VMEM_BYTES = 24 * 2**20
BLOCKS = 5


def nt(a, b):
    return lax.dot_general(a, b, (((1,), (1,)), ((), ())), preferred_element_type=F32)


def nn(a, b):
    return lax.dot_general(a, b, (((1,), (0,)), ((), ())), preferred_element_type=F32)


def tn(a, b):
    return lax.dot_general(a, b, (((0,), (0,)), ((), ())), preferred_element_type=F32)


def tap_major(seg, inverse=False):
    slot = seg // TAPS
    spot = lax.broadcasted_iota(jnp.int32, (seg, seg), 1 if inverse else 0)
    token = lax.broadcasted_iota(jnp.int32, (seg, seg), 0 if inverse else 1)
    return (token == TAPS * (spot % slot) + spot // slot).astype(BF16)


def causal(seg):
    slot = seg // TAPS
    spot = lax.broadcasted_iota(jnp.int32, (seg, seg), 0)
    query = lax.broadcasted_iota(jnp.int32, (seg, seg), 1)
    return TAPS * (spot % slot) + spot // slot <= query


def head(h, feat):
    return slice(h * feat, (h + 1) * feat)


def staged(items, first, second, third, size=2):
    groups = [items[i : i + size] for i in range(0, len(items), size)]
    begun, turned = {}, {}
    for i in range(len(groups) + 2):
        if i < len(groups):
            for item in groups[i]:
                begun[item] = first(item)
        if i >= 2:
            for item in groups[i - 2]:
                third(item, *turned.pop(item))
        if 1 <= i <= len(groups):
            for item in groups[i - 1]:
                turned[item] = second(item, *begun.pop(item))


def tap_rows(rows, heads, feat):
    slot = rows.shape[0] // TAPS
    return jnp.concatenate(
        [
            jnp.concatenate(
                [rows[t * slot : (t + 1) * slot, head(h, feat)] for t in range(TAPS)], 1
            )
            for h in range(heads)
        ],
        0,
    )


def pack_kernel(
    k_hbm, v_hbm, q_hbm, g_hbm, w_hbm,
    mine_ref, other_ref, give_ref, rows_ref, w_ref, sems,
):
    seg, width = k_hbm.shape
    feat = w_hbm.shape[1]
    half = width // 2
    heads = half // feat
    slot = seg // TAPS
    order = tap_major(seg)
    core = lax.axis_index("seq") % 2
    begin = [pl.multiple_of(core * half, half), pl.multiple_of((1 - core) * half, half)]
    steps = [(part, kv) for part in range(2) for kv in range(2)]
    pairs = [
        ((k_hbm, v_hbm)[kv].at[:, pl.ds(begin[part], half)], rows_ref.at[part, kv])
        for part, kv in steps
    ]
    pairs.insert(2, (w_hbm, w_ref))
    pairs += [
        (src.at[:, pl.ds(begin[1], half)], give_ref.at[pl.ds((2 + i) * seg, seg)])
        for i, src in enumerate((q_hbm, g_hbm))
    ]
    copies = [pltpu.make_async_copy(*pair, sems.at[n]) for n, pair in enumerate(pairs)]
    for copy in copies:
        copy.start()
    sorted_rows = []
    for n, (part, kv) in enumerate(steps):
        copies[n if n < 2 else n + 1].wait()
    copies[2].wait()
    every = jnp.concatenate([rows_ref[part, kv] for part, kv in steps], 1)
    every = nn(order, every).astype(BF16)
    half_width = heads * feat
    sorted_rows = [
        every[:, n * half_width : (n + 1) * half_width] for n in range(len(steps))
    ]
    rows = jnp.concatenate([tap_rows(rows, heads, feat) for rows in sorted_rows], 0)
    packed = nn(rows, w_ref[...]).astype(BF16).reshape(len(steps), heads, slot, feat)
    for n, (part, kv) in enumerate(steps):
        (mine_ref, other_ref)[part][kv] = packed[n]
        if part == 1:
            give_ref[kv * seg : (kv + 1) * seg] = rows_ref[part, kv]
    for copy in copies[5:]:
        copy.wait()


def choose_kernel(own_ref, got_ref, out_ref):
    first_chip = lax.axis_index("seq") % PLANE < 2
    out_ref[...] = jnp.where(first_chip, own_ref[...], got_ref[...])


def join_kernel(a_ref, b_ref, out_ref):
    slot = a_ref.shape[2]
    out_ref[:, :, :slot] = a_ref[...]
    out_ref[:, :, slot:] = b_ref[...]


def own_kernel(
    reach_ref, reach_s_ref, k_ref, v_ref, q_ref, g_ref, got_ref, w_ref,
    kv_ref, near_ref, stat_ref, kt_ref, vt_ref, bias_ref,
):
    seg, width = q_ref.shape
    feat = w_ref.shape[1]
    heads = width // feat
    slot = seg // TAPS
    scale = feat**-0.5
    mine = lax.axis_index("seq")
    partner = mine + 1 - 2 * (mine % 2)
    even = mine % 2 == 0
    sources = (mine - mine % 2, mine - 2, mine - 4, partner - 2, partner - 4)
    for b, source in enumerate(sources):
        for u, (reader, limit) in enumerate(((mine, reach_ref), (partner, reach_s_ref))):
            steps = reader - source
            shown = (steps >= 1) & (steps <= jnp.minimum(limit[0, 0], 4)) & (source >= 0)
            bias_ref[b * slot : (b + 1) * slot, u * seg : (u + 1) * seg] = jnp.full(
                (slot, seg), jnp.where(shown, 0.0, MASKED), F32
            )
    allowed = causal(seg)
    order = tap_major(seg)
    for kv, src in enumerate((k_ref, v_ref)):
        kv_ref[kv, 0] = nn(order, src[...]).astype(BF16)
        kv_ref[kv, 1] = nn(order, got_ref[kv * seg : (kv + 1) * seg]).astype(BF16)
    queries = (q_ref, got_ref.at[2 * seg : 3 * seg])
    grads = (g_ref, got_ref.at[3 * seg : 4 * seg])

    def first(item):
        h, u = item
        cols = head(h, feat)
        return (
            nt(kv_ref[0, u, :, cols], queries[u][:, cols]),
            nt(kv_ref[1, u, :, cols], grads[u][:, cols]),
        )

    def second(item, scores, grad_weights):
        h, u = item
        scores = jnp.where(allowed, scores * scale, MASKED)
        top = jnp.max(scores, axis=0, keepdims=True)
        raised = jnp.exp(scores - top)
        side = slice(u * seg, (u + 1) * seg)
        stat_ref[0, h, :, side] = top
        stat_ref[1, h, :, side] = jnp.sum(raised, axis=0, keepdims=True)
        stat_ref[2, h, :, side] = jnp.sum(raised * grad_weights, axis=0, keepdims=True)
        return ()

    staged([(h, u) for h in range(heads) for u in range(2)], first, second, lambda item: None, 4)
    rows = [
        tap_rows(jnp.where(even, kv_ref[kv, 0], kv_ref[kv, 1]), heads, feat) for kv in range(2)
    ]
    near = nn(jnp.concatenate(rows, 0), w_ref[...]).astype(BF16)
    near_ref[...] = near.reshape(near_ref.shape)
    for kv, dst in enumerate((kt_ref, vt_ref)):
        for u in range(2):
            lanes = slice(u * heads * slot, (u + 1) * heads * slot)
            for t in range(TAPS):
                part = kv_ref[kv, u, t * slot : (t + 1) * slot, :]
                stacked = jnp.concatenate([part[:, head(h, feat)] for h in range(heads)], 0)
                dst[t * feat : (t + 1) * feat, lanes] = stacked.T


def memory_rows(kv, h, slots):
    return jnp.concatenate([ref[kv, h] for ref in slots], 0)


def memory_kernel(
    bias_ref, q_ref, qs_ref, g_ref, gs_ref, stat_ref,
    near_ref, joined_ref, r2s_ref, r4s_ref,
    t0_ref, t2k_ref, t2v_ref, t4k_ref, t4v_ref, w_ref, d_ref, fin_ref,
):
    seg, width = q_ref.shape
    heads = stat_ref.shape[1]
    feat = width // heads
    slot = seg // TAPS
    scale = feat**-0.5
    slots = (near_ref, joined_ref, r2s_ref, r4s_ref)

    def both(a_ref, b_ref, h):
        return jnp.concatenate([a_ref[:, head(h, feat)], b_ref[:, head(h, feat)]], 0)

    def first(h):
        return (
            nt(memory_rows(0, h, slots), both(q_ref, qs_ref, h)),
            nt(memory_rows(1, h, slots), both(g_ref, gs_ref, h)),
        )

    def second(h, scores, grad_weights):
        scores = scores * scale + bias_ref[...]
        own_top = stat_ref[0, h]
        top = jnp.maximum(own_top, jnp.max(scores, axis=0, keepdims=True))
        raised = jnp.exp(scores - top)
        fade = jnp.exp(own_top - top)
        total = stat_ref[1, h] * fade + jnp.sum(raised, axis=0, keepdims=True)
        delta = stat_ref[2, h] * fade + jnp.sum(raised * grad_weights, axis=0, keepdims=True)
        inverse = 1.0 / total
        delta = delta * inverse
        weights = raised * inverse
        weights_low = weights.astype(BF16)
        grad_scores = (weights * (grad_weights - delta) * scale).astype(BF16)
        w_ref[h] = weights_low
        d_ref[h] = grad_scores
        fin_ref[0, h] = top
        fin_ref[1, h] = inverse
        fin_ref[2, h] = delta
        return grad_scores, weights_low

    def third(h, grad_scores, weights_low):
        pair = (nn(grad_scores, both(q_ref, qs_ref, h)), nn(weights_low, both(g_ref, gs_ref, h)))
        for kv, terms in enumerate(pair):
            t0_ref[kv, h] = terms[:slot]
            terms = terms.astype(BF16)
            for i in range(4):
                ((t2k_ref, t2v_ref), (t4k_ref, t4v_ref))[i % 2][kv][i // 2, h] = terms[(i + 1) * slot : (i + 2) * slot]

    staged(list(range(heads)), first, second, third)


def output_kernel(*refs):
    q_ref, qs_ref, g_ref, gs_ref, kv_ref = refs[:5]
    slots = refs[5:9]
    w_ref, d_ref, fin_ref, *results = refs[9:]
    att_ref, gq_ref, givea_ref, giveg_ref, terms_ref = results
    seg, width = q_ref.shape
    feat = slots[0].shape[3]
    heads = width // feat
    scale = feat**-0.5
    allowed = causal(seg)
    queries, grads = (q_ref, qs_ref), (g_ref, gs_ref)

    def first(item):
        h, u = item
        cols = head(h, feat)
        return (
            nt(kv_ref[0, u, :, cols], queries[u][:, cols]),
            nt(kv_ref[1, u, :, cols], grads[u][:, cols]),
        )

    def second(item, scores, grad_weights):
        h, u = item
        side = slice(u * seg, (u + 1) * seg)
        top, inverse, delta = (fin_ref[i, h, :, side] for i in range(3))
        scores = jnp.where(allowed, scores * scale, MASKED)
        weights = jnp.exp(scores - top) * inverse
        grad_scores = (weights * (grad_weights - delta) * scale).astype(BF16)
        return grad_scores, weights.astype(BF16)

    def third(item, grad_scores, weights_low):
        h, u = item
        cols = head(h, feat)
        side = slice(u * seg, (u + 1) * seg)
        terms_ref[0, u, :, cols] = nn(grad_scores, queries[u][:, cols])
        terms_ref[1, u, :, cols] = nn(weights_low, grads[u][:, cols])

        def whole(kv, own, memory):
            rows = jnp.concatenate([kv_ref[kv, u, :, cols], memory_rows(kv, h, slots)], 0)
            return tn(jnp.concatenate([own, memory], 0), rows)

        att = whole(1, weights_low, w_ref[h, :, side]).astype(BF16)
        gq = whole(0, grad_scores, d_ref[h, :, side]).astype(BF16)
        if u == 0:
            att_ref[:, cols] = att
            gq_ref[:, cols] = gq
        else:
            givea_ref[:, cols] = att
            giveg_ref[:, cols] = gq

    staged([(h, u) for h in range(heads) for u in range(2)], first, second, third, 4)


def relay_kernel(own_ref, passed_ref, out_ref):
    first_chip = lax.axis_index("seq") % PLANE < 2
    passed = jnp.where(first_chip, 0.0, passed_ref[...].astype(F32))
    out_ref[...] = (own_ref[...].astype(F32) + passed).astype(BF16)


def first_sum_kernel(t0_ref, k4_ref, k2_ref, v2_ref, low_ref):
    position = lax.axis_index("seq")
    even = position % 2 == 0
    first_chip = position % PLANE < 2
    for u in range(2):
        near = [jnp.where(even == (u == 0), t0_ref[kv], 0.0) for kv in range(2)]
        low_ref[0, u] = near[0] + k4_ref[u].astype(F32) + k2_ref[u].astype(F32)
        low_ref[1, u] = near[1] + jnp.where(first_chip, v2_ref[u].astype(F32), 0.0)


def sum_kernel(kt_ref, vt_ref, low_ref, v4_ref, mg_ref, mine_ref, other_ref):
    count = mine_ref.shape[0] * 2
    feat = mine_ref.shape[2]
    even = lax.axis_index("seq") % 2 == 0
    terms = jnp.zeros((kt_ref.shape[0], feat), F32)
    for kv, turned_ref in enumerate((kt_ref, vt_ref)):
        rows = []
        for u in range(2):
            low = low_ref[kv, u]
            if kv == 1:
                low = low + v4_ref[u].astype(F32)
            low = low.astype(BF16)
            mg_ref[kv, u] = low
            rows.append(low.reshape(-1, feat))
        terms = terms + nn(turned_ref[...], jnp.concatenate(rows, 0))
    rows = terms.shape[0] // count
    bits = count.bit_length() - 1
    for p in range(0, count, 2):
        spot = int(format(p, "b").zfill(bits)[::-1], 2)
        first = terms[p * rows : (p + 1) * rows]
        second = terms[(p + 1) * rows : (p + 2) * rows]
        mine_ref[spot] = jnp.where(even, first, second)
        other_ref[spot] = jnp.where(even, second, first).astype(BF16)


def back_kernel(mg_ref, w_ref, terms_ref, gk_ref, gv_ref, givek_ref, givev_ref):
    seg = terms_ref.shape[2]
    heads, slot, feat = mg_ref.shape[2:]
    restore = tap_major(seg, inverse=True)
    parts = [(kv, u) for kv in range(2) for u in range(2)]
    backs = [nt(mg_ref[kv, u].reshape(heads * slot, feat), w_ref[...]) for kv, u in parts]
    totals = []
    for (kv, u), back in zip(parts, backs):
        columns = []
        for h in range(heads):
            rows = back[h * slot : (h + 1) * slot]
            columns.append(jnp.concatenate([rows[:, head(t, feat)] for t in range(TAPS)], 0))
        totals.append((terms_ref[kv, u] + jnp.concatenate(columns, 1)).astype(BF16))
    for (kv, u), total in zip(parts, totals):
        result = nn(restore, total).astype(BF16)
        ((gk_ref, gv_ref), (givek_ref, givev_ref))[u][kv][...] = result


def finish_kernel(a_in, b_in, got_a, got_b, a_ref, b_ref, sems):
    del a_in, b_in
    width = got_a.shape[1]
    start = pl.multiple_of((1 - lax.axis_index("seq") % 2) * width, width)
    copies = [
        pltpu.make_async_copy(got, dst.at[:, pl.ds(start, width)], sems.at[i])
        for i, (got, dst) in enumerate(((got_a, a_ref), (got_b, b_ref)))
    ]
    for copy in copies:
        copy.start()
    for copy in copies:
        copy.wait()


def call(kernel, out_shape, in_specs, out_specs, flops, moved, exps=0, scratch=(), aliases=None):
    return pl.pallas_call(
        kernel,
        out_shape=out_shape,
        grid=(1,),
        in_specs=in_specs,
        out_specs=out_specs,
        scratch_shapes=scratch,
        input_output_aliases=aliases or {},
        compiler_params=pltpu.CompilerParams(vmem_limit_bytes=VMEM_BYTES),
        cost_estimate=pl.CostEstimate(flops=flops, bytes_accessed=moved, transcendentals=exps),
    )


def local(queries, key_vectors, value_vectors, cotangent, compress_kernel, memory_reach):
    q, k, v, g = queries[0], key_vectors[0], value_vectors[0], cotangent[0]
    seg, width = q.shape
    feat = compress_kernel.shape[1]
    heads = width // feat
    half = heads // 2
    slot = seg // TAPS
    span = BLOCKS * slot
    count = lax.axis_size("seq")
    books = lax.axis_size("dp")
    position = lax.axis_index("seq")
    row_bytes = 2 * seg * width
    unit = 2 * heads * seg * seg * feat

    def side():
        return lax.axis_index("seq") % 2

    def shift(value, steps):
        return lax.ppermute(value, "seq", [(s, (s + steps) % count) for s in range(count)])

    def shift_part(value, steps):
        return lax.ppermute(
            value, "seq", [(s, s + steps) for s in range(count) if 0 <= s + steps < count]
        )

    def cross_part(value, steps):
        pairs = [(s, (s ^ 1) + steps) for s in range(count)]
        return lax.ppermute(value, "seq", [(s, t) for s, t in pairs if t < count])

    def cross(value, steps):
        return lax.ppermute(value, "seq", [(s, ((s ^ 1) + steps) % count) for s in range(count)])

    def trade(value, flip=1):
        return lax.ppermute(value, "seq", [(s, s ^ flip) for s in range(count)])

    def in_hbm(value):
        return pltpu.with_memory_space_constraint(value, pltpu.HBM)

    def shape(dims, kind=BF16):
        return jax.ShapeDtypeStruct(dims, kind)

    def full(dims):
        return pl.BlockSpec(dims, lambda i: (0,) * len(dims))

    mine_cols = pl.BlockSpec((seg, half * feat), lambda i: (0, side()))
    kernel_spec = full(compress_kernel.shape)

    hbm = pl.BlockSpec(memory_space=pltpu.HBM)
    rows = 4 * seg
    half_dims = (2, half, slot, feat)
    packed_mine, packed_other, give = call(
        pack_kernel,
        (shape(half_dims), shape(half_dims), shape((rows, half * feat))),
        [hbm] * 5,
        (full(half_dims), full(half_dims), full((rows, half * feat))),
        3 * unit, 5 * row_bytes,
        scratch=[
            pltpu.VMEM((2, 2, seg, half * feat), BF16),
            pltpu.VMEM(compress_kernel.shape, BF16),
            pltpu.SemaphoreType.DMA((7,)),
        ],
    )(*[in_hbm(a) for a in (k, v, q, g, compress_kernel)])
    got = trade(give)

    r4s = cross(packed_other, 4)
    r2 = shift(packed_mine, 2)
    r4 = shift(packed_mine, 4)
    plane = range(0, count, PLANE)
    r2s = lax.ppermute(
        call(
            choose_kernel, shape(half_dims), [full(half_dims)] * 2, full(half_dims), 0, row_bytes
        )(packed_other, r4s),
        "seq",
        [(p + s, p + t) for p in plane for s, t in ((0, 3), (1, 2), (2, 0), (3, 1))],
    )
    got, late_reach = lax.optimization_barrier((got, memory_reach))
    scalar = pl.BlockSpec(memory_space=pltpu.SMEM)
    kvp, near, own_stats, kt, vt, bias = call(
        own_kernel,
        (
            shape((2, 2, seg, half * feat)),
            shape((2, half, slot, feat)),
            shape((3, half, 1, 2 * seg), F32),
            shape((TAPS * feat, heads * slot)),
            shape((TAPS * feat, heads * slot)),
            shape((span, 2 * seg), F32),
        ),
        [scalar] * 2 + [mine_cols] * 4 + [full((rows, half * feat)), kernel_spec],
        (
            full((2, 2, seg, half * feat)),
            full((2, half, slot, feat)),
            full((3, half, 1, 2 * seg)),
            full((TAPS * feat, heads * slot)),
            full((TAPS * feat, heads * slot)),
            full((span, 2 * seg)),
        ),
        unit, 8 * row_bytes, heads * seg * seg,
    )(late_reach, trade(late_reach), k, v, q, g, got, compress_kernel)

    r2, own_stats = lax.optimization_barrier((r2, own_stats))
    joined_dims = (2, half, 2 * slot, feat)
    joined = call(
        join_kernel, shape(joined_dims), [full(half_dims)] * 2, full(joined_dims), 0, 10 * row_bytes
    )(r2, r4)
    slots = [near, joined, r2s, r4s]
    got_q = pl.BlockSpec((seg, half * feat), lambda i: (2, 0))
    got_g = pl.BlockSpec((seg, half * feat), lambda i: (3, 0))
    one = (2, half, slot, feat)
    soft = (half, span, 2 * seg)
    stats = (3, half, 1, 2 * seg)
    pair = (2, 2, half, slot, feat)
    t0, t2k, t2v, t4k, t4v, w_mem, d_mem, final = call(
        memory_kernel,
        (shape(one, F32), *[shape(one)] * 4, shape(soft), shape(soft), shape(stats, F32)),
        [full((span, 2 * seg)), mine_cols, got_q, mine_cols, got_g, full(stats)]
        + [full(one), full(joined_dims), full(one), full(one)],
        (full(one), *[full(one)] * 4, full(soft), full(soft), full(stats)),
        4 * unit, 8 * row_bytes, heads * seg * seg,
    )(bias, q, got, g, got, own_stats, *slots)

    v2 = trade(t2v, 2)
    k4 = shift(t4k, -4)
    k2 = shift_part(t2k, -2)
    v4 = shift_part(
        call(relay_kernel, shape(one), [full(one)] * 2, full(one), 0, row_bytes)(t4v, v2), -4
    )
    attended, grad_queries, give_a, give_g, own_terms = call(
        output_kernel,
        (
            shape((seg, width)),
            shape((seg, width)),
            shape((seg, half * feat)),
            shape((seg, half * feat)),
            shape((2, 2, seg, half * feat), F32),
        ),
        [mine_cols, got_q, mine_cols, got_g, full((2, 2, seg, half * feat))]
        + [full(one), full(joined_dims), full(one), full(one)]
        + [full(soft), full(soft), full(stats)],
        (
            mine_cols, mine_cols,
            full((seg, half * feat)),
            full((seg, half * feat)),
            full((2, 2, seg, half * feat)),
        ),
        8 * unit, 12 * row_bytes, heads * seg * seg,
    )(q, got, g, got, kvp, *slots, w_mem, d_mem, final)

    def finish(a, b, give_a, give_b):
        anywhere = pl.BlockSpec(memory_space=pl.ANY)
        return call(
            finish_kernel,
            (shape((seg, width)), shape((seg, width))),
            [anywhere] * 4,
            (anywhere, anywhere),
            0, 2 * row_bytes,
            scratch=[pltpu.SemaphoreType.DMA((2,))],
            aliases={0: 0, 1: 1},
        )(a, b, trade(give_a), trade(give_b))

    attended, grad_queries = finish(attended, grad_queries, give_a, give_g)
    kernel_rows = compress_kernel.shape[0]
    split = (count // 2, kernel_rows // count, feat)
    turned = full((TAPS * feat, heads * slot))
    low = call(
        first_sum_kernel,
        shape(pair, F32),
        [full(one)] * 4,
        full(pair),
        0, 4 * row_bytes,
    )(t0, k4, k2, v2)
    low, own_terms = lax.optimization_barrier((low, own_terms))
    memory_grads, mine, other = call(
        sum_kernel,
        (shape(pair), shape(split, F32), shape(split)),
        [turned] * 2 + [full(pair), full(one)],
        (full(pair), full(split), full(split)),
        unit, 4 * row_bytes,
    )(kt, vt, low, v4)

    grad_keys, grad_values, give_k, give_v = call(
        back_kernel,
        (shape((seg, width)), shape((seg, width)), *[shape((seg, half * feat))] * 2),
        [full(pair), kernel_spec, full((2, 2, seg, half * feat))],
        (mine_cols, mine_cols, *[full((seg, half * feat))] * 2),
        4 * unit, 7 * row_bytes,
    )(memory_grads, compress_kernel, own_terms)

    grad_keys, grad_values = finish(grad_keys, grad_values, give_k, give_v)
    part = mine + trade(other).astype(F32)
    part, (attended, grad_queries, grad_keys, grad_values) = reduce_rest(
        part, position, count, books, (attended, grad_queries, grad_keys, grad_values)
    )
    return (attended[None], grad_queries[None], grad_keys[None], grad_values[None], part)


def reduce_rest(part, position, count, books, beside):
    bits = []
    step = 2
    while step < count:
        bits.append(("seq", step))
        step *= 2
    step = 1
    while step < books:
        bits.append(("dp", step))
        step *= 2
    for i in range(0, len(bits), 2):
        phase = bits[i : i + 2]
        split = [step for axis, step in phase if axis == "seq"]
        part = part.reshape(2 ** len(split), -1, *part.shape[1:])
        mine = jnp.int32(0)
        for step in split:
            mine = mine * 2 + (position // step) % 2
        arrived = []
        for mask in range(1, 2 ** len(phase)):
            flip, seq_xor, dp_xor = 0, 0, 0
            for j, (axis, step) in enumerate(phase):
                chosen = (mask >> (len(phase) - 1 - j)) & 1
                if axis == "seq":
                    flip = flip * 2 + chosen
                    seq_xor |= chosen * step
                else:
                    dp_xor |= chosen * step
            sent = lax.dynamic_index_in_dim(part, mine ^ flip, 0, False)
            pairs = [
                (s * books + d, (s ^ seq_xor) * books + (d ^ dp_xor))
                for s in range(count)
                for d in range(books)
            ]
            arrived.append(lax.ppermute(sent.astype(BF16), ("seq", "dp"), pairs))
        part = lax.dynamic_index_in_dim(part, mine, 0, False)
        if i + 2 >= len(bits):
            arrived[0], *beside = lax.optimization_barrier((arrived[0], *beside))
        for piece in arrived:
            part = part + piece.astype(F32)
    return part.reshape(-1, part.shape[-1]), beside


def solution(mesh):
    rows = P("dp", "seq", None)
    return jax.shard_map(
        local,
        mesh=mesh,
        in_specs=(rows, rows, rows, rows, P(), P("dp", "seq")),
        out_specs=(rows, rows, rows, rows, P("seq", None)),
        check_vma=False,
    )
```
